128 devices in a mesh: gx: 8 (over z_lo, x), gy: 16 (over y, z_hi, core).
Axes of the slice: x: 4, y: 4, z: 4 (z_hi: 2, z_lo: 2; z = z_hi * 2 + z_lo), core: 2. Of those that a mesh axis runs over, the one named last changes fastest.
Arguments:
- e_forward: float32 [3, 128, 512, 512], P(None, 'gx', 'gy'), may hold values from -6 to 6
- h_forward: float32 [3, 128, 512, 512], P(None, 'gx', 'gy'), may hold values from -6 to 6
- e_adjoint: float32 [3, 128, 512, 512], P(None, 'gx', 'gy'), may hold values from -6 to 6
- h_adjoint: float32 [3, 128, 512, 512], P(None, 'gx', 'gy'), may hold values from -6 to 6
- inv_eps: float32 [128, 512, 512], P('gx', 'gy'), may hold values from 0.08 to 1
- source: float32 [128, 512, 512], P('gx', 'gy'), may hold values from -6 to 6
- adj_source: float32 [128, 512, 512], P('gx', 'gy'), may hold values from -6 to 6
- design_mask: int32 [8, 16, 128], P('gx', 'gy'), may hold values from 0 to 1, as said below
- param_map: int32 [8, 16, 128], P('gx', 'gy'), may hold values from 0 to 8191, as said below
- step_index: int32 [1], replicated, may hold values from 0 to 4095
Outputs:
- design_grad: float32 [8192, 2048], P(('gx', 'gy'))
- e_forward_out: float32 [3, 128, 512, 512], P(None, 'gx', 'gy')
- e_adjoint_out: float32 [3, 128, 512, 512], P(None, 'gx', 'gy')
The draws below stay inside these ranges and needn't reach their ends.
Inputs may be any that keep to these rules, and one draw needn't show every extreme that they name: `design_mask`: exactly 8192 blocks are 1; the number of 1s of one device varies from device to device, and some device has all its 128 blocks at 1. `param_map`: over the blocks with design_mask 1 the values are distinct and use every one of 0..8191; parameter p is owned by device p // 64 of gx+gy; a device's design blocks go to at most 1 parameters of any one owner, a bound that some device reaches; the values of other blocks mean nothing.
All inputs are finite; a program needn't handle non-finite values.
Results may differ from the reference program's by a relative error of at most 0.00013.
Values sent between devices are 32-bit elements; how exact they have to be, the bound alone decides.
No kernel may reach another device: no remote copies, remote signals or barrier semaphores. Data moves between devices by JAX's collectives and lax.ppermute only.
A program may use at most 256 MiB of HBM per device.

```python
import math
import jax
import jax.numpy as jnp
from jax import lax

CX = 16
CY = 32
NZ = 512
BZ = 4
STEPS = 2
NX = 128
NY = 512
NB = 128
PARAMS = 8192
N_GX = 8
N_GY = 16


def design_layout(key):
    devices = N_GX * N_GY
    half_blocks = NB // 2
    key_pair, key_perm, key_rows, key_offset, key_filler = jax.random.split(jax.random.fold_in(key, 7), 5)
    imbalance = jax.random.randint(key_pair, (devices // 2,), 0, half_blocks + 1)
    imbalance = imbalance.at[0].set(half_blocks)
    region_sizes = jnp.concatenate([half_blocks + imbalance, half_blocks - imbalance])
    region_sizes = region_sizes[jax.random.permutation(key_perm, devices)]
    orders = jax.vmap(lambda single: jax.random.permutation(single, NB))(jax.random.split(key_rows, devices))
    inverse = jnp.argsort(orders, axis=1, stable=True)
    in_region = (inverse < region_sizes[:, None]).astype(jnp.int32)
    flatten = in_region.reshape(-1)
    ordinal = jnp.cumsum(flatten) - flatten
    total_params = devices * half_blocks
    offset_all = jax.random.randint(key_offset, (), 0, total_params)
    shifted = (ordinal + offset_all) % total_params
    param_index = shifted % devices * half_blocks + shifted // devices
    filler = jax.random.randint(key_filler, flatten.shape, 0, total_params)
    param_index = jnp.where(flatten == 1, param_index, filler)
    return (in_region.reshape(N_GX, N_GY, NB).astype(jnp.int32), param_index.reshape(N_GX, N_GY, NB).astype(jnp.int32))


def draw_design_mask(key, part):
    return design_layout(key)[0]


def draw_param_map(key, part):
    return design_layout(key)[1]


def block_levels(rng, shape, cuts, least, high):
    level = 1.0
    for dim, blocks in cuts:
        draws = jax.random.uniform(jax.random.fold_in(jax.random.fold_in(rng, 6), dim), (blocks,), jnp.float32, least / len(cuts), high / len(cuts))
        level = level * jnp.repeat(jnp.exp(draws), shape[dim] // blocks).reshape((-1,) + (1,) * (len(shape) - 1 - dim))
    return level


def scatter_about(key, shape, width, reach, cuts=(), dtype=jnp.bfloat16):
    array = jax.random.normal(key, shape, jnp.float32) * width
    if len(cuts) > 0:
        array = block_levels(key, shape, cuts, -0.22, 0.18) * array
    return jnp.clip(array, min=-reach, max=reach).astype(dtype)


def setup_inputs(seed: int = 0) -> dict:
    streams_of = jax.random.split(jax.random.key(seed), 11)
    e_forward = scatter_about(streams_of[0], (3, NX, NY, NZ), 1.0, 6.0, ((1, 8), (2, 16)), jnp.float32)
    h_forward = scatter_about(streams_of[1], (3, NX, NY, NZ), 1.0, 6.0, ((1, 8), (2, 16)), jnp.float32)
    e_adjoint = scatter_about(streams_of[2], (3, NX, NY, NZ), 1.0, 6.0, ((1, 8), (2, 16)), jnp.float32)
    h_adjoint = scatter_about(streams_of[3], (3, NX, NY, NZ), 1.0, 6.0, ((1, 8), (2, 16)), jnp.float32)
    inv_eps = jnp.clip(jnp.exp(math.log(1.0) - 2.5257287 * jax.random.uniform(streams_of[4], (NX, NY, NZ), jnp.float32) ** block_levels(streams_of[4], (NX, NY, NZ), ((0, 8), (1, 16)), -0.2, 0.2)), 0.08, 1.0)
    source = scatter_about(streams_of[5], (NX, NY, NZ), 1.0, 6.0, ((0, 8), (1, 16)), jnp.float32)
    adj_source = scatter_about(streams_of[6], (NX, NY, NZ), 1.0, 6.0, ((0, 8), (1, 16)), jnp.float32)
    design_mask = draw_design_mask(jax.random.fold_in(streams_of[10], 71), 0)
    param_map = draw_param_map(jax.random.fold_in(streams_of[10], 71), 0)
    step_index = jax.random.randint(streams_of[9], (1,), 0, 4096).astype(jnp.int32)
    return dict(e_forward=e_forward, h_forward=h_forward, e_adjoint=e_adjoint, h_adjoint=h_adjoint, inv_eps=inv_eps, source=source, adj_source=adj_source, design_mask=design_mask, param_map=param_map, step_index=step_index)


time_step = 0.5
period_steps = 20
phase_rate = 2.0 * math.pi / 20.0


def plus_diff(field, axis):
    rest = lax.slice_in_dim(field, 1, field.shape[axis], axis=axis)
    edge = jnp.zeros_like(lax.slice_in_dim(field, 0, 1, axis=axis))
    return jnp.concatenate([rest, edge], axis) - field


def minus_diff(field, axis):
    rest = lax.slice_in_dim(field, 0, field.shape[axis] - 1, axis=axis)
    edge = jnp.zeros_like(lax.slice_in_dim(field, 0, 1, axis=axis))
    return field - jnp.concatenate([edge, rest], axis)


def amplitude(tick):
    return jnp.sin(phase_rate * jnp.remainder(tick, period_steps).astype(jnp.float32))


def advance(e_field, h_field, inv_eps, driving):
    e_x, e_y, e_z = e_field[0], e_field[1], e_field[2]
    curl_e = jnp.stack([plus_diff(e_z, 1) - plus_diff(e_y, 2), plus_diff(e_x, 2) - plus_diff(e_z, 0), plus_diff(e_y, 0) - plus_diff(e_x, 1)])
    h_field = h_field - time_step * curl_e
    h_x, h_y, h_z = h_field[0], h_field[1], h_field[2]
    curl_h = jnp.stack([minus_diff(h_z, 1) - minus_diff(h_y, 2), minus_diff(h_x, 2) - minus_diff(h_z, 0), minus_diff(h_y, 0) - minus_diff(h_x, 1) - driving])
    e_field = e_field + time_step * inv_eps * curl_h
    return e_field, h_field


def reference(e_forward, h_forward, e_adjoint, h_adjoint, inv_eps, source, adj_source, design_mask, param_map, step_index):
    start = step_index[0]
    accumulated = jnp.zeros(inv_eps.shape, jnp.float32)
    e_fwd, h_fwd, e_adj, h_adj = e_forward, h_forward, e_adjoint, h_adjoint
    for step in range(1, STEPS + 1):
        e_fwd, h_fwd = advance(e_fwd, h_fwd, inv_eps, source * amplitude(start + step))
        e_adj, h_adj = advance(e_adj, h_adj, inv_eps, adj_source * amplitude(start - step))
        accumulated = accumulated + (e_fwd[0] * e_adj[0] + e_fwd[1] * e_adj[1] + e_fwd[2] * e_adj[2])
    gradient = time_step * accumulated
    blocks = gradient.reshape(N_GX, CX, N_GY, CY, NB, BZ).transpose(0, 2, 4, 1, 3, 5).reshape(N_GX * N_GY * NB, CX * CY * BZ)
    in_region = design_mask.reshape(-1)
    targets = jnp.where(in_region == 1, param_map.reshape(-1), PARAMS).astype(jnp.int32)
    design_grad = jnp.zeros((PARAMS, CX * CY * BZ), jnp.float32).at[targets].set(blocks, mode="drop")
    return design_grad, e_fwd, e_adj
```

```python
import functools
import math

import jax
import jax.numpy as jnp
from jax import lax
from jax.experimental import pallas as pl
from jax.experimental.pallas import tpu as pltpu
from jax.sharding import PartitionSpec as P

BZ = 4
STEPS = 2
DT = 0.5
PERIOD = 20
RATE = 2.0 * math.pi / 20.0
CX, CY, NZ = 16, 32, 512
RING = 40
F32 = jnp.float32
VMEM_BYTES = 48 * 1024 * 1024

FIELDS = [(a, c) for a in range(4) for c in range(3)] + [(4, 0), (5, 0), (6, 0)]
UP = [(a, c, 31) for a, c in FIELDS] + [(a, c, 30) for a, c in FIELDS if a < 4 and (a % 2 == 0 or c != 1)]
DOWN = [(a, c, 0) for a, c in FIELDS] + [(a, c, 1) for a, c in FIELDS if a in (0, 2) and c != 1]
UP_AT = {key: k for k, key in enumerate(UP)}
DOWN_AT = {key: k for k, key in enumerate(DOWN)}


def cycled(value, axis, by):
    devices = lax.axis_size(axis)
    return lax.ppermute(value, axis, [(i, (i + by) % devices) for i in range(devices)])


def rows_iota(shape):
    return lax.broadcasted_iota(jnp.int32, shape, 0)


def lanes_iota(shape):
    return lax.broadcasted_iota(jnp.int32, shape, 1)


def plus_y(f):
    return pltpu.roll(f, f.shape[0] - 1, 0) - f


def minus_y(f):
    return f - pltpu.roll(f, 1, 0)


def plus_z(f):
    return jnp.where(lanes_iota(f.shape) == NZ - 1, 0.0, pltpu.roll(f, NZ - 1, 1)) - f


def minus_z(f):
    return f - jnp.where(lanes_iota(f.shape) == 0, 0.0, pltpu.roll(f, 1, 1))


def magnetic(e, e_next, h, row_dt):
    ahead_y = -e[1] if e_next is None else e_next[1] - e[1]
    ahead_z = -e[2] if e_next is None else e_next[2] - e[2]
    return (
        h[0] - row_dt * (plus_y(e[2]) - plus_z(e[1])),
        h[1] - row_dt * (plus_z(e[0]) - ahead_z),
        h[2] - row_dt * (ahead_y - plus_y(e[0])),
    )


def electric(e, h, h_prev, coef, drive):
    back_y = h[1] if h_prev is None else h[1] - h_prev[1]
    back_z = h[2] if h_prev is None else h[2] - h_prev[2]
    return (
        e[0] + coef * (minus_y(h[2]) - minus_z(h[1])),
        e[1] + coef * (minus_z(h[0]) - back_z),
        e[2] + coef * (back_y - minus_y(h[0]) - drive),
    )


def dot_three(a, b):
    return a[0] * b[0] + a[1] * b[1] + a[2] * b[2]


def ring_of(own, above, below, array, comp, x):
    rows = rows_iota((8, NZ))
    tile = jnp.zeros((8, NZ), F32)

    def put(tile, ref, at, row):
        if at is None:
            return tile
        return jnp.where(rows == row, ref[at, pl.ds(x, 1), :], tile)

    tile = put(tile, below, DOWN_AT.get((array, comp, 0)), 0)
    tile = put(tile, below, DOWN_AT.get((array, comp, 1)), 1)
    has_below, has_above = has_rows()
    tile = jnp.where(has_below, tile, 0.0)
    prev = jnp.zeros((8, NZ), F32)
    prev = put(prev, above, UP_AT.get((array, comp, 30)), 6)
    prev = put(prev, above, UP_AT.get((array, comp, 31)), 7)
    tile = tile + jnp.where(has_above, prev, 0.0)
    return jnp.concatenate([own, tile], axis=0)


def has_rows():
    place = lax.axis_index("gy")
    return place < lax.axis_size("gy") - 1, place > 0


def row_steps():
    rows = rows_iota((RING, NZ))
    _, has_above = has_rows()
    return jnp.where((rows >= RING - 2) & jnp.logical_not(has_above), 0.0, DT)


def pack_kernel(*refs):
    firsts, lasts, up, down = refs[:7], refs[7:14], refs[14], refs[15]

    def row(ref, a, c, r):
        return ref[c, :, r, :] if a < 4 else ref[:, r, :]

    for k, (a, c, r) in enumerate(UP):
        up[k] = row(lasts[a], a, c, r - 24)
    for k, (a, c, r) in enumerate(DOWN):
        down[k] = row(firsts[a], a, c, r)


def pack_rows(arrays):
    part = 8

    def spec(a, tile):
        if a < 4:
            return pl.BlockSpec((3, part, 8, NZ), lambda i, tile=tile: (0, i, tile, 0))
        return pl.BlockSpec((part, 8, NZ), lambda i, tile=tile: (i, tile, 0))

    return pl.pallas_call(
        pack_kernel,
        grid=(CX // part,),
        in_specs=[spec(a, 0) for a in range(7)] + [spec(a, 3) for a in range(7)],
        out_specs=[
            pl.BlockSpec((len(UP), part, NZ), lambda i: (0, i, 0)),
            pl.BlockSpec((len(DOWN), part, NZ), lambda i: (0, i, 0)),
        ],
        out_shape=[
            jax.ShapeDtypeStruct((len(UP), CX, NZ), F32),
            jax.ShapeDtypeStruct((len(DOWN), CX, NZ), F32),
        ],
        compiler_params=pltpu.CompilerParams(vmem_limit_bytes=VMEM_BYTES),
        cost_estimate=pl.CostEstimate(flops=0, bytes_accessed=10 << 20, transcendentals=0),
        name="pack_rows",
    )(*arrays, *arrays)


def edge_kernel(amp, e_f0, h_f0, e_a0, h_a0, inv0, src0, adj0, e_f1, h_f1, e_a1, h_a1, inv1, src1, adj1, above, below, to_prev, to_next, keep):
    row_dt = row_steps()

    def layer(ref, array, at, x):
        return tuple(ring_of(ref[c, at], above, below, array, c, x) for c in range(3))

    coef_first = DT * ring_of(inv0[0], above, below, 4, 0, 0)
    coef_last = DT * ring_of(inv1[1], above, below, 4, 0, CX - 1)
    to_prev[8] = coef_first
    to_next[8] = coef_last
    for run, (e0, h0, s0, e1, h1, s1, amp_at) in enumerate(
        [(e_f0, h_f0, src0, e_f1, h_f1, src1, 0), (e_a0, h_a0, adj0, e_a1, h_a1, adj1, 2)]
    ):
        e_id, h_id, s_id = 2 * run, 2 * run + 1, 5 + run
        e, ahead = layer(e0, e_id, 0, 0), layer(e0, e_id, 1, 1)
        h = magnetic(e, ahead, layer(h0, h_id, 0, 0), row_dt)
        drive = amp[0, amp_at] * ring_of(s0[0], above, below, s_id, 0, 0)
        new = electric(e, h, None, coef_first, drive)
        to_prev[4 * run] = e[1]
        to_prev[4 * run + 1] = e[2]
        to_prev[4 * run + 2] = new[1]
        to_prev[4 * run + 3] = new[2]
        keep[4 * run] = new[0][:CY]
        e, back = layer(e1, e_id, 1, CX - 1), layer(e1, e_id, 0, CX - 2)
        h = magnetic(e, None, layer(h1, h_id, 1, CX - 1), row_dt)
        h_back = magnetic(back, e, layer(h1, h_id, 0, CX - 2), row_dt)
        drive = amp[0, amp_at] * ring_of(s1[1], above, below, s_id, 0, CX - 1)
        new = electric(e, h, h_back, coef_last, drive)
        later = magnetic(new, None, h, row_dt)
        to_next[4 * run] = h[1]
        to_next[4 * run + 1] = h[2]
        to_next[4 * run + 2] = later[1]
        to_next[4 * run + 3] = later[2]
        for c in range(3):
            keep[4 * run + 1 + c] = new[c][:CY]


def solve_edges(amp, arrays, above, below):
    def spec(a, tile):
        if a < 4:
            return pl.BlockSpec((3, 2, CY, NZ), lambda i, tile=tile: (0, tile, 0, 0))
        return pl.BlockSpec((2, CY, NZ), lambda i, tile=tile: (tile, 0, 0))

    whole = lambda shape: pl.BlockSpec(shape, lambda i: (0,) * len(shape))
    shapes = [(9, RING, NZ), (9, RING, NZ), (8, CY, NZ)]
    return pl.pallas_call(
        edge_kernel,
        grid=(1,),
        in_specs=[pl.BlockSpec(memory_space=pltpu.SMEM)]
        + [spec(a, 0) for a in range(7)]
        + [spec(a, CX // 2 - 1) for a in range(7)]
        + [whole(above.shape), whole(below.shape)],
        out_specs=[whole(s) for s in shapes],
        out_shape=[jax.ShapeDtypeStruct(s, F32) for s in shapes],
        compiler_params=pltpu.CompilerParams(vmem_limit_bytes=VMEM_BYTES),
        cost_estimate=pl.CostEstimate(flops=1 << 24, bytes_accessed=8 << 20, transcendentals=0),
        name="solve_edges",
    )(amp, *arrays, *arrays, above, below)


def main_kernel(amp, e_f, h_f, e_a, h_a, inv, src, adj, above, below, out_f, out_a, grad, raw, mid_h, mid_e, late_h, misc, product):
    step = pl.program_id(0)
    x = jnp.minimum(step, CX - 1)
    row_dt = row_steps()

    @pl.when(step == 0)
    def _():
        raw[...] = jnp.zeros_like(raw)
        mid_h[...] = jnp.zeros_like(mid_h)
        mid_e[...] = jnp.zeros_like(mid_e)
        late_h[...] = jnp.zeros_like(late_h)
        misc[...] = jnp.zeros_like(misc)
        product[...] = jnp.zeros_like(product)

    inside = step < CX
    runs = ((e_f, h_f, src, out_f, 0), (e_a, h_a, adj, out_a, 2))
    coef_mid, coef_late = misc[0], misc[1]
    firsts, lasts = [], []
    for run, (e_ref, h_ref, s_ref, out, amp_at) in enumerate(runs):
        base = 6 * run
        ahead = tuple(
            jnp.where(inside, ring_of(e_ref[c, 0], above, below, 2 * run, c, x), 0.0) for c in range(3)
        )
        e = tuple(raw[base + c] for c in range(3))
        h = tuple(raw[base + 3 + c] for c in range(3))
        h_back = tuple(mid_h[3 * run + c] for c in range(3))
        e_late = tuple(mid_e[3 * run + c] for c in range(3))
        h_late_back = tuple(late_h[3 * run + c] for c in range(3))
        h_new = magnetic(e, ahead, h, row_dt)
        e_new = electric(e, h_new, h_back, coef_mid, amp[0, amp_at] * misc[2 + run])
        live = step <= CX
        e_new = tuple(jnp.where(live, v, 0.0) for v in e_new)
        h_last = magnetic(e_late, e_new, h_back, row_dt)
        e_last = electric(e_late, h_last, h_late_back, coef_late, amp[0, amp_at + 1] * misc[4 + run])
        for c in range(3):
            out[c, 0] = e_last[c][:CY]
        firsts.append(e_new)
        lasts.append(e_last)
        for c in range(3):
            raw[base + c] = ahead[c]
            raw[base + 3 + c] = ring_of(h_ref[c, 0], above, below, 2 * run + 1, c, x)
            mid_h[3 * run + c] = h_new[c]
            mid_e[3 * run + c] = e_new[c]
            late_h[3 * run + c] = h_last[c]
        misc[4 + run] = misc[2 + run]
        misc[2 + run] = ring_of(s_ref[0], above, below, 5 + run, 0, x)
    grad[0] = DT * (product[...] + dot_three(*[[v[:CY] for v in e] for e in lasts]))
    product[...] = dot_three(*[[v[:CY] for v in e] for e in firsts])
    misc[1] = coef_mid
    misc[0] = DT * ring_of(inv[0], above, below, 4, 0, x)

    @pl.when(step <= 1)
    def _():
        late_h[...] = jnp.zeros_like(late_h)

    @pl.when(step == 0)
    def _():
        mid_h[...] = jnp.zeros_like(mid_h)
        mid_e[...] = jnp.zeros_like(mid_e)


def solve_main(amp, arrays, above, below):
    held = lambda i: jnp.minimum(i, CX - 1)
    behind = lambda i: jnp.maximum(i - 2, 0)

    def spec(a):
        if a < 4:
            return pl.BlockSpec((3, 1, CY, NZ), lambda i: (0, held(i), 0, 0))
        return pl.BlockSpec((1, CY, NZ), lambda i: (held(i), 0, 0))

    whole = lambda shape: pl.BlockSpec(shape, lambda i: (0,) * len(shape))
    field = pl.BlockSpec((3, 1, CY, NZ), lambda i: (0, behind(i), 0, 0))
    return pl.pallas_call(
        main_kernel,
        grid=(CX + 2,),
        in_specs=[pl.BlockSpec(memory_space=pltpu.SMEM)]
        + [spec(a) for a in range(7)]
        + [whole(above.shape), whole(below.shape)],
        out_specs=[field, field, pl.BlockSpec((1, CY, NZ), lambda i: (behind(i), 0, 0))],
        out_shape=[
            jax.ShapeDtypeStruct((3, CX, CY, NZ), F32),
            jax.ShapeDtypeStruct((3, CX, CY, NZ), F32),
            jax.ShapeDtypeStruct((CX, CY, NZ), F32),
        ],
        scratch_shapes=[
            pltpu.VMEM((12, RING, NZ), F32),
            pltpu.VMEM((6, RING, NZ), F32),
            pltpu.VMEM((6, RING, NZ), F32),
            pltpu.VMEM((6, RING, NZ), F32),
            pltpu.VMEM((6, RING, NZ), F32),
            pltpu.VMEM((CY, NZ), F32),
        ],
        compiler_params=pltpu.CompilerParams(vmem_limit_bytes=VMEM_BYTES),
        cost_estimate=pl.CostEstimate(flops=1 << 27, bytes_accessed=24 << 20, transcendentals=0),
        name="solve_main",
    )(amp, *arrays, above, below)


def split(value):
    high = value.astype(jnp.bfloat16)
    return high, (value - high.astype(F32)).astype(jnp.bfloat16)


def exact_dot(a, b, dims):
    high, low = split(b)
    a = a.astype(jnp.bfloat16)
    return lax.dot_general(a, high, dims, preferred_element_type=F32) + lax.dot_general(
        a, low, dims, preferred_element_type=F32
    )


def correct_prev(run, from_prev, own, row_dt, present):
    e0y, e0z, e1y, e1z = (own[4 * run + k] for k in range(4))
    coef, ghost_coef = own[8], jnp.where(present, from_prev[8], 0.0)
    h1y, h1z, h2y, h2z = (from_prev[4 * run + k] for k in range(4))
    d_h1y, d_h1z = DT * e0z, -DT * e0y
    h1y = jnp.where(present, h1y + d_h1y, 0.0)
    h1z = jnp.where(present, h1z + d_h1z, 0.0)
    d_e1y, d_e1z = coef * h1z, -coef * h1y
    g_e1x = ghost_coef * (minus_y(d_h1z) - minus_z(d_h1y))
    g_e1y, g_e1z = -ghost_coef * d_h1z, ghost_coef * d_h1y
    h2y = jnp.where(present, h2y + d_h1y - DT * (plus_z(g_e1x) - (e1z + d_e1z - g_e1z)), 0.0)
    h2z = jnp.where(present, h2z + d_h1z - DT * ((e1y + d_e1y - g_e1y) - plus_y(g_e1x)), 0.0)
    d_h2x = -row_dt * (plus_y(d_e1z) - plus_z(d_e1y))
    d_h2y, d_h2z = -row_dt * d_e1z, row_dt * d_e1y
    first = (None, d_e1y, d_e1z)
    last = (
        coef * (minus_y(d_h2z) - minus_z(d_h2y)),
        d_e1y + coef * (minus_z(d_h2x) - d_h2z + h2z),
        d_e1z + coef * (d_h2y - h2y - minus_y(d_h2x)),
    )
    return first, last, d_h2y, d_h2z


def correct_next(run, from_next, own, row_dt, present):
    e0y, e0z, e1y, e1z = (jnp.where(present, from_next[4 * run + k], 0.0) for k in range(4))
    coef, ghost_coef = own[8], jnp.where(present, from_next[8], 0.0)
    h1y, h1z = own[4 * run], own[4 * run + 1]
    d_h1y, d_h1z = DT * e0z, -DT * e0y
    d_e1x = coef * (minus_y(d_h1z) - minus_z(d_h1y))
    d_e1y, d_e1z = -coef * d_h1z, coef * d_h1y
    e1y = e1y + ghost_coef * (h1z + d_h1z)
    e1z = e1z - ghost_coef * (h1y + d_h1y)
    d_h2x = -row_dt * (plus_y(d_e1z) - plus_z(d_e1y))
    d_h2y = d_h1y - row_dt * (plus_z(d_e1x) - (e1z - d_e1z))
    d_h2z = d_h1z - row_dt * ((e1y - d_e1y) - plus_y(d_e1x))
    b_h2y, b_h2z = row_dt * d_e1z, -row_dt * d_e1y
    first = (d_e1x, d_e1y, d_e1z)
    last = (
        d_e1x + coef * (minus_y(d_h2z) - minus_z(d_h2y)),
        d_e1y + coef * (minus_z(d_h2x) - d_h2z + b_h2z),
        d_e1z + coef * (d_h2y - b_h2y - minus_y(d_h2x)),
    )
    return first, last, b_h2y, b_h2z


def correct_kernel(
    owner, slot, from_prev, from_next, to_prev, to_next, keep, inv, grad, fields_f, fields_a, out_f, out_a, rows_out, chosen, work
):
    step = pl.program_id(0)
    place = lax.axis_index("gx")
    has_prev, has_next = place > 0, place < lax.axis_size("gx") - 1
    row_dt = row_steps()
    work[...] = grad[...]

    def finish(edge_at, inner_at, firsts, lasts, d_inner, inner_coef, base_first):
        total_f, total_a, inner_f, inner_a = [], [], [], []
        before = jnp.zeros((CY, NZ), F32)
        for c in range(3):
            before = before + fields_f[c, inner_at] * fields_a[c, inner_at]
        for run, (ref, out, total, inner) in enumerate(
            [(fields_f, out_f, total_f, inner_f), (fields_a, out_a, total_a, inner_a)]
        ):
            for c in range(3):
                total.append(ref[c, edge_at] + lasts[run][c][:CY])
                out[c, edge_at] = total[c]
                add = d_inner[run][c]
                inner.append(ref[c, inner_at] if add is None else ref[c, inner_at] + inner_coef * add[:CY])
                out[c, inner_at] = inner[c]
        e1 = [
            [base_first[run][c] if firsts[run][c] is None else base_first[run][c] + firsts[run][c][:CY] for c in range(3)]
            for run in range(2)
        ]
        edge_grad = DT * (dot_three(e1[0], e1[1]) + dot_three(total_f, total_a))
        inner_change = DT * (dot_three(inner_f, inner_a) - before)
        return edge_grad, inner_change

    @pl.when(step == 0)
    def _():
        firsts, lasts, d_inner, base = [], [], [], []
        for run in range(2):
            first, last, d_h2y, d_h2z = correct_prev(run, from_prev, to_prev, row_dt, has_prev)
            firsts.append(first)
            lasts.append(last)
            d_inner.append((None, d_h2z, -d_h2y))
            base.append((keep[4 * run], to_prev[4 * run + 2][:CY], to_prev[4 * run + 3][:CY]))
        edge, inner = finish(0, 1, firsts, lasts, d_inner, DT * inv[1], base)
        work[0] = edge
        work[1] = work[1] + inner

    @pl.when(step == 2)
    def _():
        firsts, lasts, d_inner, base = [], [], [], []
        for run in range(2):
            first, last, b_h2y, b_h2z = correct_next(run, from_next, to_next, row_dt, has_next)
            firsts.append(first)
            lasts.append(last)
            d_inner.append((minus_y(b_h2z) - minus_z(b_h2y), -b_h2z, b_h2y))
            base.append(tuple(keep[4 * run + 1 + c] for c in range(3)))
        edge, inner = finish(1, 0, firsts, lasts, d_inner, DT * inv[0], base)
        work[3] = edge
        work[2] = work[2] + inner

    devices = rows_out.shape[0]

    @pl.when(step == 0)
    def _():
        lanes = lanes_iota((devices, NZ))
        blocks = lax.broadcasted_iota(jnp.int32, (NZ // BZ, NZ), 0)
        spread = (blocks == lanes_iota((NZ // BZ, NZ)) // BZ).astype(jnp.bfloat16)
        numbers = jnp.concatenate([owner[...], slot[...], jnp.zeros((14, NZ // BZ), F32)], axis=0)
        numbers = jnp.dot(numbers.astype(jnp.bfloat16), spread, preferred_element_type=F32)
        mine = numbers[0:1, :] == rows_iota((devices, NZ)).astype(F32)
        for part in range(BZ):
            chosen[pl.ds(part * devices, devices), :] = jnp.where(mine & (lanes % BZ == part), 1.0, 0.0).astype(
                jnp.bfloat16
            )
        found = jnp.sum(jnp.where(mine & (lanes % BZ == 0), numbers[1:2, :] + 1.0, 0.0), axis=1, keepdims=True) - 1.0
        rows_out[:, 0, BZ * CX * CY :] = jnp.broadcast_to(found, (devices, 128))

    cells = exact_dot(chosen[...], work[...].reshape(4 * CY, NZ), (((1,), (1,)), ((), ())))
    quarter = jnp.where(step < 2, step, 5 - step)
    for q in range(4):

        @pl.when(quarter == q)
        def _():
            for part in range(BZ):
                at = part * CX * CY + q * 4 * CY
                rows_out[:, 0, at : at + 4 * CY] = cells[part * devices : (part + 1) * devices]


def correct_and_pack(owner, slot, from_prev, from_next, to_prev, to_next, keep, inv, grad, fields_f, fields_a, devices):
    whole = lambda shape: pl.BlockSpec(shape, lambda i: (0,) * len(shape))
    end = lambda i: jnp.where(i < 2, 0, CX // 2 - 1)
    field = pl.BlockSpec((3, 2, CY, NZ), lambda i: (0, end(i), 0, 0))
    width = BZ * CX * CY + 128
    return pl.pallas_call(
        correct_kernel,
        grid=(4,),
        in_specs=[
            whole((1, NZ // BZ)),
            whole((1, NZ // BZ)),
            whole((9, RING, NZ)),
            whole((9, RING, NZ)),
            whole((9, RING, NZ)),
            whole((9, RING, NZ)),
            whole((8, CY, NZ)),
            pl.BlockSpec((2, CY, NZ), lambda i: (end(i), 0, 0)),
            pl.BlockSpec((4, CY, NZ), lambda i: (jnp.where(i < 2, i, 5 - i), 0, 0)),
            field,
            field,
        ],
        out_specs=[field, field, whole((devices, 1, width))],
        out_shape=[
            jax.ShapeDtypeStruct((3, CX, CY, NZ), F32),
            jax.ShapeDtypeStruct((3, CX, CY, NZ), F32),
            jax.ShapeDtypeStruct((devices, 1, width), F32),
        ],
        scratch_shapes=[pltpu.VMEM((BZ * devices, NZ), jnp.bfloat16), pltpu.VMEM((4, CY, NZ), F32)],
        input_output_aliases={9: 0, 10: 1},
        compiler_params=pltpu.CompilerParams(vmem_limit_bytes=VMEM_BYTES),
        cost_estimate=pl.CostEstimate(flops=1 << 30, bytes_accessed=10 << 20, transcendentals=0),
        name="correct_and_pack",
    )(owner, slot, from_prev, from_next, to_prev, to_next, keep, inv, grad, fields_f, fields_a)


def place_kernel(got, out):
    devices = got.shape[0]
    owned = out.shape[0]
    cells = BZ * CX * CY
    numbers = got[:, 0, cells:]
    wanted = (numbers == lanes_iota((devices, 128)).astype(F32)).astype(F32)
    placing = jnp.transpose(wanted)[:owned]
    order_from = rows_iota((4 * 128, 4 * 128))
    order_to = lanes_iota((4 * 128, 4 * 128))
    order = (order_from == (order_to % BZ) * 128 + order_to // BZ).astype(jnp.bfloat16)
    dims = (((1,), (0,)), ((), ()))
    for q in range(4):
        parts = [got[:, 0, part * CX * CY + q * 128 : part * CX * CY + (q + 1) * 128] for part in range(BZ)]
        rows = exact_dot(placing, jnp.concatenate(parts, axis=1), dims)
        high, low = split(rows)
        out[:, q * 512 : (q + 1) * 512] = lax.dot_general(
            high, order, dims, preferred_element_type=F32
        ) + lax.dot_general(low, order, dims, preferred_element_type=F32)


def place_rows(got, owned):
    return pl.pallas_call(
        place_kernel,
        out_shape=jax.ShapeDtypeStruct((owned, BZ * CX * CY), F32),
        compiler_params=pltpu.CompilerParams(vmem_limit_bytes=VMEM_BYTES),
        cost_estimate=pl.CostEstimate(flops=1 << 28, bytes_accessed=2 << 20, transcendentals=0),
        name="place_rows",
    )(got)


def amplitude(tick):
    return jnp.sin(RATE * jnp.remainder(tick, PERIOD).astype(F32))


def body(e_forward, h_forward, e_adjoint, h_adjoint, inv_eps, source, adj_source, design_mask, param_map, step_index):
    arrays = (e_forward, h_forward, e_adjoint, h_adjoint, inv_eps, source, adj_source)
    devices = lax.axis_size("gx") * lax.axis_size("gy")
    blocks = NZ // BZ
    owned = blocks // 2
    start = step_index[0]
    amp = amplitude(start + jnp.array([1, 2, -1, -2], jnp.int32)).reshape(1, 4)
    owner = jnp.where(design_mask == 1, param_map // owned, -1).reshape(1, blocks).astype(F32)
    slot = (param_map % owned).reshape(1, blocks).astype(F32)

    up, down = pack_rows(arrays)
    above, below = cycled(up, "gy", 1), cycled(down, "gy", -1)
    to_prev, to_next, keep = solve_edges(amp, arrays, above, below)
    from_next, from_prev = cycled(to_prev, "gx", -1), cycled(to_next, "gx", 1)
    fields_f, fields_a, grad = solve_main(amp, arrays, above, below)
    fields_f, fields_a, rows = correct_and_pack(
        owner, slot, from_prev, from_next, to_prev, to_next, keep, inv_eps, grad, fields_f, fields_a, devices
    )
    got = lax.all_to_all(rows, ("gx", "gy"), split_axis=0, concat_axis=0, tiled=True)
    return place_rows(got, owned), fields_f, fields_a


def solution(mesh):
    field, cells = P(None, "gx", "gy", None), P("gx", "gy", None)
    in_specs = (field, field, field, field, cells, cells, cells, cells, cells, P())
    out_specs = (P(("gx", "gy"), None), field, field)
    return jax.shard_map(body, mesh=mesh, in_specs=in_specs, out_specs=out_specs, check_vma=False)
```

```python
import functools
import math

import jax
import jax.numpy as jnp
from jax import lax
from jax.experimental import pallas as pl
from jax.experimental.pallas import tpu as pltpu
from jax.sharding import PartitionSpec as P

BZ = 4
STEPS = 2
DT = 0.5
PERIOD = 20
RATE = 2.0 * math.pi / 20.0
CX, CY, NZ = 16, 32, 512
RING = 40
F32 = jnp.float32
VMEM_BYTES = (64 << 20) - (128 << 10)

UP, DOWN = 14, 10


def cycled(value, axis, by):
    devices = lax.axis_size(axis)
    return lax.ppermute(value, axis, [(i, (i + by) % devices) for i in range(devices)])


def rows_iota(shape):
    return lax.broadcasted_iota(jnp.int32, shape, 0)


def lanes_iota(shape):
    return lax.broadcasted_iota(jnp.int32, shape, 1)


def plus_y(f):
    return pltpu.roll(f, f.shape[0] - 1, 0) - f


def minus_y(f):
    return f - pltpu.roll(f, 1, 0)


def plus_z(f):
    return jnp.where(lanes_iota(f.shape) == NZ - 1, 0.0, pltpu.roll(f, NZ - 1, 1)) - f


def minus_z(f):
    return f - jnp.where(lanes_iota(f.shape) == 0, 0.0, pltpu.roll(f, 1, 1))


def magnetic(e, e_next, h, row_dt):
    ahead_y = -e[1] if e_next is None else e_next[1] - e[1]
    ahead_z = -e[2] if e_next is None else e_next[2] - e[2]
    return (
        h[0] - row_dt * (plus_y(e[2]) - plus_z(e[1])),
        h[1] - row_dt * (plus_z(e[0]) - ahead_z),
        h[2] - row_dt * (ahead_y - plus_y(e[0])),
    )


def electric(e, h, h_prev, coef, drive):
    back_y = h[1] if h_prev is None else h[1] - h_prev[1]
    back_z = h[2] if h_prev is None else h[2] - h_prev[2]
    return (
        e[0] + coef * (minus_y(h[2]) - minus_z(h[1])),
        e[1] + coef * (minus_z(h[0]) - back_z),
        e[2] + coef * (back_y - minus_y(h[0]) - drive),
    )


def amplitude(step_index, ticks, rows):
    tick = lax.rem(step_index[0] + (PERIOD + ticks), PERIOD)
    tile = jnp.sin(RATE * jnp.full((8, 128), tick, jnp.int32).astype(F32))
    return jnp.concatenate([jnp.concatenate([tile] * (NZ // 128), axis=1)] * (rows // 8), axis=0)


def dot_three(a, b):
    return a[0] * b[0] + a[1] * b[1] + a[2] * b[2]


def plus_x(f):
    return jnp.where(rows_iota(f.shape) == f.shape[0] - 1, 0.0, pltpu.roll(f, f.shape[0] - 1, 0)) - f


def minus_x(f):
    return f - jnp.where(rows_iota(f.shape) == 0, 0.0, pltpu.roll(f, 1, 0))


def has_rows():
    place = lax.axis_index("gy")
    return place < lax.axis_size("gy") - 1, place > 0


def row_steps():
    _, has_above = has_rows()
    rows = rows_iota((8, NZ))
    tile = jnp.where((rows >= 6) & jnp.logical_not(has_above), 0.0, DT)
    return jnp.concatenate([jnp.full((CY, NZ), DT, F32), tile], axis=0)


def ring_steps():
    _, has_above = has_rows()
    tile = jnp.where((rows_iota((8, NZ)) == 7) & has_above, DT, 0.0)
    return jnp.concatenate([jnp.full((CY, NZ), DT, F32), tile], axis=0)


class Ghosts:
    def __init__(self, above, below, x):
        has_below, has_above = has_rows()
        self.refs = above, below
        self.flags = jnp.where(has_above, 1.0, 0.0).astype(F32), jnp.where(has_below, 1.0, 0.0).astype(F32)
        self.x = x

    def up(self, k, x=None):
        return self.refs[0][k, pl.ds(self.x if x is None else x, 1), :] * self.flags[0]

    def down(self, k, x=None):
        return self.refs[1][k, pl.ds(self.x if x is None else x, 1), :] * self.flags[1]

    def tile(self, rows):
        at = rows_iota((8, NZ))
        tile = jnp.zeros((8, NZ), F32)
        for row, value in rows.items():
            tile = jnp.where(at == row, value, tile)
        return tile

    def e_before(self, run):
        return (
            self.tile({0: self.down(4 * run)}),
            jnp.zeros((8, NZ), F32),
            self.tile({0: self.down(4 * run + 1)}),
        )

    def e_middle(self, run):
        return (
            self.tile({0: self.down(4 * run + 2), 7: self.up(6 * run)}),
            self.tile({7: self.up(6 * run + 1)}),
            self.tile({0: self.down(4 * run + 3), 7: self.up(6 * run + 2)}),
        )

    def h_before(self, run):
        return tuple(self.tile({7: self.up(6 * run + 3 + c)}) for c in range(3))

    def coef(self):
        return DT * self.tile({0: self.down(8), 7: self.up(12)})


def ring(own, tile):
    return jnp.concatenate([own, tile], axis=0)


def rings(own, tiles):
    return tuple(ring(own[c], tiles[c]) for c in range(3))


def rows_up(amp, e_refs, h_refs, inv, drives, out):
    coef = DT * inv[:, 7, :]
    singles = []
    for run in range(2):
        e, e_in = ([e_refs[run][c, :, r, :] for c in range(3)] for r in (7, 6))
        h, h_in = ([h_refs[run][c, :, r, :] for c in range(3)] for r in (7, 6))
        hx_in = h_in[0] - DT * ((e[2] - e_in[2]) - plus_z(e_in[1]))
        hz_in = h_in[2] - DT * (plus_x(e_in[1]) - (e[0] - e_in[0]))
        out[6 * run] = e[0] - coef * hz_in
        out[6 * run + 1] = e[1]
        out[6 * run + 2] = e[2] + coef * (hx_in - amp[run] * drives[run][:, 7, :])
        out[6 * run + 3] = h[0] + DT * (e[2] + plus_z(e[1]))
        out[6 * run + 4] = h[1] - DT * (plus_z(e[0]) - plus_x(e[2]))
        out[6 * run + 5] = h[2] - DT * (plus_x(e[1]) + e[0])
        singles += [e[2], e_in[1]]
    out[12] = inv[:, 7, :]
    rows = rows_iota((CX, NZ))
    held = singles[0]
    for k in range(1, 4):
        held = jnp.where(rows == k, pltpu.roll(singles[k], k, 0), held)
    out[13] = held


def rows_down(amp, e_refs, h_refs, inv, drives, out):
    coef = DT * inv[:, 0, :]
    singles, others = [], []
    for run in range(2):
        e, e_in = ([e_refs[run][c, :, r, :] for c in range(3)] for r in (0, 1))
        h = [h_refs[run][c, :, 0, :] for c in range(3)]
        hx = h[0] - DT * ((e_in[2] - e[2]) - plus_z(e[1]))
        hy = h[1] - DT * (plus_z(e[0]) - plus_x(e[2]))
        hz = h[2] - DT * (plus_x(e[1]) - (e_in[0] - e[0]))
        out[4 * run] = e[0]
        out[4 * run + 1] = e[2]
        out[4 * run + 2] = e[0] + coef * (hz - minus_z(hy))
        out[4 * run + 3] = e[2] + coef * (minus_x(hy) - hx - amp[run] * drives[run][:, 0, :])
        singles.append(e[1])
        others.append(hy)
    out[8] = inv[:, 0, :]
    rows = rows_iota((CX, NZ))
    held = singles[0]
    for k, (value, by) in enumerate([(singles[1], 1), (others[0], 3), (others[1], 4)], 1):
        held = jnp.where(rows == k, pltpu.roll(value, by, 0), held)
    out[9] = held


def pack_kernel(step_index, e_f, h_f, e_a, h_a, inv, src, adj, far_up, far_down, *scratch):
    sources = (e_f, h_f, e_a, h_a, inv, src, adj)
    places, (up, down, sems, out_sems) = scratch[:7], scratch[7:]
    stores = [pltpu.make_async_copy(up, far_up, out_sems.at[0]), pltpu.make_async_copy(down, far_down, out_sems.at[1])]

    def load(a, side):
        at = pl.ds(24 if side == 0 else 0, 8)
        source = sources[a].at[:, :, at] if a < 4 else sources[a].at[:, at]
        return pltpu.make_async_copy(source, places[a].at[side], sems.at[a, side])

    for side in range(2):
        for a in range(7):
            load(a, side).start()
    amp = [amplitude(step_index, ticks, CX) for ticks in (1, -1)]
    for side, (rows_of, out) in enumerate([(rows_up, up), (rows_down, down)]):
        for a in range(7):
            load(a, side).wait()
        ef, hf, ea, ha, coef, drive_f, drive_a = (place.at[side] for place in places)
        rows_of(amp, (ef, ea), (hf, ha), coef, (drive_f, drive_a), out)
        stores[side].start()
    for copy in stores:
        copy.wait()


def pack_rows(step_index, arrays):
    hbm = pl.BlockSpec(memory_space=pl.ANY)
    shapes = [(UP, CX, NZ), (DOWN, CX, NZ)]
    return pl.pallas_call(
        pack_kernel,
        in_specs=[pl.BlockSpec(memory_space=pltpu.SMEM)] + [hbm] * 7,
        out_specs=[hbm] * 2,
        out_shape=[jax.ShapeDtypeStruct(s, F32) for s in shapes],
        scratch_shapes=[pltpu.VMEM((2, 3, CX, 8, NZ), F32)] * 4
        + [pltpu.VMEM((2, CX, 8, NZ), F32)] * 3
        + [pltpu.VMEM(s, F32) for s in shapes]
        + [pltpu.SemaphoreType.DMA((7, 2)), pltpu.SemaphoreType.DMA((2,))],
        compiler_params=pltpu.CompilerParams(vmem_limit_bytes=VMEM_BYTES),
        cost_estimate=pl.CostEstimate(flops=4 * 10**9, bytes_accessed=0, transcendentals=0),
        name="pack_rows",
    )(step_index, *arrays)


def call_edges(kernel, name, step_index, arrays, messages, shapes):
    free = pl.BlockSpec(memory_space=pl.ANY)
    count = len(messages)

    def body(step_index, *refs):
        sources, far_outs = refs[: 7 + count], refs[7 + count : 7 + count + len(shapes)]
        places, outs = refs[7 + count + len(shapes) : -2 - len(shapes)], refs[-2 - len(shapes) : -2]
        sems, out_sems = refs[-2:]
        copies = []
        for a in range(7):
            for side in range(2):
                at = pl.ds(side * (CX - 2), 2)
                source = sources[a].at[:, at] if a < 4 else sources[a].at[at]
                copies.append(pltpu.make_async_copy(source, places[a].at[side], sems.at[a, side]))
        for k in range(count):
            copies.append(pltpu.make_async_copy(sources[7 + k], places[7 + k], sems.at[7 + k, 0]))
        for copy in copies:
            copy.start()
        for copy in copies:
            copy.wait()
        sides = [places[a].at[side] for side in range(2) for a in range(7)]
        kernel(step_index, *sides, *places[7:], *outs)
        copies = [pltpu.make_async_copy(a, b, out_sems.at[k]) for k, (a, b) in enumerate(zip(outs, far_outs))]
        for copy in copies:
            copy.start()
        for copy in copies:
            copy.wait()

    return pl.pallas_call(
        body,
        in_specs=[pl.BlockSpec(memory_space=pltpu.SMEM)] + [free] * (7 + count),
        out_specs=[free] * len(shapes),
        out_shape=[jax.ShapeDtypeStruct(s, F32) for s in shapes],
        scratch_shapes=[pltpu.VMEM((2, 3, 2, CY, NZ), F32)] * 4
        + [pltpu.VMEM((2, 2, CY, NZ), F32)] * 3
        + [pltpu.VMEM(m.shape, F32) for m in messages]
        + [pltpu.VMEM(s, F32) for s in shapes]
        + [pltpu.SemaphoreType.DMA((7 + count, 2)), pltpu.SemaphoreType.DMA((len(shapes),))],
        compiler_params=pltpu.CompilerParams(vmem_limit_bytes=VMEM_BYTES),
        cost_estimate=pl.CostEstimate(flops=3 * 10**9, bytes_accessed=0, transcendentals=0),
        name=name,
    )(step_index, *arrays, *messages)


def edge_kernel(step_index, e_f0, h_f0, e_a0, h_a0, inv0, src0, adj0, e_f1, h_f1, e_a1, h_a1, inv1, src1, adj1, above, below, to_prev, to_next, keep):
    row_dt = ring_steps()
    ghosts = {x: Ghosts(above, below, x) for x in (0, 1, CX - 2, CX - 1)}
    still = jnp.zeros((8, NZ), F32)
    amp = [amplitude(step_index, ticks, CY) for ticks in (1, -1)]

    def before(ref, at, run, x):
        return rings([ref[c, at] for c in range(3)], ghosts[x].e_before(run))

    def middle(ref, at, run, x):
        return rings([ref[c, at] for c in range(3)], ghosts[x].e_middle(run))

    def magnet(ref, at, run, x):
        return rings([ref[c, at] for c in range(3)], ghosts[x].h_before(run))

    coef_first = ring(DT * inv0[0], ghosts[0].coef())
    coef_last = ring(DT * inv1[1], ghosts[CX - 1].coef())
    to_prev[8] = coef_first
    to_next[8] = coef_last
    for run, (e0, h0, s0, e1, h1, s1) in enumerate(
        [(e_f0, h_f0, src0, e_f1, h_f1, src1), (e_a0, h_a0, adj0, e_a1, h_a1, adj1)]
    ):
        near = ghosts[0]
        h = magnetic(before(e0, 0, run, 0), before(e0, 1, run, 1), magnet(h0, 0, run, 0), row_dt)
        drive = ring(amp[run] * s0[0], still)
        new = electric(middle(e0, 0, run, 0), h, None, coef_first, drive)
        sides_y = {0: near.down(9, run), 6: near.up(13, 2 * run + 1), 7: near.up(6 * run + 1)}
        sides_z = {0: near.down(4 * run + 1), 7: near.up(13, 2 * run)}
        to_prev[4 * run] = ring(e0[1, 0], near.tile(sides_y))
        to_prev[4 * run + 1] = ring(e0[2, 0], near.tile(sides_z))
        to_prev[4 * run + 2] = new[1]
        to_prev[4 * run + 3] = new[2]
        keep[4 * run] = new[0][:CY]
        e, back = before(e1, 1, run, CX - 1), before(e1, 0, run, CX - 2)
        h = magnetic(e, None, magnet(h1, 1, run, CX - 1), row_dt)
        h_back = magnetic(back, e, magnet(h1, 0, run, CX - 2), row_dt)
        drive = ring(amp[run] * s1[1], still)
        new = electric(middle(e1, 1, run, CX - 1), h, h_back, coef_last, drive)
        later = magnetic(new, None, h, row_dt)
        beyond = ghosts[CX - 1].down(9, 2 + run)
        to_next[4 * run] = jnp.where(rows_iota((RING, NZ)) == CY, beyond, h[1])
        to_next[4 * run + 1] = h[2]
        to_next[4 * run + 2] = later[1]
        to_next[4 * run + 3] = later[2]
        for c in range(3):
            keep[4 * run + 1 + c] = new[c][:CY]


def solve_edges(step_index, arrays, above, below):
    shapes = [(9, RING, NZ), (9, RING, NZ), (8, CY, NZ)]
    return call_edges(edge_kernel, "solve_edges", step_index, arrays, [above, below], shapes)


CHUNK = 2
DRAIN = 4


def zplus(tile):
    moved = pltpu.roll(tile, NZ - 1, 1)
    last = jnp.where(lanes_iota((8, 128)) == 127, 0.0, moved[:, NZ - 128 :])
    return jnp.concatenate([moved[:, : NZ - 128], last], axis=1) - tile


def zminus(tile):
    moved = pltpu.roll(tile, 1, 1)
    first = jnp.where(lanes_iota((8, 128)) == 0, 0.0, moved[:, :128])
    return tile - jnp.concatenate([first, moved[:, 128:]], axis=1)


def magnetic_tiles(tiles, e, e_next, h, row_dts, put, closed):
    end = rows_iota((8, NZ)) == 7
    firsts = {c: pltpu.roll(e(c, 0), 7, 0) for c in (0, 2)}
    here = firsts
    for t in range(tiles):
        if t == tiles - 1:
            after = {c: jnp.zeros((8, NZ), F32) for c in (0, 2)} if closed else firsts
        else:
            after = {c: pltpu.roll(e(c, t + 1), 7, 0) for c in (0, 2)}
        ex, ey, ez = (e(c, t) for c in range(3))
        put(0, t, h(0, t) - row_dts[t] * ((jnp.where(end, after[2], here[2]) - ez) - zplus(ey)))
        put(1, t, h(1, t) - row_dts[t] * (zplus(ex) - (e_next(2, t) - ez)))
        put(2, t, h(2, t) - row_dts[t] * ((e_next(1, t) - ey) - (jnp.where(end, after[0], here[0]) - ex)))
        here = after


def electric_tile(e, h, h_prev, coef, drive, t, rolled):
    start = rows_iota((8, NZ)) == 0
    hx, hy, hz = (h(c, t) for c in range(3))
    moved = {0: pltpu.roll(hx, 1, 0), 2: pltpu.roll(hz, 1, 0)}
    new_x = e(0, t) + coef * ((hz - jnp.where(start, rolled[2], moved[2])) - zminus(hy))
    new_y = e(1, t) + coef * (zminus(hx) - (hz - h_prev(2, t)))
    curl = (hy - h_prev(1, t)) - (hx - jnp.where(start, rolled[0], moved[0]))
    new_z = e(2, t) + coef * (curl if drive is None else curl - drive)
    return (new_x, new_y, new_z), moved


def sweep(step_index, places, load, store, mid_h, mid_e, late_h, tiles, at_rows, ghosts, put_last):
    v_ef, v_hf, v_ea, v_ha, v_inv, v_src, v_adj = places
    height = v_ef.shape[2]
    own = [t for t in range(tiles) if at_rows[t] is not None]
    closed = len(own) == tiles
    mid_h[...] = jnp.zeros_like(mid_h)
    late_h[...] = jnp.zeros_like(late_h)
    v_ef[:, CX] = jnp.zeros((3, height, NZ), F32)
    v_ea[:, CX] = jnp.zeros((3, height, NZ), F32)
    for a in range(7):
        load(a, 0).wait()
    ghost_dt = None if closed else ring_steps()[CY:]
    row_dts = [DT if t in own else ghost_dt for t in range(tiles)]
    amp = [[amplitude(step_index, ticks, 8) for ticks in pair] for pair in ((1, 2), (-1, -2))]
    runs = ((v_ef, v_hf, v_src), (v_ea, v_ha, v_adj))
    nothing = {c: jnp.zeros((8, NZ), F32) for c in (0, 2)}

    def rows(t):
        return pl.ds(at_rows[t], 8)

    def ring_rows(t):
        return pl.ds(8 * t, 8)

    def one(step, carry):
        @pl.when((step % CHUNK == 0) & (step < CX))
        def _():
            for a in range(7):
                load(a, step // CHUNK).wait()

        now, then = lax.rem(step, 2), lax.rem(step + 1, 2)

        @pl.when(step <= CX)
        def _():
            x = step - 1
            inside = step < CX
            if not closed:
                here, there = ghosts(x), ghosts(jnp.minimum(step, CX - 1))
                coef_ghost = here.coef()
            for run, (e_ref, h_ref, s_ref) in enumerate(runs):
                beside = beside_next = beside_h = middle = None
                if not closed:
                    beside = here.e_before(run)
                    beside_next = [jnp.where(inside, v, 0.0) for v in there.e_before(run)]
                    beside_h = here.h_before(run)
                    middle = here.e_middle(run)

                def put_h(c, t, value):
                    mid_h[now, 3 * run + c, ring_rows(t), :] = value

                magnetic_tiles(
                    tiles,
                    lambda c, t: e_ref[c, x, rows(t), :] if t in own else beside[c],
                    lambda c, t: e_ref[c, step, rows(t), :] if t in own else beside_next[c],
                    lambda c, t: h_ref[c, x, rows(t), :] if t in own else beside_h[c],
                    row_dts,
                    put_h,
                    closed,
                )
                rolled = nothing
                if not closed:
                    end = ring_rows(tiles - 1)
                    rolled = {c: pltpu.roll(mid_h[now, 3 * run + c, end, :], 1, 0) for c in (0, 2)}
                for t in range(tiles):
                    if t in own:
                        coef, drive = DT * v_inv[x, rows(t), :], amp[run][0] * s_ref[x, rows(t), :]
                    else:
                        coef, drive = coef_ghost, None
                    new, rolled = electric_tile(
                        lambda c, t: e_ref[c, x, rows(t), :] if t in own else middle[c],
                        lambda c, t: mid_h[now, 3 * run + c, ring_rows(t), :],
                        lambda c, t: mid_h[then, 3 * run + c, ring_rows(t), :],
                        coef,
                        drive,
                        t,
                        rolled,
                    )
                    for c in range(3):
                        mid_e[now, 3 * run + c, ring_rows(t), :] = new[c]

        @pl.when(step > CX)
        def _():
            mid_e[now] = jnp.zeros((6, 8 * tiles, NZ), F32)

        @pl.when(step > 1)
        def _():
            x = step - 2
            rolled = [nothing, nothing]
            for run in range(2):

                def put_late(c, t, value):
                    late_h[now, 3 * run + c, ring_rows(t), :] = value

                magnetic_tiles(
                    tiles,
                    lambda c, t: mid_e[then, 3 * run + c, ring_rows(t), :],
                    lambda c, t: mid_e[now, 3 * run + c, ring_rows(t), :],
                    lambda c, t: mid_h[then, 3 * run + c, ring_rows(t), :],
                    row_dts,
                    put_late,
                    closed,
                )
            for t in range(tiles):
                if t not in own:
                    rolled = [
                        {c: pltpu.roll(late_h[now, 3 * run + c, ring_rows(t), :], 1, 0) for c in (0, 2)}
                        for run in range(2)
                    ]
                    continue
                coef = DT * v_inv[x, rows(t), :]
                new = [None, None]
                for run, (e_ref, _, s_ref) in enumerate(runs):
                    new[run], rolled[run] = electric_tile(
                        lambda c, t: mid_e[then, 3 * run + c, ring_rows(t), :],
                        lambda c, t: late_h[now, 3 * run + c, ring_rows(t), :],
                        lambda c, t: late_h[then, 3 * run + c, ring_rows(t), :],
                        coef,
                        amp[run][1] * s_ref[x, rows(t), :],
                        t,
                        rolled[run],
                    )
                first = [[mid_e[then, 3 * run + c, ring_rows(t), :] for c in range(3)] for run in range(2)]
                put_last(x, t, new, DT * (dot_three(*first) + dot_three(*new)))

        @pl.when((step > 2) & (step % DRAIN == 1))
        def _():
            for a in range(3):
                store(a, step // DRAIN - 1).start()

        return carry

    lax.fori_loop(1, CX + 2, one, 0)
    for part in range(CX // DRAIN):
        for a in range(3):
            store(a, part).wait()


def main_kernel(
    step_index, e_f, h_f, e_a, h_a, inv, src, adj, far_above, far_below, out_f, out_a, out_g,
    v_ef, v_hf, v_ea, v_ha, v_inv, v_src, v_adj, grad, mid_h, mid_e, late_h, above, below, load_sem, store_sem, row_sem,
):
    messages = [
        pltpu.make_async_copy(far_above, above, row_sem.at[0]),
        pltpu.make_async_copy(far_below, below, row_sem.at[1]),
    ]
    for copy in messages:
        copy.start()
    sources = (e_f, h_f, e_a, h_a, inv, src, adj)
    places = (v_ef, v_hf, v_ea, v_ha, v_inv, v_src, v_adj)

    def load(a, chunk):
        at = pl.ds(chunk * CHUNK, CHUNK)
        if a < 4:
            return pltpu.make_async_copy(sources[a].at[:, at], places[a].at[:, at], load_sem.at[a, chunk])
        return pltpu.make_async_copy(sources[a].at[at], places[a].at[at], load_sem.at[a, chunk])

    def store(a, part):
        at = pl.ds(part * DRAIN, DRAIN)
        if a < 2:
            return pltpu.make_async_copy((v_ef, v_ea)[a].at[:, at], (out_f, out_a)[a].at[:, at], store_sem.at[a, part])
        return pltpu.make_async_copy(grad.at[at], out_g.at[at], store_sem.at[a, part])

    def put_last(x, t, new, product):
        for c in range(3):
            v_ef[c, x, pl.ds(8 * t - 8, 8), :] = new[0][c]
            v_ea[c, x, pl.ds(8 * t - 8, 8), :] = new[1][c]
        grad[x, pl.ds(8 * t - 8, 8), :] = product

    for chunk in range(CX // CHUNK):
        for a in range(7):
            load(a, chunk).start()
    for copy in messages:
        copy.wait()
    sweep(
        step_index, places, load, store, mid_h, mid_e, late_h, 5, [None, 0, 8, 16, 24],
        lambda x: Ghosts(above, below, x), put_last,
    )


def solve_main(step_index, arrays, above, below):
    hbm = pl.BlockSpec(memory_space=pl.ANY)
    field, cells = (3, CX, CY, NZ), (CX, CY, NZ)
    return pl.pallas_call(
        main_kernel,
        in_specs=[pl.BlockSpec(memory_space=pltpu.SMEM)] + [hbm] * 9,
        out_specs=[hbm] * 3,
        out_shape=[jax.ShapeDtypeStruct(s, F32) for s in (field, field, cells)],
        scratch_shapes=[pltpu.VMEM((3, CX + 1, CY, NZ), F32), pltpu.VMEM(field, F32)] * 2
        + [pltpu.VMEM(cells, F32)] * 4
        + [pltpu.VMEM((2, 6, RING, NZ), F32)] * 3
        + [pltpu.VMEM(above.shape, F32), pltpu.VMEM(below.shape, F32)]
        + [pltpu.SemaphoreType.DMA(s) for s in ((7, CX // CHUNK), (3, CX // DRAIN), (2,))],
        compiler_params=pltpu.CompilerParams(vmem_limit_bytes=VMEM_BYTES),
        cost_estimate=pl.CostEstimate(flops=14 * 10**9, bytes_accessed=0, transcendentals=0),
        name="solve_main",
    )(step_index, *arrays, above, below)


def split(value):
    high = value.astype(jnp.bfloat16)
    return high, (value - high.astype(F32)).astype(jnp.bfloat16)


def exact_dot(a, b, dims):
    high, low = split(b)
    a = a.astype(jnp.bfloat16)
    return lax.dot_general(a, high, dims, preferred_element_type=F32) + lax.dot_general(
        a, low, dims, preferred_element_type=F32
    )


def correct_prev(run, from_prev, own, row_dt, present):
    e0y, e0z, e1y, e1z = (own[4 * run + k] for k in range(4))
    coef, ghost_coef = own[8], jnp.where(present, from_prev[8], 0.0)
    h1y, h1z, h2y, h2z = (from_prev[4 * run + k] for k in range(4))
    d_h1y, d_h1z = DT * e0z, -DT * e0y
    h1y = jnp.where(present, h1y + d_h1y, 0.0)
    h1z = jnp.where(present, h1z + d_h1z, 0.0)
    d_e1y, d_e1z = coef * h1z, -coef * h1y
    g_e1x = ghost_coef * (minus_y(d_h1z) - minus_z(d_h1y))
    g_e1y, g_e1z = -ghost_coef * d_h1z, ghost_coef * d_h1y
    h2y = jnp.where(present, h2y + d_h1y - DT * (plus_z(g_e1x) - (e1z + d_e1z - g_e1z)), 0.0)
    h2z = jnp.where(present, h2z + d_h1z - DT * ((e1y + d_e1y - g_e1y) - plus_y(g_e1x)), 0.0)
    d_h2x = -row_dt * (plus_y(d_e1z) - plus_z(d_e1y))
    d_h2y, d_h2z = -row_dt * d_e1z, row_dt * d_e1y
    first = (None, d_e1y, d_e1z)
    last = (
        coef * (minus_y(d_h2z) - minus_z(d_h2y)),
        d_e1y + coef * (minus_z(d_h2x) - d_h2z + h2z),
        d_e1z + coef * (d_h2y - h2y - minus_y(d_h2x)),
    )
    return first, last, d_h2y, d_h2z


def correct_next(run, from_next, own, row_dt, present):
    e0y, e0z, e1y, e1z = (jnp.where(present, from_next[4 * run + k], 0.0) for k in range(4))
    coef, ghost_coef = own[8], jnp.where(present, from_next[8], 0.0)
    h1y, h1z = own[4 * run], own[4 * run + 1]
    d_h1y, d_h1z = DT * e0z, -DT * e0y
    d_e1x = coef * (minus_y(d_h1z) - minus_z(d_h1y))
    d_e1y, d_e1z = -coef * d_h1z, coef * d_h1y
    e1y = e1y + ghost_coef * (h1z + d_h1z)
    e1z = e1z - ghost_coef * (h1y + d_h1y)
    d_h2x = -row_dt * (plus_y(d_e1z) - plus_z(d_e1y))
    d_h2y = d_h1y - row_dt * (plus_z(d_e1x) - (e1z - d_e1z))
    d_h2z = d_h1z - row_dt * ((e1y - d_e1y) - plus_y(d_e1x))
    b_h2y, b_h2z = row_dt * d_e1z, -row_dt * d_e1y
    first = (d_e1x, d_e1y, d_e1z)
    last = (
        d_e1x + coef * (minus_y(d_h2z) - minus_z(d_h2y)),
        d_e1y + coef * (minus_z(d_h2x) - d_h2z + b_h2z),
        d_e1z + coef * (d_h2y - b_h2y - minus_y(d_h2x)),
    )
    return first, last, b_h2y, b_h2z


def correct_kernel(
    mask, param, *refs
):
    far, refs = refs[:5], refs[5:]
    far_inv, far_grad, old_f, old_a, out_f, out_a, far_rows, *refs = refs
    near, refs = refs[:5], refs[5:]
    (
    v_inv, work, v_f, v_a, chosen, rows_out,
    message_sem, inv_sem, grad_sem, field_sem, store_sem, rows_sem,
    ) = refs
    from_prev, to_prev, keep, from_next, to_next = near
    place = lax.axis_index("gx")
    has_prev, has_next = place > 0, place < lax.axis_size("gx") - 1
    row_dt = row_steps()
    messages = [pltpu.make_async_copy(a, b, message_sem.at[k]) for k, (a, b) in enumerate(zip(far, near))]
    grads = [
        pltpu.make_async_copy(far_grad.at[pl.ds(4 * q, 4)], work.at[pl.ds(4 * q, 4)], grad_sem.at[q]) for q in range(4)
    ]
    ends, stores = [], []
    for side in range(2):
        at = pl.ds(side * (CX - 2), 2)
        ends.append(
            [
                pltpu.make_async_copy(far_inv.at[at], v_inv.at[side], inv_sem.at[side]),
                pltpu.make_async_copy(old_f.at[:, at], v_f.at[side], field_sem.at[0, side]),
                pltpu.make_async_copy(old_a.at[:, at], v_a.at[side], field_sem.at[1, side]),
            ]
        )
        stores.append(
            [
                pltpu.make_async_copy(v_f.at[side], out_f.at[:, at], store_sem.at[0, side]),
                pltpu.make_async_copy(v_a.at[side], out_a.at[:, at], store_sem.at[1, side]),
            ]
        )
    for copy in [grads[1], grads[2], *messages[:3], *ends[0], grads[0], *messages[3:], *ends[1], grads[3]]:
        copy.start()

    def finish(side, edge_at, inner_at, firsts, lasts, d_inner, inner_coef, base_first):
        total_f, total_a, inner_f, inner_a = [], [], [], []
        fields_f, fields_a = v_f.at[side], v_a.at[side]
        before = jnp.zeros((CY, NZ), F32)
        for c in range(3):
            before = before + fields_f[c, inner_at] * fields_a[c, inner_at]
        for run, (ref, total, inner) in enumerate([(fields_f, total_f, inner_f), (fields_a, total_a, inner_a)]):
            for c in range(3):
                total.append(ref[c, edge_at] + lasts[run][c][:CY])
                ref[c, edge_at] = total[c]
                add = d_inner[run][c]
                inner.append(ref[c, inner_at] if add is None else ref[c, inner_at] + inner_coef * add[:CY])
                ref[c, inner_at] = inner[c]
        e1 = [
            [base_first[run][c] if firsts[run][c] is None else base_first[run][c] + firsts[run][c][:CY] for c in range(3)]
            for run in range(2)
        ]
        edge_grad = DT * (dot_three(e1[0], e1[1]) + dot_three(total_f, total_a))
        inner_change = DT * (dot_three(inner_f, inner_a) - before)
        return edge_grad, inner_change

    def first_edge():
        firsts, lasts, d_inner, base = [], [], [], []
        for run in range(2):
            first, last, d_h2y, d_h2z = correct_prev(run, from_prev, to_prev, row_dt, has_prev)
            firsts.append(first)
            lasts.append(last)
            d_inner.append((None, d_h2z, -d_h2y))
            base.append((keep[4 * run], to_prev[4 * run + 2][:CY], to_prev[4 * run + 3][:CY]))
        edge, inner = finish(0, 0, 1, firsts, lasts, d_inner, DT * v_inv[0, 1], base)
        work[0] = edge
        work[1] = work[1] + inner

    def last_edge():
        firsts, lasts, d_inner, base = [], [], [], []
        for run in range(2):
            first, last, b_h2y, b_h2z = correct_next(run, from_next, to_next, row_dt, has_next)
            firsts.append(first)
            lasts.append(last)
            d_inner.append((minus_y(b_h2z) - minus_z(b_h2y), -b_h2z, b_h2y))
            base.append(tuple(keep[4 * run + 1 + c] for c in range(3)))
        edge, inner = finish(1, 1, 0, firsts, lasts, d_inner, DT * v_inv[1, 0], base)
        work[CX - 1] = edge
        work[CX - 2] = work[CX - 2] + inner

    devices = rows_out.shape[0]
    lanes = lanes_iota((devices, NZ))
    blocks = lax.broadcasted_iota(jnp.int32, (NZ // BZ, NZ), 0)
    spread = (blocks == lanes_iota((NZ // BZ, NZ)) // BZ).astype(jnp.bfloat16)
    owned = NZ // BZ // 2
    owner = jnp.where(mask[0] == 1, param[0] // owned, -1).astype(F32)
    slot = (param[0] & (owned - 1)).astype(F32)
    numbers = jnp.concatenate([owner, slot, jnp.zeros((14, NZ // BZ), F32)], axis=0)
    numbers = jnp.dot(numbers.astype(jnp.bfloat16), spread, preferred_element_type=F32)
    mine = numbers[0:1, :] == rows_iota((devices, NZ)).astype(F32)
    for part in range(BZ):
        chosen[pl.ds(part * devices, devices), :] = jnp.where(mine & (lanes % BZ == part), 1.0, 0.0).astype(jnp.bfloat16)
    found = jnp.sum(jnp.where(mine & (lanes % BZ == 0), numbers[1:2, :] + 1.0, 0.0), axis=1, keepdims=True) - 1.0
    rows_out[:, 0, BZ * CX * CY :] = jnp.broadcast_to(found, (devices, 128))

    def pack(q):
        values = work[pl.ds(4 * q, 4)].reshape(4 * CY, NZ)
        cells = exact_dot(chosen[...], values, (((1,), (1,)), ((), ())))
        for part in range(BZ):
            at = part * CX * CY + q * 4 * CY
            rows_out[:, 0, at : at + 4 * CY] = cells[part * devices : (part + 1) * devices]
            columns = pl.ds(at, 4 * CY)
            row_copies.append(
                pltpu.make_async_copy(rows_out.at[:, :, columns], far_rows.at[:, :, columns], rows_sem.at[4 * q + part])
            )
            row_copies[-1].start()

    columns = pl.ds(BZ * CX * CY, 128)
    row_copies = [pltpu.make_async_copy(rows_out.at[:, :, columns], far_rows.at[:, :, columns], rows_sem.at[16])]
    row_copies[0].start()
    for q in (1, 2):
        grads[q].wait()
        pack(q)
    for copy in [*messages[:3], *ends[0], grads[0]]:
        copy.wait()
    first_edge()
    for copy in stores[0]:
        copy.start()
    pack(0)
    for copy in [*messages[3:], *ends[1], grads[3]]:
        copy.wait()
    last_edge()
    for copy in stores[1]:
        copy.start()
    pack(3)
    for copy in [*stores[0], *stores[1], *row_copies]:
        copy.wait()


def correct_and_pack(mask, param, messages, inv, grad, fields_f, fields_a, devices):
    free, whole = pl.BlockSpec(memory_space=pl.ANY), pl.BlockSpec(memory_space=pltpu.VMEM)
    width = BZ * CX * CY + 128
    vmem = lambda shape: pltpu.VMEM(shape, F32)
    return pl.pallas_call(
        correct_kernel,
        in_specs=[whole] * 2 + [free] * 9,
        out_specs=[free] * 3,
        out_shape=[
            jax.ShapeDtypeStruct((3, CX, CY, NZ), F32),
            jax.ShapeDtypeStruct((3, CX, CY, NZ), F32),
            jax.ShapeDtypeStruct((devices, 1, width), F32),
        ],
        scratch_shapes=[vmem(m.shape) for m in messages]
        + [vmem((2, 2, CY, NZ)), vmem((CX, CY, NZ))]
        + [vmem((2, 3, 2, CY, NZ))] * 2
        + [pltpu.VMEM((BZ * devices, NZ), jnp.bfloat16), vmem((devices, 1, width))]
        + [pltpu.SemaphoreType.DMA(s) for s in ((5,), (2,), (4,), (2, 2), (2, 2), (17,))],
        input_output_aliases={9: 0, 10: 1},
        compiler_params=pltpu.CompilerParams(vmem_limit_bytes=VMEM_BYTES),
        cost_estimate=pl.CostEstimate(flops=6 * 10**9, bytes_accessed=0, transcendentals=0),
        name="correct_and_pack",
    )(mask, param, *messages, inv, grad, fields_f, fields_a)


def place_kernel(got, out):
    devices = got.shape[0]
    owned = out.shape[0]
    cells = BZ * CX * CY
    numbers = got[:, 0, cells:]
    wanted = (numbers == lanes_iota((devices, 128)).astype(F32)).astype(F32)
    placing = jnp.transpose(wanted)[:owned]
    order_from = rows_iota((4 * 128, 4 * 128))
    order_to = lanes_iota((4 * 128, 4 * 128))
    order = (order_from == (order_to % BZ) * 128 + order_to // BZ).astype(jnp.bfloat16)
    dims = (((1,), (0,)), ((), ()))
    for q in range(4):
        parts = [got[:, 0, part * CX * CY + q * 128 : part * CX * CY + (q + 1) * 128] for part in range(BZ)]
        rows = exact_dot(placing, jnp.concatenate(parts, axis=1), dims)
        high, low = split(rows)
        out[:, q * 512 : (q + 1) * 512] = lax.dot_general(
            high, order, dims, preferred_element_type=F32
        ) + lax.dot_general(low, order, dims, preferred_element_type=F32)


def place_rows(got, owned):
    return pl.pallas_call(
        place_kernel,
        out_shape=jax.ShapeDtypeStruct((owned, BZ * CX * CY), F32),
        compiler_params=pltpu.CompilerParams(vmem_limit_bytes=32 << 20),
        cost_estimate=pl.CostEstimate(flops=2 * 10**9, bytes_accessed=0, transcendentals=0),
        name="place_rows",
    )(got)


def body(e_forward, h_forward, e_adjoint, h_adjoint, inv_eps, source, adj_source, design_mask, param_map, step_index):
    arrays = (e_forward, h_forward, e_adjoint, h_adjoint, inv_eps, source, adj_source)
    devices = lax.axis_size("gx") * lax.axis_size("gy")
    blocks = NZ // BZ
    owned = blocks // 2
    up, down = pack_rows(step_index, arrays)
    above, below = cycled(up, "gy", 1), cycled(down, "gy", -1)
    to_prev, to_next, keep = solve_edges(step_index, arrays, above, below)
    from_next, from_prev = cycled(to_prev, "gx", -1), cycled(to_next, "gx", 1)
    fields_f, fields_a, grad = solve_main(step_index, arrays, above, below)
    messages = (from_prev, to_prev, keep, from_next, to_next)
    fields_f, fields_a, rows = correct_and_pack(
        design_mask, param_map, messages, inv_eps, grad, fields_f, fields_a, devices
    )
    got = lax.all_to_all(rows, ("gx", "gy"), split_axis=0, concat_axis=0, tiled=True)
    return place_rows(got, owned), fields_f, fields_a


def solution(mesh):
    field, cells = P(None, "gx", "gy", None), P("gx", "gy", None)
    in_specs = (field, field, field, field, cells, cells, cells, cells, cells, P())
    out_specs = (P(("gx", "gy"), None), field, field)
    return jax.shard_map(body, mesh=mesh, in_specs=in_specs, out_specs=out_specs, check_vma=False)
```

```python
import functools
import math

import jax
import jax.numpy as jnp
from jax import lax
from jax.experimental import pallas as pl
from jax.experimental.pallas import tpu as pltpu
from jax.sharding import PartitionSpec as P

BZ = 4
STEPS = 2
DT = 0.5
PERIOD = 20
RATE = 2.0 * math.pi / 20.0
CX, CY, NZ = 16, 32, 512
RING = 40
F32 = jnp.float32
VMEM_BYTES = (64 << 20) - (128 << 10)
TOUCH_BYTES, EDGE_BYTES, MAIN_BYTES, PACK_BYTES = 24 << 20, 24 << 20, 24 << 20, 32 << 20

UP, DOWN = 14, 10


def cycled(value, axis, by):
    devices = lax.axis_size(axis)
    return lax.ppermute(value, axis, [(i, (i + by) % devices) for i in range(devices)])


def rows_iota(shape):
    return lax.broadcasted_iota(jnp.int32, shape, 0)


def lanes_iota(shape):
    return lax.broadcasted_iota(jnp.int32, shape, 1)


def plus_y(f):
    return pltpu.roll(f, f.shape[0] - 1, 0) - f


def minus_y(f):
    return f - pltpu.roll(f, 1, 0)


def plus_z(f):
    return jnp.where(lanes_iota(f.shape) == NZ - 1, 0.0, pltpu.roll(f, NZ - 1, 1)) - f


def minus_z(f):
    return f - jnp.where(lanes_iota(f.shape) == 0, 0.0, pltpu.roll(f, 1, 1))


def magnetic(e, e_next, h, row_dt):
    ahead_y = -e[1] if e_next is None else e_next[1] - e[1]
    ahead_z = -e[2] if e_next is None else e_next[2] - e[2]
    return (
        h[0] - row_dt * (plus_y(e[2]) - plus_z(e[1])),
        h[1] - row_dt * (plus_z(e[0]) - ahead_z),
        h[2] - row_dt * (ahead_y - plus_y(e[0])),
    )


def electric(e, h, h_prev, coef, drive):
    back_y = h[1] if h_prev is None else h[1] - h_prev[1]
    back_z = h[2] if h_prev is None else h[2] - h_prev[2]
    return (
        e[0] + coef * (minus_y(h[2]) - minus_z(h[1])),
        e[1] + coef * (minus_z(h[0]) - back_z),
        e[2] + coef * (back_y - minus_y(h[0]) - drive),
    )


def amplitude(step_index, ticks, rows):
    tick = lax.rem(step_index[0] + (PERIOD + ticks), PERIOD)
    tile = jnp.sin(RATE * jnp.full((8, 128), tick, jnp.int32).astype(F32))
    return jnp.concatenate([jnp.concatenate([tile] * (NZ // 128), axis=1)] * (rows // 8), axis=0)


def dot_three(a, b):
    return a[0] * b[0] + a[1] * b[1] + a[2] * b[2]


def plus_x(f):
    return jnp.where(rows_iota(f.shape) == f.shape[0] - 1, 0.0, pltpu.roll(f, f.shape[0] - 1, 0)) - f


def minus_x(f):
    return f - jnp.where(rows_iota(f.shape) == 0, 0.0, pltpu.roll(f, 1, 0))


def has_rows():
    place = lax.axis_index("gy")
    return place < lax.axis_size("gy") - 1, place > 0


def row_steps():
    _, has_above = has_rows()
    rows = rows_iota((8, NZ))
    tile = jnp.where((rows >= 6) & jnp.logical_not(has_above), 0.0, DT)
    return jnp.concatenate([jnp.full((CY, NZ), DT, F32), tile], axis=0)


def ring_steps():
    _, has_above = has_rows()
    tile = jnp.where((rows_iota((8, NZ)) == 7) & has_above, DT, 0.0)
    return jnp.concatenate([jnp.full((CY, NZ), DT, F32), tile], axis=0)


class Ghosts:
    def __init__(self, above, below, x):
        has_below, has_above = has_rows()
        self.refs = above, below
        self.flags = jnp.where(has_above, 1.0, 0.0).astype(F32), jnp.where(has_below, 1.0, 0.0).astype(F32)
        self.x = x

    def up(self, k, x=None):
        return self.refs[0][k, pl.ds(self.x if x is None else x, 1), :] * self.flags[0]

    def down(self, k, x=None):
        return self.refs[1][k, pl.ds(self.x if x is None else x, 1), :] * self.flags[1]

    def tile(self, rows):
        at = rows_iota((8, NZ))
        tile = jnp.zeros((8, NZ), F32)
        for row, value in rows.items():
            tile = jnp.where(at == row, value, tile)
        return tile

    def e_before(self, run):
        return (
            self.tile({0: self.down(4 * run)}),
            jnp.zeros((8, NZ), F32),
            self.tile({0: self.down(4 * run + 1)}),
        )

    def e_middle(self, run):
        return (
            self.tile({0: self.down(4 * run + 2), 7: self.up(6 * run)}),
            self.tile({7: self.up(6 * run + 1)}),
            self.tile({0: self.down(4 * run + 3), 7: self.up(6 * run + 2)}),
        )

    def h_before(self, run):
        return tuple(self.tile({7: self.up(6 * run + 3 + c)}) for c in range(3))

    def coef(self):
        return DT * self.tile({0: self.down(8), 7: self.up(12)})


def ring(own, tile):
    return jnp.concatenate([own, tile], axis=0)


def rings(own, tiles):
    return tuple(ring(own[c], tiles[c]) for c in range(3))


def rows_up(amp, e_refs, h_refs, inv, drives, out):
    coef = DT * inv[:, 7, :]
    singles = []
    for run in range(2):
        e, e_in = ([e_refs[run][c, :, r, :] for c in range(3)] for r in (7, 6))
        h, h_in = ([h_refs[run][c, :, r, :] for c in range(3)] for r in (7, 6))
        hx_in = h_in[0] - DT * ((e[2] - e_in[2]) - plus_z(e_in[1]))
        hz_in = h_in[2] - DT * (plus_x(e_in[1]) - (e[0] - e_in[0]))
        out[6 * run] = e[0] - coef * hz_in
        out[6 * run + 1] = e[1]
        out[6 * run + 2] = e[2] + coef * (hx_in - amp[run] * drives[run][:, 7, :])
        out[6 * run + 3] = h[0] + DT * (e[2] + plus_z(e[1]))
        out[6 * run + 4] = h[1] - DT * (plus_z(e[0]) - plus_x(e[2]))
        out[6 * run + 5] = h[2] - DT * (plus_x(e[1]) + e[0])
        singles += [e[2], e_in[1]]
    out[12] = inv[:, 7, :]
    rows = rows_iota((CX, NZ))
    held = singles[0]
    for k in range(1, 4):
        held = jnp.where(rows == k, pltpu.roll(singles[k], k, 0), held)
    out[13] = held


def rows_down(amp, e_refs, h_refs, inv, drives, out):
    coef = DT * inv[:, 0, :]
    singles, others = [], []
    for run in range(2):
        e, e_in = ([e_refs[run][c, :, r, :] for c in range(3)] for r in (0, 1))
        h = [h_refs[run][c, :, 0, :] for c in range(3)]
        hx = h[0] - DT * ((e_in[2] - e[2]) - plus_z(e[1]))
        hy = h[1] - DT * (plus_z(e[0]) - plus_x(e[2]))
        hz = h[2] - DT * (plus_x(e[1]) - (e_in[0] - e[0]))
        out[4 * run] = e[0]
        out[4 * run + 1] = e[2]
        out[4 * run + 2] = e[0] + coef * (hz - minus_z(hy))
        out[4 * run + 3] = e[2] + coef * (minus_x(hy) - hx - amp[run] * drives[run][:, 0, :])
        singles.append(e[1])
        others.append(hy)
    out[8] = inv[:, 0, :]
    rows = rows_iota((CX, NZ))
    held = singles[0]
    for k, (value, by) in enumerate([(singles[1], 1), (others[0], 3), (others[1], 4)], 1):
        held = jnp.where(rows == k, pltpu.roll(value, by, 0), held)
    out[9] = held


def pack_kernel(step_index, e_f, h_f, e_a, h_a, inv, src, adj, far_up, far_down, *scratch):
    sources = (e_f, h_f, e_a, h_a, inv, src, adj)
    places, (up, down, sems, out_sems) = scratch[:7], scratch[7:]
    stores = [pltpu.make_async_copy(up, far_up, out_sems.at[0]), pltpu.make_async_copy(down, far_down, out_sems.at[1])]

    def load(a, side):
        at = pl.ds(24 if side == 0 else 0, 8)
        source = sources[a].at[:, :, at] if a < 4 else sources[a].at[:, at]
        return pltpu.make_async_copy(source, places[a].at[side], sems.at[a, side])

    for side in range(2):
        for a in range(7):
            load(a, side).start()
    amp = [amplitude(step_index, ticks, CX) for ticks in (1, -1)]
    for side, (rows_of, out) in enumerate([(rows_up, up), (rows_down, down)]):
        for a in range(7):
            load(a, side).wait()
        ef, hf, ea, ha, coef, drive_f, drive_a = (place.at[side] for place in places)
        rows_of(amp, (ef, ea), (hf, ha), coef, (drive_f, drive_a), out)
        stores[side].start()
    for copy in stores:
        copy.wait()


def pack_rows(step_index, arrays):
    hbm = pl.BlockSpec(memory_space=pl.ANY)
    shapes = [(UP, CX, NZ), (DOWN, CX, NZ)]
    return pl.pallas_call(
        pack_kernel,
        in_specs=[pl.BlockSpec(memory_space=pltpu.SMEM)] + [hbm] * 7,
        out_specs=[hbm] * 2,
        out_shape=[jax.ShapeDtypeStruct(s, F32) for s in shapes],
        scratch_shapes=[pltpu.VMEM((2, 3, CX, 8, NZ), F32)] * 4
        + [pltpu.VMEM((2, CX, 8, NZ), F32)] * 3
        + [pltpu.VMEM(s, F32) for s in shapes]
        + [pltpu.SemaphoreType.DMA((7, 2)), pltpu.SemaphoreType.DMA((2,))],
        compiler_params=pltpu.CompilerParams(vmem_limit_bytes=VMEM_BYTES),
        cost_estimate=pl.CostEstimate(flops=4 * 10**9, bytes_accessed=0, transcendentals=0),
        name="pack_rows",
    )(step_index, *arrays)


def touch_kernel(*refs):
    refs[-1][...] = refs[4][0, :8, :128]


def touch(arrays):
    whole = pl.BlockSpec(memory_space=pltpu.VMEM)
    return pl.pallas_call(
        touch_kernel,
        in_specs=[whole] * 7,
        out_specs=whole,
        out_shape=jax.ShapeDtypeStruct((8, 128), F32),
        compiler_params=pltpu.CompilerParams(vmem_limit_bytes=TOUCH_BYTES),
        cost_estimate=pl.CostEstimate(flops=6 * 10**9, bytes_accessed=0, transcendentals=0),
        name="touch",
    )(*arrays)


def call_edges(kernel, name, step_index, arrays, messages, shapes):
    whole = pl.BlockSpec(memory_space=pltpu.VMEM)

    def body(step_index, *refs):
        sides = []
        for side in range(2):
            at = pl.ds(side * (CX - 2), 2)
            sides += [refs[a].at[:, at] if a < 4 else refs[a].at[at] for a in range(7)]
        kernel(step_index, *sides, *refs[7:9], *refs[10:])

    return pl.pallas_call(
        body,
        in_specs=[pl.BlockSpec(memory_space=pltpu.SMEM)] + [whole] * (7 + len(messages)),
        out_specs=[whole] * len(shapes),
        out_shape=[jax.ShapeDtypeStruct(s, F32) for s in shapes],
        compiler_params=pltpu.CompilerParams(vmem_limit_bytes=EDGE_BYTES),
        cost_estimate=pl.CostEstimate(flops=3 * 10**9, bytes_accessed=0, transcendentals=0),
        name=name,
    )(step_index, *arrays, *messages)


def edge_kernel(step_index, e_f0, h_f0, e_a0, h_a0, inv0, src0, adj0, e_f1, h_f1, e_a1, h_a1, inv1, src1, adj1, above, below, to_prev, to_next, keep):
    row_dt = ring_steps()
    ghosts = {x: Ghosts(above, below, x) for x in (0, 1, CX - 2, CX - 1)}
    still = jnp.zeros((8, NZ), F32)
    amp = [amplitude(step_index, ticks, CY) for ticks in (1, -1)]

    def before(ref, at, run, x):
        return rings([ref[c, at] for c in range(3)], ghosts[x].e_before(run))

    def middle(ref, at, run, x):
        return rings([ref[c, at] for c in range(3)], ghosts[x].e_middle(run))

    def magnet(ref, at, run, x):
        return rings([ref[c, at] for c in range(3)], ghosts[x].h_before(run))

    coef_first = ring(DT * inv0[0], ghosts[0].coef())
    coef_last = ring(DT * inv1[1], ghosts[CX - 1].coef())
    to_prev[8] = coef_first
    to_next[8] = coef_last
    for run, (e0, h0, s0, e1, h1, s1) in enumerate(
        [(e_f0, h_f0, src0, e_f1, h_f1, src1), (e_a0, h_a0, adj0, e_a1, h_a1, adj1)]
    ):
        near = ghosts[0]
        h = magnetic(before(e0, 0, run, 0), before(e0, 1, run, 1), magnet(h0, 0, run, 0), row_dt)
        drive = ring(amp[run] * s0[0], still)
        new = electric(middle(e0, 0, run, 0), h, None, coef_first, drive)
        sides_y = {0: near.down(9, run), 6: near.up(13, 2 * run + 1), 7: near.up(6 * run + 1)}
        sides_z = {0: near.down(4 * run + 1), 7: near.up(13, 2 * run)}
        to_prev[4 * run] = ring(e0[1, 0], near.tile(sides_y))
        to_prev[4 * run + 1] = ring(e0[2, 0], near.tile(sides_z))
        to_prev[4 * run + 2] = new[1]
        to_prev[4 * run + 3] = new[2]
        keep[4 * run] = new[0][:CY]
        e, back = before(e1, 1, run, CX - 1), before(e1, 0, run, CX - 2)
        h = magnetic(e, None, magnet(h1, 1, run, CX - 1), row_dt)
        h_back = magnetic(back, e, magnet(h1, 0, run, CX - 2), row_dt)
        drive = ring(amp[run] * s1[1], still)
        new = electric(middle(e1, 1, run, CX - 1), h, h_back, coef_last, drive)
        later = magnetic(new, None, h, row_dt)
        beyond = ghosts[CX - 1].down(9, 2 + run)
        to_next[4 * run] = jnp.where(rows_iota((RING, NZ)) == CY, beyond, h[1])
        to_next[4 * run + 1] = h[2]
        to_next[4 * run + 2] = later[1]
        to_next[4 * run + 3] = later[2]
        for c in range(3):
            keep[4 * run + 1 + c] = new[c][:CY]


def solve_edges(step_index, arrays, above, below, touched):
    shapes = [(9, RING, NZ), (9, RING, NZ), (8, CY, NZ)]
    return call_edges(edge_kernel, "solve_edges", step_index, arrays, [above, below, touched], shapes)


CHUNK = 2
DRAIN = 4


def zplus(tile):
    moved = pltpu.roll(tile, NZ - 1, 1)
    last = jnp.where(lanes_iota((8, 128)) == 127, 0.0, moved[:, NZ - 128 :])
    return jnp.concatenate([moved[:, : NZ - 128], last], axis=1) - tile


def zminus(tile):
    moved = pltpu.roll(tile, 1, 1)
    first = jnp.where(lanes_iota((8, 128)) == 0, 0.0, moved[:, :128])
    return tile - jnp.concatenate([first, moved[:, 128:]], axis=1)


def magnetic_tiles(tiles, e, e_next, h, row_dts, put, closed):
    end = rows_iota((8, NZ)) == 7
    firsts = {c: pltpu.roll(e(c, 0), 7, 0) for c in (0, 2)}
    here = firsts
    for t in range(tiles):
        if t == tiles - 1:
            after = {c: jnp.zeros((8, NZ), F32) for c in (0, 2)} if closed else firsts
        else:
            after = {c: pltpu.roll(e(c, t + 1), 7, 0) for c in (0, 2)}
        ex, ey, ez = (e(c, t) for c in range(3))
        put(0, t, h(0, t) - row_dts[t] * ((jnp.where(end, after[2], here[2]) - ez) - zplus(ey)))
        put(1, t, h(1, t) - row_dts[t] * (zplus(ex) - (e_next(2, t) - ez)))
        put(2, t, h(2, t) - row_dts[t] * ((e_next(1, t) - ey) - (jnp.where(end, after[0], here[0]) - ex)))
        here = after


def electric_tile(e, h, h_prev, coef, drive, t, rolled):
    start = rows_iota((8, NZ)) == 0
    hx, hy, hz = (h(c, t) for c in range(3))
    moved = {0: pltpu.roll(hx, 1, 0), 2: pltpu.roll(hz, 1, 0)}
    new_x = e(0, t) + coef * ((hz - jnp.where(start, rolled[2], moved[2])) - zminus(hy))
    new_y = e(1, t) + coef * (zminus(hx) - (hz - h_prev(2, t)))
    curl = (hy - h_prev(1, t)) - (hx - jnp.where(start, rolled[0], moved[0]))
    new_z = e(2, t) + coef * (curl if drive is None else curl - drive)
    return (new_x, new_y, new_z), moved


def sweep(step_index, places, store, mid_h, mid_e, late_h, tiles, at_rows, ghosts, put_last):
    v_ef, v_hf, v_ea, v_ha, v_inv, v_src, v_adj = places
    own = [t for t in range(tiles) if at_rows[t] is not None]
    closed = len(own) == tiles
    mid_h[...] = jnp.zeros_like(mid_h)
    late_h[...] = jnp.zeros_like(late_h)
    ghost_dt = None if closed else ring_steps()[CY:]
    row_dts = [DT if t in own else ghost_dt for t in range(tiles)]
    amp = [[amplitude(step_index, ticks, 8) for ticks in pair] for pair in ((1, 2), (-1, -2))]
    runs = ((v_ef, v_hf, v_src), (v_ea, v_ha, v_adj))
    nothing = {c: jnp.zeros((8, NZ), F32) for c in (0, 2)}

    def rows(t):
        return pl.ds(at_rows[t], 8)

    def ring_rows(t):
        return pl.ds(8 * t, 8)

    def one(step, carry):
        now, then = lax.rem(step, 2), lax.rem(step + 1, 2)

        @pl.when(step <= CX)
        def _():
            x = step - 1
            inside, x_next = step < CX, jnp.minimum(step, CX - 1)
            if not closed:
                here, there = ghosts(x), ghosts(jnp.minimum(step, CX - 1))
                coef_ghost = here.coef()
            for run, (e_ref, h_ref, s_ref) in enumerate(runs):
                beside = beside_next = beside_h = middle = None
                if not closed:
                    beside = here.e_before(run)
                    beside_next = [jnp.where(inside, v, 0.0) for v in there.e_before(run)]
                    beside_h = here.h_before(run)
                    middle = here.e_middle(run)

                def put_h(c, t, value):
                    mid_h[now, 3 * run + c, ring_rows(t), :] = value

                magnetic_tiles(
                    tiles,
                    lambda c, t: e_ref[c, x, rows(t), :] if t in own else beside[c],
                    lambda c, t: jnp.where(inside, e_ref[c, x_next, rows(t), :], 0.0) if t in own else beside_next[c],
                    lambda c, t: h_ref[c, x, rows(t), :] if t in own else beside_h[c],
                    row_dts,
                    put_h,
                    closed,
                )
                rolled = nothing
                if not closed:
                    end = ring_rows(tiles - 1)
                    rolled = {c: pltpu.roll(mid_h[now, 3 * run + c, end, :], 1, 0) for c in (0, 2)}
                for t in range(tiles):
                    if t in own:
                        coef, drive = DT * v_inv[x, rows(t), :], amp[run][0] * s_ref[x, rows(t), :]
                    else:
                        coef, drive = coef_ghost, None
                    new, rolled = electric_tile(
                        lambda c, t: e_ref[c, x, rows(t), :] if t in own else middle[c],
                        lambda c, t: mid_h[now, 3 * run + c, ring_rows(t), :],
                        lambda c, t: mid_h[then, 3 * run + c, ring_rows(t), :],
                        coef,
                        drive,
                        t,
                        rolled,
                    )
                    for c in range(3):
                        mid_e[now, 3 * run + c, ring_rows(t), :] = new[c]

        @pl.when(step > CX)
        def _():
            mid_e[now] = jnp.zeros((6, 8 * tiles, NZ), F32)

        @pl.when(step > 1)
        def _():
            x = step - 2
            rolled = [nothing, nothing]
            for run in range(2):

                def put_late(c, t, value):
                    late_h[now, 3 * run + c, ring_rows(t), :] = value

                magnetic_tiles(
                    tiles,
                    lambda c, t: mid_e[then, 3 * run + c, ring_rows(t), :],
                    lambda c, t: mid_e[now, 3 * run + c, ring_rows(t), :],
                    lambda c, t: mid_h[then, 3 * run + c, ring_rows(t), :],
                    row_dts,
                    put_late,
                    closed,
                )
            for t in range(tiles):
                if t not in own:
                    rolled = [
                        {c: pltpu.roll(late_h[now, 3 * run + c, ring_rows(t), :], 1, 0) for c in (0, 2)}
                        for run in range(2)
                    ]
                    continue
                coef = DT * v_inv[x, rows(t), :]
                new = [None, None]
                for run, (e_ref, _, s_ref) in enumerate(runs):
                    new[run], rolled[run] = electric_tile(
                        lambda c, t: mid_e[then, 3 * run + c, ring_rows(t), :],
                        lambda c, t: late_h[now, 3 * run + c, ring_rows(t), :],
                        lambda c, t: late_h[then, 3 * run + c, ring_rows(t), :],
                        coef,
                        amp[run][1] * s_ref[x, rows(t), :],
                        t,
                        rolled[run],
                    )
                first = [[mid_e[then, 3 * run + c, ring_rows(t), :] for c in range(3)] for run in range(2)]
                put_last(x, t, new, DT * (dot_three(*first) + dot_three(*new)))

        @pl.when((step > 2) & (step % DRAIN == 1))
        def _():
            for a in range(2):
                store(a, step // DRAIN - 1).start()

        return carry

    lax.fori_loop(1, CX + 2, one, 0)
    for part in range(CX // DRAIN):
        for a in range(2):
            store(a, part).wait()


def main_kernel(
    step_index, e_f, h_f, e_a, h_a, inv, src, adj, above, below, out_f, out_a, grad,
    last_f, last_a, mid_h, mid_e, late_h, store_sem,
):
    def store(a, part):
        at = pl.ds(part * DRAIN, DRAIN)
        return pltpu.make_async_copy((last_f, last_a)[a].at[:, at], (out_f, out_a)[a].at[:, at], store_sem.at[a, part])

    def put_last(x, t, new, product):
        for c in range(3):
            last_f[c, x, pl.ds(8 * t - 8, 8), :] = new[0][c]
            last_a[c, x, pl.ds(8 * t - 8, 8), :] = new[1][c]
        grad[x, pl.ds(8 * t - 8, 8), :] = product

    sweep(
        step_index, (e_f, h_f, e_a, h_a, inv, src, adj), store, mid_h, mid_e, late_h, 5, [None, 0, 8, 16, 24],
        lambda x: Ghosts(above, below, x), put_last,
    )


def solve_main(step_index, arrays, above, below):
    free, whole = pl.BlockSpec(memory_space=pl.ANY), pl.BlockSpec(memory_space=pltpu.VMEM)
    field, cells = (3, CX, CY, NZ), (CX, CY, NZ)
    return pl.pallas_call(
        main_kernel,
        in_specs=[pl.BlockSpec(memory_space=pltpu.SMEM)] + [whole] * 9,
        out_specs=[free, free, whole],
        out_shape=[jax.ShapeDtypeStruct(s, F32) for s in (field, field, cells)],
        scratch_shapes=[pltpu.VMEM(field, F32)] * 2
        + [pltpu.VMEM((2, 6, RING, NZ), F32)] * 3
        + [pltpu.SemaphoreType.DMA((2, CX // DRAIN))],
        compiler_params=pltpu.CompilerParams(vmem_limit_bytes=MAIN_BYTES),
        cost_estimate=pl.CostEstimate(flops=14 * 10**9, bytes_accessed=0, transcendentals=0),
        name="solve_main",
    )(step_index, *arrays, above, below)


def split(value):
    high = value.astype(jnp.bfloat16)
    return high, (value - high.astype(F32)).astype(jnp.bfloat16)


def exact_dot(a, b, dims):
    high, low = split(b)
    a = a.astype(jnp.bfloat16)
    return lax.dot_general(a, high, dims, preferred_element_type=F32) + lax.dot_general(
        a, low, dims, preferred_element_type=F32
    )


def correct_prev(run, from_prev, own, row_dt, present):
    e0y, e0z, e1y, e1z = (own[4 * run + k] for k in range(4))
    coef, ghost_coef = own[8], jnp.where(present, from_prev[8], 0.0)
    h1y, h1z, h2y, h2z = (from_prev[4 * run + k] for k in range(4))
    d_h1y, d_h1z = DT * e0z, -DT * e0y
    h1y = jnp.where(present, h1y + d_h1y, 0.0)
    h1z = jnp.where(present, h1z + d_h1z, 0.0)
    d_e1y, d_e1z = coef * h1z, -coef * h1y
    g_e1x = ghost_coef * (minus_y(d_h1z) - minus_z(d_h1y))
    g_e1y, g_e1z = -ghost_coef * d_h1z, ghost_coef * d_h1y
    h2y = jnp.where(present, h2y + d_h1y - DT * (plus_z(g_e1x) - (e1z + d_e1z - g_e1z)), 0.0)
    h2z = jnp.where(present, h2z + d_h1z - DT * ((e1y + d_e1y - g_e1y) - plus_y(g_e1x)), 0.0)
    d_h2x = -row_dt * (plus_y(d_e1z) - plus_z(d_e1y))
    d_h2y, d_h2z = -row_dt * d_e1z, row_dt * d_e1y
    first = (None, d_e1y, d_e1z)
    last = (
        coef * (minus_y(d_h2z) - minus_z(d_h2y)),
        d_e1y + coef * (minus_z(d_h2x) - d_h2z + h2z),
        d_e1z + coef * (d_h2y - h2y - minus_y(d_h2x)),
    )
    return first, last, d_h2y, d_h2z


def correct_next(run, from_next, own, row_dt, present):
    e0y, e0z, e1y, e1z = (jnp.where(present, from_next[4 * run + k], 0.0) for k in range(4))
    coef, ghost_coef = own[8], jnp.where(present, from_next[8], 0.0)
    h1y, h1z = own[4 * run], own[4 * run + 1]
    d_h1y, d_h1z = DT * e0z, -DT * e0y
    d_e1x = coef * (minus_y(d_h1z) - minus_z(d_h1y))
    d_e1y, d_e1z = -coef * d_h1z, coef * d_h1y
    e1y = e1y + ghost_coef * (h1z + d_h1z)
    e1z = e1z - ghost_coef * (h1y + d_h1y)
    d_h2x = -row_dt * (plus_y(d_e1z) - plus_z(d_e1y))
    d_h2y = d_h1y - row_dt * (plus_z(d_e1x) - (e1z - d_e1z))
    d_h2z = d_h1z - row_dt * ((e1y - d_e1y) - plus_y(d_e1x))
    b_h2y, b_h2z = row_dt * d_e1z, -row_dt * d_e1y
    first = (d_e1x, d_e1y, d_e1z)
    last = (
        d_e1x + coef * (minus_y(d_h2z) - minus_z(d_h2y)),
        d_e1y + coef * (minus_z(d_h2x) - d_h2z + b_h2z),
        d_e1z + coef * (d_h2y - b_h2y - minus_y(d_h2x)),
    )
    return first, last, b_h2y, b_h2z


def correct_kernel(
    mask, param, *refs
):
    far, refs = refs[:5], refs[5:]
    far_inv, far_grad, old_f, old_a, out_f, out_a, rows_out, *refs = refs
    near, refs = refs[:5], refs[5:]
    (
    v_inv, work, v_f, v_a, chosen,
    message_sem, inv_sem, grad_sem, field_sem, store_sem,
    ) = refs
    from_prev, to_prev, keep, from_next, to_next = near
    place = lax.axis_index("gx")
    has_prev, has_next = place > 0, place < lax.axis_size("gx") - 1
    row_dt = row_steps()
    messages = [pltpu.make_async_copy(a, b, message_sem.at[k]) for k, (a, b) in enumerate(zip(far, near))]
    grads = [
        pltpu.make_async_copy(far_grad.at[pl.ds(4 * q, 4)], work.at[pl.ds(4 * q, 4)], grad_sem.at[q]) for q in range(4)
    ]
    ends, stores = [], []
    for side in range(2):
        at = pl.ds(side * (CX - 2), 2)
        ends.append(
            [
                pltpu.make_async_copy(far_inv.at[at], v_inv.at[side], inv_sem.at[side]),
                pltpu.make_async_copy(old_f.at[:, at], v_f.at[side], field_sem.at[0, side]),
                pltpu.make_async_copy(old_a.at[:, at], v_a.at[side], field_sem.at[1, side]),
            ]
        )
        stores.append(
            [
                pltpu.make_async_copy(v_f.at[side], out_f.at[:, at], store_sem.at[0, side]),
                pltpu.make_async_copy(v_a.at[side], out_a.at[:, at], store_sem.at[1, side]),
            ]
        )
    for copy in [grads[1], grads[2], *messages[:3], *ends[0], grads[0], *messages[3:], *ends[1], grads[3]]:
        copy.start()

    def finish(side, edge_at, inner_at, firsts, lasts, d_inner, inner_coef, base_first):
        total_f, total_a, inner_f, inner_a = [], [], [], []
        fields_f, fields_a = v_f.at[side], v_a.at[side]
        before = jnp.zeros((CY, NZ), F32)
        for c in range(3):
            before = before + fields_f[c, inner_at] * fields_a[c, inner_at]
        for run, (ref, total, inner) in enumerate([(fields_f, total_f, inner_f), (fields_a, total_a, inner_a)]):
            for c in range(3):
                total.append(ref[c, edge_at] + lasts[run][c][:CY])
                ref[c, edge_at] = total[c]
                add = d_inner[run][c]
                inner.append(ref[c, inner_at] if add is None else ref[c, inner_at] + inner_coef * add[:CY])
                ref[c, inner_at] = inner[c]
        e1 = [
            [base_first[run][c] if firsts[run][c] is None else base_first[run][c] + firsts[run][c][:CY] for c in range(3)]
            for run in range(2)
        ]
        edge_grad = DT * (dot_three(e1[0], e1[1]) + dot_three(total_f, total_a))
        inner_change = DT * (dot_three(inner_f, inner_a) - before)
        return edge_grad, inner_change

    def first_edge():
        firsts, lasts, d_inner, base = [], [], [], []
        for run in range(2):
            first, last, d_h2y, d_h2z = correct_prev(run, from_prev, to_prev, row_dt, has_prev)
            firsts.append(first)
            lasts.append(last)
            d_inner.append((None, d_h2z, -d_h2y))
            base.append((keep[4 * run], to_prev[4 * run + 2][:CY], to_prev[4 * run + 3][:CY]))
        edge, inner = finish(0, 0, 1, firsts, lasts, d_inner, DT * v_inv[0, 1], base)
        work[0] = edge
        work[1] = work[1] + inner

    def last_edge():
        firsts, lasts, d_inner, base = [], [], [], []
        for run in range(2):
            first, last, b_h2y, b_h2z = correct_next(run, from_next, to_next, row_dt, has_next)
            firsts.append(first)
            lasts.append(last)
            d_inner.append((minus_y(b_h2z) - minus_z(b_h2y), -b_h2z, b_h2y))
            base.append(tuple(keep[4 * run + 1 + c] for c in range(3)))
        edge, inner = finish(1, 1, 0, firsts, lasts, d_inner, DT * v_inv[1, 0], base)
        work[CX - 1] = edge
        work[CX - 2] = work[CX - 2] + inner

    devices = rows_out.shape[0]
    lanes = lanes_iota((devices, NZ))
    blocks = lax.broadcasted_iota(jnp.int32, (NZ // BZ, NZ), 0)
    spread = (blocks == lanes_iota((NZ // BZ, NZ)) // BZ).astype(jnp.bfloat16)
    owned = NZ // BZ // 2
    owner = jnp.where(mask[0] == 1, param[0] // owned, -1).astype(F32)
    slot = (param[0] & (owned - 1)).astype(F32)
    numbers = jnp.concatenate([owner, slot, jnp.zeros((14, NZ // BZ), F32)], axis=0)
    numbers = jnp.dot(numbers.astype(jnp.bfloat16), spread, preferred_element_type=F32)
    mine = numbers[0:1, :] == rows_iota((devices, NZ)).astype(F32)
    for part in range(BZ):
        chosen[pl.ds(part * devices, devices), :] = jnp.where(mine & (lanes % BZ == part), 1.0, 0.0).astype(jnp.bfloat16)
    found = jnp.sum(jnp.where(mine & (lanes % BZ == 0), numbers[1:2, :] + 1.0, 0.0), axis=1, keepdims=True) - 1.0
    rows_out[:, 0, BZ * CX * CY :] = jnp.broadcast_to(found, (devices, 128))

    def pack(q):
        values = work[pl.ds(4 * q, 4)].reshape(4 * CY, NZ)
        cells = exact_dot(chosen[...], values, (((1,), (1,)), ((), ())))
        for part in range(BZ):
            at = part * CX * CY + q * 4 * CY
            rows_out[:, 0, at : at + 4 * CY] = cells[part * devices : (part + 1) * devices]

    for q in (1, 2):
        grads[q].wait()
        pack(q)
    for copy in [*messages[:3], *ends[0], grads[0]]:
        copy.wait()
    first_edge()
    for copy in stores[0]:
        copy.start()
    pack(0)
    for copy in [*messages[3:], *ends[1], grads[3]]:
        copy.wait()
    last_edge()
    for copy in stores[1]:
        copy.start()
    pack(3)
    for copy in [*stores[0], *stores[1]]:
        copy.wait()


def correct_and_pack(mask, param, messages, inv, grad, fields_f, fields_a, devices):
    free, whole = pl.BlockSpec(memory_space=pl.ANY), pl.BlockSpec(memory_space=pltpu.VMEM)
    width = BZ * CX * CY + 128
    vmem = lambda shape: pltpu.VMEM(shape, F32)
    return pl.pallas_call(
        correct_kernel,
        in_specs=[whole] * 2 + [free] * 9,
        out_specs=[free, free, whole],
        out_shape=[
            jax.ShapeDtypeStruct((3, CX, CY, NZ), F32),
            jax.ShapeDtypeStruct((3, CX, CY, NZ), F32),
            jax.ShapeDtypeStruct((devices, 1, width), F32),
        ],
        scratch_shapes=[vmem(m.shape) for m in messages]
        + [vmem((2, 2, CY, NZ)), vmem((CX, CY, NZ))]
        + [vmem((2, 3, 2, CY, NZ))] * 2
        + [pltpu.VMEM((BZ * devices, NZ), jnp.bfloat16)]
        + [pltpu.SemaphoreType.DMA(s) for s in ((5,), (2,), (4,), (2, 2), (2, 2))],
        input_output_aliases={9: 0, 10: 1},
        compiler_params=pltpu.CompilerParams(vmem_limit_bytes=PACK_BYTES),
        cost_estimate=pl.CostEstimate(flops=6 * 10**9, bytes_accessed=0, transcendentals=0),
        name="correct_and_pack",
    )(mask, param, *messages, inv, grad, fields_f, fields_a)


def place_kernel(got, out):
    devices = got.shape[0]
    owned = out.shape[0]
    cells = BZ * CX * CY
    numbers = got[:, 0, cells:]
    wanted = (numbers == lanes_iota((devices, 128)).astype(F32)).astype(F32)
    placing = jnp.transpose(wanted)[:owned]
    order_from = rows_iota((4 * 128, 4 * 128))
    order_to = lanes_iota((4 * 128, 4 * 128))
    order = (order_from == (order_to % BZ) * 128 + order_to // BZ).astype(jnp.bfloat16)
    dims = (((1,), (0,)), ((), ()))
    for q in range(4):
        parts = [got[:, 0, part * CX * CY + q * 128 : part * CX * CY + (q + 1) * 128] for part in range(BZ)]
        rows = exact_dot(placing, jnp.concatenate(parts, axis=1), dims)
        high, low = split(rows)
        out[:, q * 512 : (q + 1) * 512] = lax.dot_general(
            high, order, dims, preferred_element_type=F32
        ) + lax.dot_general(low, order, dims, preferred_element_type=F32)


def place_rows(got, owned):
    return pl.pallas_call(
        place_kernel,
        out_shape=jax.ShapeDtypeStruct((owned, BZ * CX * CY), F32),
        compiler_params=pltpu.CompilerParams(vmem_limit_bytes=32 << 20),
        cost_estimate=pl.CostEstimate(flops=2 * 10**9, bytes_accessed=0, transcendentals=0),
        name="place_rows",
    )(got)


def body(e_forward, h_forward, e_adjoint, h_adjoint, inv_eps, source, adj_source, design_mask, param_map, step_index):
    arrays = (e_forward, h_forward, e_adjoint, h_adjoint, inv_eps, source, adj_source)
    devices = lax.axis_size("gx") * lax.axis_size("gy")
    blocks = NZ // BZ
    owned = blocks // 2
    up, down = pack_rows(step_index, arrays)
    above, below = cycled(up, "gy", 1), cycled(down, "gy", -1)
    touched = touch(arrays)
    to_prev, to_next, keep = solve_edges(step_index, arrays, above, below, touched)
    from_next, from_prev = cycled(to_prev, "gx", -1), cycled(to_next, "gx", 1)
    fields_f, fields_a, grad = solve_main(step_index, arrays, above, below)
    messages = (from_prev, to_prev, keep, from_next, to_next)
    fields_f, fields_a, rows = correct_and_pack(
        design_mask, param_map, messages, inv_eps, grad, fields_f, fields_a, devices
    )
    got = lax.all_to_all(rows, ("gx", "gy"), split_axis=0, concat_axis=0, tiled=True)
    return place_rows(got, owned), fields_f, fields_a


def solution(mesh):
    field, cells = P(None, "gx", "gy", None), P("gx", "gy", None)
    in_specs = (field, field, field, field, cells, cells, cells, cells, cells, P())
    out_specs = (P(("gx", "gy"), None), field, field)
    return jax.shard_map(body, mesh=mesh, in_specs=in_specs, out_specs=out_specs, check_vma=False)
```

```python
import functools
import math

import jax
import jax.numpy as jnp
from jax import lax
from jax.experimental import pallas as pl
from jax.experimental.pallas import tpu as pltpu
from jax.sharding import PartitionSpec as P

BZ = 4
STEPS = 2
DT = 0.5
PERIOD = 20
RATE = 2.0 * math.pi / 20.0
CX, CY, NZ = 16, 32, 512
RING = 40
F32 = jnp.float32
VMEM_BYTES = (64 << 20) - (128 << 10)
TOUCH_BYTES, EDGE_BYTES, MAIN_BYTES, PACK_BYTES = 24 << 20, 24 << 20, 24 << 20, 32 << 20

UP, DOWN = 14, 10


def cycled(value, axis, by):
    devices = lax.axis_size(axis)
    return lax.ppermute(value, axis, [(i, (i + by) % devices) for i in range(devices)])


def rows_iota(shape):
    return lax.broadcasted_iota(jnp.int32, shape, 0)


def lanes_iota(shape):
    return lax.broadcasted_iota(jnp.int32, shape, 1)


def plus_y(f):
    return pltpu.roll(f, f.shape[0] - 1, 0) - f


def minus_y(f):
    return f - pltpu.roll(f, 1, 0)


def plus_z(f):
    return jnp.where(lanes_iota(f.shape) == NZ - 1, 0.0, pltpu.roll(f, NZ - 1, 1)) - f


def minus_z(f):
    return f - jnp.where(lanes_iota(f.shape) == 0, 0.0, pltpu.roll(f, 1, 1))


def magnetic(e, e_next, h, row_dt):
    ahead_y = -e[1] if e_next is None else e_next[1] - e[1]
    ahead_z = -e[2] if e_next is None else e_next[2] - e[2]
    return (
        h[0] - row_dt * (plus_y(e[2]) - plus_z(e[1])),
        h[1] - row_dt * (plus_z(e[0]) - ahead_z),
        h[2] - row_dt * (ahead_y - plus_y(e[0])),
    )


def electric(e, h, h_prev, coef, drive):
    back_y = h[1] if h_prev is None else h[1] - h_prev[1]
    back_z = h[2] if h_prev is None else h[2] - h_prev[2]
    return (
        e[0] + coef * (minus_y(h[2]) - minus_z(h[1])),
        e[1] + coef * (minus_z(h[0]) - back_z),
        e[2] + coef * (back_y - minus_y(h[0]) - drive),
    )


def amplitude(step_index, ticks, rows):
    tick = lax.rem(step_index[0] + (PERIOD + ticks), PERIOD)
    tile = jnp.sin(RATE * jnp.full((8, 128), tick, jnp.int32).astype(F32))
    return jnp.concatenate([jnp.concatenate([tile] * (NZ // 128), axis=1)] * (rows // 8), axis=0)


def dot_three(a, b):
    return a[0] * b[0] + a[1] * b[1] + a[2] * b[2]


def plus_x(f):
    return jnp.where(rows_iota(f.shape) == f.shape[0] - 1, 0.0, pltpu.roll(f, f.shape[0] - 1, 0)) - f


def minus_x(f):
    return f - jnp.where(rows_iota(f.shape) == 0, 0.0, pltpu.roll(f, 1, 0))


def has_rows():
    place = lax.axis_index("gy")
    return place < lax.axis_size("gy") - 1, place > 0


def row_steps():
    _, has_above = has_rows()
    rows = rows_iota((8, NZ))
    tile = jnp.where((rows >= 6) & jnp.logical_not(has_above), 0.0, DT)
    return jnp.concatenate([jnp.full((CY, NZ), DT, F32), tile], axis=0)


def ring_steps():
    _, has_above = has_rows()
    tile = jnp.where((rows_iota((8, NZ)) == 7) & has_above, DT, 0.0)
    return jnp.concatenate([jnp.full((CY, NZ), DT, F32), tile], axis=0)


class Ghosts:
    def __init__(self, above, below, x):
        has_below, has_above = has_rows()
        self.refs = above, below
        self.flags = jnp.where(has_above, 1.0, 0.0).astype(F32), jnp.where(has_below, 1.0, 0.0).astype(F32)
        self.x = x

    def up(self, k, x=None):
        return self.refs[0][k, pl.ds(self.x if x is None else x, 1), :] * self.flags[0]

    def down(self, k, x=None):
        return self.refs[1][k, pl.ds(self.x if x is None else x, 1), :] * self.flags[1]

    def tile(self, rows):
        at = rows_iota((8, NZ))
        tile = jnp.zeros((8, NZ), F32)
        for row, value in rows.items():
            tile = jnp.where(at == row, value, tile)
        return tile

    def e_before(self, run):
        return (
            self.tile({0: self.down(4 * run)}),
            jnp.zeros((8, NZ), F32),
            self.tile({0: self.down(4 * run + 1)}),
        )

    def e_middle(self, run):
        return (
            self.tile({0: self.down(4 * run + 2), 7: self.up(6 * run)}),
            self.tile({7: self.up(6 * run + 1)}),
            self.tile({0: self.down(4 * run + 3), 7: self.up(6 * run + 2)}),
        )

    def h_before(self, run):
        return tuple(self.tile({7: self.up(6 * run + 3 + c)}) for c in range(3))

    def coef(self):
        return DT * self.tile({0: self.down(8), 7: self.up(12)})


def ring(own, tile):
    return jnp.concatenate([own, tile], axis=0)


def rings(own, tiles):
    return tuple(ring(own[c], tiles[c]) for c in range(3))


def rows_up(amp, e_refs, h_refs, inv, drives, out):
    coef = DT * inv[:, 7, :]
    singles = []
    for run in range(2):
        e, e_in = ([e_refs[run][c, :, r, :] for c in range(3)] for r in (7, 6))
        h, h_in = ([h_refs[run][c, :, r, :] for c in range(3)] for r in (7, 6))
        hx_in = h_in[0] - DT * ((e[2] - e_in[2]) - plus_z(e_in[1]))
        hz_in = h_in[2] - DT * (plus_x(e_in[1]) - (e[0] - e_in[0]))
        out[6 * run] = e[0] - coef * hz_in
        out[6 * run + 1] = e[1]
        out[6 * run + 2] = e[2] + coef * (hx_in - amp[run] * drives[run][:, 7, :])
        out[6 * run + 3] = h[0] + DT * (e[2] + plus_z(e[1]))
        out[6 * run + 4] = h[1] - DT * (plus_z(e[0]) - plus_x(e[2]))
        out[6 * run + 5] = h[2] - DT * (plus_x(e[1]) + e[0])
        singles += [e[2], e_in[1]]
    out[12] = inv[:, 7, :]
    rows = rows_iota((CX, NZ))
    held = singles[0]
    for k in range(1, 4):
        held = jnp.where(rows == k, pltpu.roll(singles[k], k, 0), held)
    out[13] = held


def rows_down(amp, e_refs, h_refs, inv, drives, out):
    coef = DT * inv[:, 0, :]
    singles, others = [], []
    for run in range(2):
        e, e_in = ([e_refs[run][c, :, r, :] for c in range(3)] for r in (0, 1))
        h = [h_refs[run][c, :, 0, :] for c in range(3)]
        hx = h[0] - DT * ((e_in[2] - e[2]) - plus_z(e[1]))
        hy = h[1] - DT * (plus_z(e[0]) - plus_x(e[2]))
        hz = h[2] - DT * (plus_x(e[1]) - (e_in[0] - e[0]))
        out[4 * run] = e[0]
        out[4 * run + 1] = e[2]
        out[4 * run + 2] = e[0] + coef * (hz - minus_z(hy))
        out[4 * run + 3] = e[2] + coef * (minus_x(hy) - hx - amp[run] * drives[run][:, 0, :])
        singles.append(e[1])
        others.append(hy)
    out[8] = inv[:, 0, :]
    rows = rows_iota((CX, NZ))
    held = singles[0]
    for k, (value, by) in enumerate([(singles[1], 1), (others[0], 3), (others[1], 4)], 1):
        held = jnp.where(rows == k, pltpu.roll(value, by, 0), held)
    out[9] = held


def pack_kernel(step_index, e_f, h_f, e_a, h_a, inv, src, adj, far_up, far_down, *scratch):
    sources = (e_f, h_f, e_a, h_a, inv, src, adj)
    places, (up, down, sems, out_sems) = scratch[:7], scratch[7:]
    stores = [pltpu.make_async_copy(up, far_up, out_sems.at[0]), pltpu.make_async_copy(down, far_down, out_sems.at[1])]

    def load(a, side):
        at = pl.ds(24 if side == 0 else 0, 8)
        source = sources[a].at[:, :, at] if a < 4 else sources[a].at[:, at]
        return pltpu.make_async_copy(source, places[a].at[side], sems.at[a, side])

    for side in range(2):
        for a in range(7):
            load(a, side).start()
    amp = [amplitude(step_index, ticks, CX) for ticks in (1, -1)]
    for side, (rows_of, out) in enumerate([(rows_up, up), (rows_down, down)]):
        for a in range(7):
            load(a, side).wait()
        ef, hf, ea, ha, coef, drive_f, drive_a = (place.at[side] for place in places)
        rows_of(amp, (ef, ea), (hf, ha), coef, (drive_f, drive_a), out)
        stores[side].start()
    for copy in stores:
        copy.wait()


def pack_rows(step_index, arrays):
    hbm = pl.BlockSpec(memory_space=pl.ANY)
    shapes = [(UP, CX, NZ), (DOWN, CX, NZ)]
    return pl.pallas_call(
        pack_kernel,
        in_specs=[pl.BlockSpec(memory_space=pltpu.SMEM)] + [hbm] * 7,
        out_specs=[hbm] * 2,
        out_shape=[jax.ShapeDtypeStruct(s, F32) for s in shapes],
        scratch_shapes=[pltpu.VMEM((2, 3, CX, 8, NZ), F32)] * 4
        + [pltpu.VMEM((2, CX, 8, NZ), F32)] * 3
        + [pltpu.VMEM(s, F32) for s in shapes]
        + [pltpu.SemaphoreType.DMA((7, 2)), pltpu.SemaphoreType.DMA((2,))],
        compiler_params=pltpu.CompilerParams(vmem_limit_bytes=VMEM_BYTES),
        cost_estimate=pl.CostEstimate(flops=4 * 10**9, bytes_accessed=0, transcendentals=0),
        name="pack_rows",
    )(step_index, *arrays)


def touch_kernel(*refs):
    refs[-1][...] = refs[4][0, :8, :128]


def touch(arrays):
    whole = pl.BlockSpec(memory_space=pltpu.VMEM)
    return pl.pallas_call(
        touch_kernel,
        in_specs=[whole] * 7,
        out_specs=whole,
        out_shape=jax.ShapeDtypeStruct((8, 128), F32),
        compiler_params=pltpu.CompilerParams(vmem_limit_bytes=TOUCH_BYTES),
        cost_estimate=pl.CostEstimate(flops=6 * 10**9, bytes_accessed=0, transcendentals=0),
        name="touch",
    )(*arrays)


def write_layers(out, values):
    rows = rows_iota((8, NZ))
    for k, value in enumerate(values):
        out[pl.ds(CY * k, CY), :] = value[:CY]
    for k in range(0, 9, 2):
        tile = pltpu.roll(values[k][CY:], 2, 0)
        if k < 8:
            tile = jnp.where(rows < 4, tile, pltpu.roll(values[k + 1][CY:], 6, 0))
        out[pl.ds(9 * CY + 4 * k, 8), :] = tile


def read_layer(ref, k):
    tile = ref[pl.ds(9 * CY + 8 * (k // 2), 8), :]
    return ring(ref[pl.ds(CY * k, CY), :], pltpu.roll(tile, 2 if k % 2 else 6, 0))


def call_edges(kernel, name, step_index, arrays, messages, shapes):
    whole = pl.BlockSpec(memory_space=pltpu.VMEM)

    def body(step_index, *refs):
        sides = []
        for side in range(2):
            at = pl.ds(side * (CX - 2), 2)
            sides += [refs[a].at[:, at] if a < 4 else refs[a].at[at] for a in range(7)]
        kernel(step_index, *sides, *refs[7:9], *refs[10:])

    return pl.pallas_call(
        body,
        in_specs=[pl.BlockSpec(memory_space=pltpu.SMEM)] + [whole] * (7 + len(messages)),
        out_specs=[whole] * len(shapes),
        out_shape=[jax.ShapeDtypeStruct(s, F32) for s in shapes],
        compiler_params=pltpu.CompilerParams(vmem_limit_bytes=EDGE_BYTES),
        cost_estimate=pl.CostEstimate(flops=3 * 10**9, bytes_accessed=0, transcendentals=0),
        name=name,
    )(step_index, *arrays, *messages)


def edge_kernel(step_index, e_f0, h_f0, e_a0, h_a0, inv0, src0, adj0, e_f1, h_f1, e_a1, h_a1, inv1, src1, adj1, above, below, out_prev, out_next, keep):
    row_dt = ring_steps()
    ghosts = {x: Ghosts(above, below, x) for x in (0, 1, CX - 2, CX - 1)}
    still = jnp.zeros((8, NZ), F32)
    amp = [amplitude(step_index, ticks, CY) for ticks in (1, -1)]

    def before(ref, at, run, x):
        return rings([ref[c, at] for c in range(3)], ghosts[x].e_before(run))

    def middle(ref, at, run, x):
        return rings([ref[c, at] for c in range(3)], ghosts[x].e_middle(run))

    def magnet(ref, at, run, x):
        return rings([ref[c, at] for c in range(3)], ghosts[x].h_before(run))

    coef_first = ring(DT * inv0[0], ghosts[0].coef())
    coef_last = ring(DT * inv1[1], ghosts[CX - 1].coef())
    to_prev, to_next = [None] * 9, [None] * 9
    to_prev[8] = coef_first
    to_next[8] = coef_last
    for run, (e0, h0, s0, e1, h1, s1) in enumerate(
        [(e_f0, h_f0, src0, e_f1, h_f1, src1), (e_a0, h_a0, adj0, e_a1, h_a1, adj1)]
    ):
        near = ghosts[0]
        h = magnetic(before(e0, 0, run, 0), before(e0, 1, run, 1), magnet(h0, 0, run, 0), row_dt)
        drive = ring(amp[run] * s0[0], still)
        new = electric(middle(e0, 0, run, 0), h, None, coef_first, drive)
        sides_y = {0: near.down(9, run), 6: near.up(13, 2 * run + 1), 7: near.up(6 * run + 1)}
        sides_z = {0: near.down(4 * run + 1), 7: near.up(13, 2 * run)}
        to_prev[4 * run] = ring(e0[1, 0], near.tile(sides_y))
        to_prev[4 * run + 1] = ring(e0[2, 0], near.tile(sides_z))
        to_prev[4 * run + 2] = new[1]
        to_prev[4 * run + 3] = new[2]
        keep[4 * run] = new[0][:CY]
        e, back = before(e1, 1, run, CX - 1), before(e1, 0, run, CX - 2)
        h = magnetic(e, None, magnet(h1, 1, run, CX - 1), row_dt)
        h_back = magnetic(back, e, magnet(h1, 0, run, CX - 2), row_dt)
        drive = ring(amp[run] * s1[1], still)
        new = electric(middle(e1, 1, run, CX - 1), h, h_back, coef_last, drive)
        later = magnetic(new, None, h, row_dt)
        beyond = ghosts[CX - 1].down(9, 2 + run)
        to_next[4 * run] = jnp.where(rows_iota((RING, NZ)) == CY, beyond, h[1])
        to_next[4 * run + 1] = h[2]
        to_next[4 * run + 2] = later[1]
        to_next[4 * run + 3] = later[2]
        for c in range(3):
            keep[4 * run + 1 + c] = new[c][:CY]
    write_layers(out_prev, to_prev)
    write_layers(out_next, to_next)


def solve_edges(step_index, arrays, above, below, touched):
    shapes = [(9 * CY + 40, NZ), (9 * CY + 40, NZ), (8, CY, NZ)]
    return call_edges(edge_kernel, "solve_edges", step_index, arrays, [above, below, touched], shapes)


CHUNK = 2
DRAIN = 4


def zplus(tile):
    moved = pltpu.roll(tile, NZ - 1, 1)
    last = jnp.where(lanes_iota((8, 128)) == 127, 0.0, moved[:, NZ - 128 :])
    return jnp.concatenate([moved[:, : NZ - 128], last], axis=1) - tile


def zminus(tile):
    moved = pltpu.roll(tile, 1, 1)
    first = jnp.where(lanes_iota((8, 128)) == 0, 0.0, moved[:, :128])
    return tile - jnp.concatenate([first, moved[:, 128:]], axis=1)


def magnetic_tiles(tiles, e, e_next, h, row_dts, put, closed):
    end = rows_iota((8, NZ)) == 7
    firsts = {c: pltpu.roll(e(c, 0), 7, 0) for c in (0, 2)}
    here = firsts
    for t in range(tiles):
        if t == tiles - 1:
            after = {c: jnp.zeros((8, NZ), F32) for c in (0, 2)} if closed else firsts
        else:
            after = {c: pltpu.roll(e(c, t + 1), 7, 0) for c in (0, 2)}
        ex, ey, ez = (e(c, t) for c in range(3))
        put(0, t, h(0, t) - row_dts[t] * ((jnp.where(end, after[2], here[2]) - ez) - zplus(ey)))
        put(1, t, h(1, t) - row_dts[t] * (zplus(ex) - (e_next(2, t) - ez)))
        put(2, t, h(2, t) - row_dts[t] * ((e_next(1, t) - ey) - (jnp.where(end, after[0], here[0]) - ex)))
        here = after


def electric_tile(e, h, h_prev, coef, drive, t, rolled):
    start = rows_iota((8, NZ)) == 0
    hx, hy, hz = (h(c, t) for c in range(3))
    moved = {0: pltpu.roll(hx, 1, 0), 2: pltpu.roll(hz, 1, 0)}
    new_x = e(0, t) + coef * ((hz - jnp.where(start, rolled[2], moved[2])) - zminus(hy))
    new_y = e(1, t) + coef * (zminus(hx) - (hz - h_prev(2, t)))
    curl = (hy - h_prev(1, t)) - (hx - jnp.where(start, rolled[0], moved[0]))
    new_z = e(2, t) + coef * (curl if drive is None else curl - drive)
    return (new_x, new_y, new_z), moved


def sweep(step_index, places, store, mid_h, mid_e, late_h, tiles, at_rows, ghosts, put_last):
    v_ef, v_hf, v_ea, v_ha, v_inv, v_src, v_adj = places
    own = [t for t in range(tiles) if at_rows[t] is not None]
    closed = len(own) == tiles
    mid_h[...] = jnp.zeros_like(mid_h)
    late_h[...] = jnp.zeros_like(late_h)
    ghost_dt = None if closed else ring_steps()[CY:]
    row_dts = [DT if t in own else ghost_dt for t in range(tiles)]
    amp = [[amplitude(step_index, ticks, 8) for ticks in pair] for pair in ((1, 2), (-1, -2))]
    runs = ((v_ef, v_hf, v_src), (v_ea, v_ha, v_adj))
    nothing = {c: jnp.zeros((8, NZ), F32) for c in (0, 2)}

    def rows(t):
        return pl.ds(at_rows[t], 8)

    def ring_rows(t):
        return pl.ds(8 * t, 8)

    def one(step, carry):
        now, then = lax.rem(step, 2), lax.rem(step + 1, 2)

        @pl.when(step <= CX)
        def _():
            x = step - 1
            inside, x_next = step < CX, jnp.minimum(step, CX - 1)
            if not closed:
                here, there = ghosts(x), ghosts(jnp.minimum(step, CX - 1))
                coef_ghost = here.coef()
            for run, (e_ref, h_ref, s_ref) in enumerate(runs):
                beside = beside_next = beside_h = middle = None
                if not closed:
                    beside = here.e_before(run)
                    beside_next = [jnp.where(inside, v, 0.0) for v in there.e_before(run)]
                    beside_h = here.h_before(run)
                    middle = here.e_middle(run)

                def put_h(c, t, value):
                    mid_h[now, 3 * run + c, ring_rows(t), :] = value

                magnetic_tiles(
                    tiles,
                    lambda c, t: e_ref[c, x, rows(t), :] if t in own else beside[c],
                    lambda c, t: jnp.where(inside, e_ref[c, x_next, rows(t), :], 0.0) if t in own else beside_next[c],
                    lambda c, t: h_ref[c, x, rows(t), :] if t in own else beside_h[c],
                    row_dts,
                    put_h,
                    closed,
                )
                rolled = nothing
                if not closed:
                    end = ring_rows(tiles - 1)
                    rolled = {c: pltpu.roll(mid_h[now, 3 * run + c, end, :], 1, 0) for c in (0, 2)}
                for t in range(tiles):
                    if t in own:
                        coef, drive = DT * v_inv[x, rows(t), :], amp[run][0] * s_ref[x, rows(t), :]
                    else:
                        coef, drive = coef_ghost, None
                    new, rolled = electric_tile(
                        lambda c, t: e_ref[c, x, rows(t), :] if t in own else middle[c],
                        lambda c, t: mid_h[now, 3 * run + c, ring_rows(t), :],
                        lambda c, t: mid_h[then, 3 * run + c, ring_rows(t), :],
                        coef,
                        drive,
                        t,
                        rolled,
                    )
                    for c in range(3):
                        mid_e[now, 3 * run + c, ring_rows(t), :] = new[c]

        @pl.when(step > CX)
        def _():
            mid_e[now] = jnp.zeros((6, 8 * tiles, NZ), F32)

        @pl.when(step > 1)
        def _():
            x = step - 2
            rolled = [nothing, nothing]
            for run in range(2):

                def put_late(c, t, value):
                    late_h[now, 3 * run + c, ring_rows(t), :] = value

                magnetic_tiles(
                    tiles,
                    lambda c, t: mid_e[then, 3 * run + c, ring_rows(t), :],
                    lambda c, t: mid_e[now, 3 * run + c, ring_rows(t), :],
                    lambda c, t: mid_h[then, 3 * run + c, ring_rows(t), :],
                    row_dts,
                    put_late,
                    closed,
                )
            for t in range(tiles):
                if t not in own:
                    rolled = [
                        {c: pltpu.roll(late_h[now, 3 * run + c, ring_rows(t), :], 1, 0) for c in (0, 2)}
                        for run in range(2)
                    ]
                    continue
                coef = DT * v_inv[x, rows(t), :]
                new = [None, None]
                for run, (e_ref, _, s_ref) in enumerate(runs):
                    new[run], rolled[run] = electric_tile(
                        lambda c, t: mid_e[then, 3 * run + c, ring_rows(t), :],
                        lambda c, t: late_h[now, 3 * run + c, ring_rows(t), :],
                        lambda c, t: late_h[then, 3 * run + c, ring_rows(t), :],
                        coef,
                        amp[run][1] * s_ref[x, rows(t), :],
                        t,
                        rolled[run],
                    )
                first = [[mid_e[then, 3 * run + c, ring_rows(t), :] for c in range(3)] for run in range(2)]
                put_last(x, t, new, DT * (dot_three(*first) + dot_three(*new)))

        @pl.when((step > 2) & (step % DRAIN == 1))
        def _():
            for a in range(2):
                store(a, step // DRAIN - 1).start()

        return carry

    lax.fori_loop(1, CX + 2, one, 0)
    for part in range(CX // DRAIN):
        for a in range(2):
            store(a, part).wait()


def main_kernel(
    step_index, e_f, h_f, e_a, h_a, inv, src, adj, above, below, out_f, out_a, grad,
    last_f, last_a, mid_h, mid_e, late_h, store_sem,
):
    def store(a, part):
        at = pl.ds(part * DRAIN, DRAIN)
        return pltpu.make_async_copy((last_f, last_a)[a].at[:, at], (out_f, out_a)[a].at[:, at], store_sem.at[a, part])

    def put_last(x, t, new, product):
        for c in range(3):
            last_f[c, x, pl.ds(8 * t - 8, 8), :] = new[0][c]
            last_a[c, x, pl.ds(8 * t - 8, 8), :] = new[1][c]
        grad[x, pl.ds(8 * t - 8, 8), :] = product

    sweep(
        step_index, (e_f, h_f, e_a, h_a, inv, src, adj), store, mid_h, mid_e, late_h, 5, [None, 0, 8, 16, 24],
        lambda x: Ghosts(above, below, x), put_last,
    )


def solve_main(step_index, arrays, above, below):
    free, whole = pl.BlockSpec(memory_space=pl.ANY), pl.BlockSpec(memory_space=pltpu.VMEM)
    field, cells = (3, CX, CY, NZ), (CX, CY, NZ)
    return pl.pallas_call(
        main_kernel,
        in_specs=[pl.BlockSpec(memory_space=pltpu.SMEM)] + [whole] * 9,
        out_specs=[free, free, whole],
        out_shape=[jax.ShapeDtypeStruct(s, F32) for s in (field, field, cells)],
        scratch_shapes=[pltpu.VMEM(field, F32)] * 2
        + [pltpu.VMEM((2, 6, RING, NZ), F32)] * 3
        + [pltpu.SemaphoreType.DMA((2, CX // DRAIN))],
        compiler_params=pltpu.CompilerParams(vmem_limit_bytes=MAIN_BYTES),
        cost_estimate=pl.CostEstimate(flops=14 * 10**9, bytes_accessed=0, transcendentals=0),
        name="solve_main",
    )(step_index, *arrays, above, below)


def split(value):
    high = value.astype(jnp.bfloat16)
    return high, (value - high.astype(F32)).astype(jnp.bfloat16)


def exact_dot(a, b, dims):
    high, low = split(b)
    a = a.astype(jnp.bfloat16)
    return lax.dot_general(a, high, dims, preferred_element_type=F32) + lax.dot_general(
        a, low, dims, preferred_element_type=F32
    )


def correct_prev(run, from_prev, own, row_dt, present):
    e0y, e0z, e1y, e1z = (own[4 * run + k] for k in range(4))
    coef, ghost_coef = own[8], jnp.where(present, from_prev[8], 0.0)
    h1y, h1z, h2y, h2z = (from_prev[4 * run + k] for k in range(4))
    d_h1y, d_h1z = DT * e0z, -DT * e0y
    h1y = jnp.where(present, h1y + d_h1y, 0.0)
    h1z = jnp.where(present, h1z + d_h1z, 0.0)
    d_e1y, d_e1z = coef * h1z, -coef * h1y
    g_e1x = ghost_coef * (minus_y(d_h1z) - minus_z(d_h1y))
    g_e1y, g_e1z = -ghost_coef * d_h1z, ghost_coef * d_h1y
    h2y = jnp.where(present, h2y + d_h1y - DT * (plus_z(g_e1x) - (e1z + d_e1z - g_e1z)), 0.0)
    h2z = jnp.where(present, h2z + d_h1z - DT * ((e1y + d_e1y - g_e1y) - plus_y(g_e1x)), 0.0)
    d_h2x = -row_dt * (plus_y(d_e1z) - plus_z(d_e1y))
    d_h2y, d_h2z = -row_dt * d_e1z, row_dt * d_e1y
    first = (None, d_e1y, d_e1z)
    last = (
        coef * (minus_y(d_h2z) - minus_z(d_h2y)),
        d_e1y + coef * (minus_z(d_h2x) - d_h2z + h2z),
        d_e1z + coef * (d_h2y - h2y - minus_y(d_h2x)),
    )
    return first, last, d_h2y, d_h2z


def correct_next(run, from_next, own, row_dt, present):
    e0y, e0z, e1y, e1z = (jnp.where(present, from_next[4 * run + k], 0.0) for k in range(4))
    coef, ghost_coef = own[8], jnp.where(present, from_next[8], 0.0)
    h1y, h1z = own[4 * run], own[4 * run + 1]
    d_h1y, d_h1z = DT * e0z, -DT * e0y
    d_e1x = coef * (minus_y(d_h1z) - minus_z(d_h1y))
    d_e1y, d_e1z = -coef * d_h1z, coef * d_h1y
    e1y = e1y + ghost_coef * (h1z + d_h1z)
    e1z = e1z - ghost_coef * (h1y + d_h1y)
    d_h2x = -row_dt * (plus_y(d_e1z) - plus_z(d_e1y))
    d_h2y = d_h1y - row_dt * (plus_z(d_e1x) - (e1z - d_e1z))
    d_h2z = d_h1z - row_dt * ((e1y - d_e1y) - plus_y(d_e1x))
    b_h2y, b_h2z = row_dt * d_e1z, -row_dt * d_e1y
    first = (d_e1x, d_e1y, d_e1z)
    last = (
        d_e1x + coef * (minus_y(d_h2z) - minus_z(d_h2y)),
        d_e1y + coef * (minus_z(d_h2x) - d_h2z + b_h2z),
        d_e1z + coef * (d_h2y - b_h2y - minus_y(d_h2x)),
    )
    return first, last, b_h2y, b_h2z


def correct_kernel(
    mask, param, *refs
):
    far, refs = refs[:5], refs[5:]
    far_inv, far_grad, old_f, old_a, out_f, out_a, rows_out, *refs = refs
    near, refs = refs[:5], refs[5:]
    (
    v_inv, work, v_f, v_a, chosen,
    message_sem, inv_sem, grad_sem, field_sem, store_sem,
    ) = refs
    ref_from_prev, ref_to_prev, keep, ref_from_next, ref_to_next = near
    place = lax.axis_index("gx")
    has_prev, has_next = place > 0, place < lax.axis_size("gx") - 1
    row_dt = row_steps()
    messages = [pltpu.make_async_copy(a, b, message_sem.at[k]) for k, (a, b) in enumerate(zip(far, near))]
    grads = [
        pltpu.make_async_copy(far_grad.at[pl.ds(4 * q, 4)], work.at[pl.ds(4 * q, 4)], grad_sem.at[q]) for q in range(4)
    ]
    ends, stores = [], []
    for side in range(2):
        at = pl.ds(side * (CX - 2), 2)
        ends.append(
            [
                pltpu.make_async_copy(far_inv.at[at], v_inv.at[side], inv_sem.at[side]),
                pltpu.make_async_copy(old_f.at[:, at], v_f.at[side], field_sem.at[0, side]),
                pltpu.make_async_copy(old_a.at[:, at], v_a.at[side], field_sem.at[1, side]),
            ]
        )
        stores.append(
            [
                pltpu.make_async_copy(v_f.at[side], out_f.at[:, at], store_sem.at[0, side]),
                pltpu.make_async_copy(v_a.at[side], out_a.at[:, at], store_sem.at[1, side]),
            ]
        )
    for copy in [grads[1], grads[2], *messages[:3], *ends[0], grads[0], *messages[3:], *ends[1], grads[3]]:
        copy.start()

    def finish(side, edge_at, inner_at, firsts, lasts, d_inner, inner_coef, base_first):
        total_f, total_a, inner_f, inner_a = [], [], [], []
        fields_f, fields_a = v_f.at[side], v_a.at[side]
        before = jnp.zeros((CY, NZ), F32)
        for c in range(3):
            before = before + fields_f[c, inner_at] * fields_a[c, inner_at]
        for run, (ref, total, inner) in enumerate([(fields_f, total_f, inner_f), (fields_a, total_a, inner_a)]):
            for c in range(3):
                total.append(ref[c, edge_at] + lasts[run][c][:CY])
                ref[c, edge_at] = total[c]
                add = d_inner[run][c]
                inner.append(ref[c, inner_at] if add is None else ref[c, inner_at] + inner_coef * add[:CY])
                ref[c, inner_at] = inner[c]
        e1 = [
            [base_first[run][c] if firsts[run][c] is None else base_first[run][c] + firsts[run][c][:CY] for c in range(3)]
            for run in range(2)
        ]
        edge_grad = DT * (dot_three(e1[0], e1[1]) + dot_three(total_f, total_a))
        inner_change = DT * (dot_three(inner_f, inner_a) - before)
        return edge_grad, inner_change

    def first_edge():
        firsts, lasts, d_inner, base = [], [], [], []
        from_prev, to_prev = ([read_layer(ref, k) for k in range(9)] for ref in (ref_from_prev, ref_to_prev))
        for run in range(2):
            first, last, d_h2y, d_h2z = correct_prev(run, from_prev, to_prev, row_dt, has_prev)
            firsts.append(first)
            lasts.append(last)
            d_inner.append((None, d_h2z, -d_h2y))
            base.append((keep[4 * run], to_prev[4 * run + 2][:CY], to_prev[4 * run + 3][:CY]))
        edge, inner = finish(0, 0, 1, firsts, lasts, d_inner, DT * v_inv[0, 1], base)
        work[0] = edge
        work[1] = work[1] + inner

    def last_edge():
        firsts, lasts, d_inner, base = [], [], [], []
        from_next = [read_layer(ref_from_next, k) for k in range(9)]
        to_next = {k: read_layer(ref_to_next, k) for k in (0, 1, 4, 5, 8)}
        for run in range(2):
            first, last, b_h2y, b_h2z = correct_next(run, from_next, to_next, row_dt, has_next)
            firsts.append(first)
            lasts.append(last)
            d_inner.append((minus_y(b_h2z) - minus_z(b_h2y), -b_h2z, b_h2y))
            base.append(tuple(keep[4 * run + 1 + c] for c in range(3)))
        edge, inner = finish(1, 1, 0, firsts, lasts, d_inner, DT * v_inv[1, 0], base)
        work[CX - 1] = edge
        work[CX - 2] = work[CX - 2] + inner

    devices = rows_out.shape[0]
    lanes = lanes_iota((devices, NZ))
    blocks = lax.broadcasted_iota(jnp.int32, (NZ // BZ, NZ), 0)
    spread = (blocks == lanes_iota((NZ // BZ, NZ)) // BZ).astype(jnp.bfloat16)
    owned = NZ // BZ // 2
    owner = jnp.where(mask[0] == 1, param[0] // owned, -1).astype(F32)
    slot = (param[0] & (owned - 1)).astype(F32)
    numbers = jnp.concatenate([owner, slot, jnp.zeros((14, NZ // BZ), F32)], axis=0)
    numbers = jnp.dot(numbers.astype(jnp.bfloat16), spread, preferred_element_type=F32)
    mine = numbers[0:1, :] == rows_iota((devices, NZ)).astype(F32)
    for part in range(BZ):
        chosen[pl.ds(part * devices, devices), :] = jnp.where(mine & (lanes % BZ == part), 1.0, 0.0).astype(jnp.bfloat16)
    found = jnp.sum(jnp.where(mine & (lanes % BZ == 0), numbers[1:2, :] + 1.0, 0.0), axis=1, keepdims=True) - 1.0
    rows_out[:, 0, BZ * CX * CY :] = jnp.broadcast_to(found, (devices, 128))

    def pack(q):
        values = work[pl.ds(4 * q, 4)].reshape(4 * CY, NZ)
        cells = exact_dot(chosen[...], values, (((1,), (1,)), ((), ())))
        for part in range(BZ):
            at = part * CX * CY + q * 4 * CY
            rows_out[:, 0, at : at + 4 * CY] = cells[part * devices : (part + 1) * devices]

    for q in (1, 2):
        grads[q].wait()
        pack(q)
    for copy in [*messages[:3], *ends[0], grads[0]]:
        copy.wait()
    first_edge()
    for copy in stores[0]:
        copy.start()
    pack(0)
    for copy in [*messages[3:], *ends[1], grads[3]]:
        copy.wait()
    last_edge()
    for copy in stores[1]:
        copy.start()
    pack(3)
    for copy in [*stores[0], *stores[1]]:
        copy.wait()


def correct_and_pack(mask, param, messages, inv, grad, fields_f, fields_a, devices):
    free, whole = pl.BlockSpec(memory_space=pl.ANY), pl.BlockSpec(memory_space=pltpu.VMEM)
    width = BZ * CX * CY + 128
    vmem = lambda shape: pltpu.VMEM(shape, F32)
    return pl.pallas_call(
        correct_kernel,
        in_specs=[whole] * 2 + [free] * 9,
        out_specs=[free, free, whole],
        out_shape=[
            jax.ShapeDtypeStruct((3, CX, CY, NZ), F32),
            jax.ShapeDtypeStruct((3, CX, CY, NZ), F32),
            jax.ShapeDtypeStruct((devices, 1, width), F32),
        ],
        scratch_shapes=[vmem(m.shape) for m in messages]
        + [vmem((2, 2, CY, NZ)), vmem((CX, CY, NZ))]
        + [vmem((2, 3, 2, CY, NZ))] * 2
        + [pltpu.VMEM((BZ * devices, NZ), jnp.bfloat16)]
        + [pltpu.SemaphoreType.DMA(s) for s in ((5,), (2,), (4,), (2, 2), (2, 2))],
        input_output_aliases={9: 0, 10: 1},
        compiler_params=pltpu.CompilerParams(vmem_limit_bytes=PACK_BYTES),
        cost_estimate=pl.CostEstimate(flops=6 * 10**9, bytes_accessed=0, transcendentals=0),
        name="correct_and_pack",
    )(mask, param, *messages, inv, grad, fields_f, fields_a)


def place_kernel(got, out):
    devices = got.shape[0]
    owned = out.shape[0]
    cells = BZ * CX * CY
    numbers = got[:, 0, cells:]
    wanted = (numbers == lanes_iota((devices, 128)).astype(F32)).astype(F32)
    placing = jnp.transpose(wanted)[:owned]
    order_from = rows_iota((4 * 128, 4 * 128))
    order_to = lanes_iota((4 * 128, 4 * 128))
    order = (order_from == (order_to % BZ) * 128 + order_to // BZ).astype(jnp.bfloat16)
    dims = (((1,), (0,)), ((), ()))
    for q in range(4):
        parts = [got[:, 0, part * CX * CY + q * 128 : part * CX * CY + (q + 1) * 128] for part in range(BZ)]
        rows = exact_dot(placing, jnp.concatenate(parts, axis=1), dims)
        high, low = split(rows)
        out[:, q * 512 : (q + 1) * 512] = lax.dot_general(
            high, order, dims, preferred_element_type=F32
        ) + lax.dot_general(low, order, dims, preferred_element_type=F32)


def place_rows(got, owned):
    return pl.pallas_call(
        place_kernel,
        out_shape=jax.ShapeDtypeStruct((owned, BZ * CX * CY), F32),
        compiler_params=pltpu.CompilerParams(vmem_limit_bytes=32 << 20),
        cost_estimate=pl.CostEstimate(flops=2 * 10**9, bytes_accessed=0, transcendentals=0),
        name="place_rows",
    )(got)


def body(e_forward, h_forward, e_adjoint, h_adjoint, inv_eps, source, adj_source, design_mask, param_map, step_index):
    arrays = (e_forward, h_forward, e_adjoint, h_adjoint, inv_eps, source, adj_source)
    devices = lax.axis_size("gx") * lax.axis_size("gy")
    blocks = NZ // BZ
    owned = blocks // 2
    up, down = pack_rows(step_index, arrays)
    above, below = cycled(up, "gy", 1), cycled(down, "gy", -1)
    touched = touch(arrays)
    to_prev, to_next, keep = solve_edges(step_index, arrays, above, below, touched)
    from_next, from_prev = cycled(to_prev, "gx", -1), cycled(to_next, "gx", 1)
    fields_f, fields_a, grad = solve_main(step_index, arrays, above, below)
    messages = (from_prev, to_prev, keep, from_next, to_next)
    fields_f, fields_a, rows = correct_and_pack(
        design_mask, param_map, messages, inv_eps, grad, fields_f, fields_a, devices
    )
    got = lax.all_to_all(rows, ("gx", "gy"), split_axis=0, concat_axis=0, tiled=True)
    return place_rows(got, owned), fields_f, fields_a


def solution(mesh):
    field, cells = P(None, "gx", "gy", None), P("gx", "gy", None)
    in_specs = (field, field, field, field, cells, cells, cells, cells, cells, P())
    out_specs = (P(("gx", "gy"), None), field, field)
    return jax.shard_map(body, mesh=mesh, in_specs=in_specs, out_specs=out_specs, check_vma=False)
```

```python
import functools
import math

import jax
import jax.numpy as jnp
from jax import lax
from jax.experimental import pallas as pl
from jax.experimental.pallas import tpu as pltpu
from jax.sharding import PartitionSpec as P

BZ = 4
STEPS = 2
DT = 0.5
PERIOD = 20
RATE = 2.0 * math.pi / 20.0
CX, CY, NZ = 16, 32, 512
RING = 40
F32 = jnp.float32
VMEM_BYTES = (64 << 20) - (128 << 10)
TOUCH_BYTES, EDGE_BYTES, MAIN_BYTES, PACK_BYTES = 24 << 20, 24 << 20, 24 << 20, 32 << 20

UP, DOWN = 14, 10


def cycled(value, axis, by):
    devices = lax.axis_size(axis)
    return lax.ppermute(value, axis, [(i, (i + by) % devices) for i in range(devices)])


def rows_iota(shape):
    return lax.broadcasted_iota(jnp.int32, shape, 0)


def lanes_iota(shape):
    return lax.broadcasted_iota(jnp.int32, shape, 1)


def plus_y(f):
    return pltpu.roll(f, f.shape[0] - 1, 0) - f


def minus_y(f):
    return f - pltpu.roll(f, 1, 0)


def plus_z(f):
    return jnp.where(lanes_iota(f.shape) == NZ - 1, 0.0, pltpu.roll(f, NZ - 1, 1)) - f


def minus_z(f):
    return f - jnp.where(lanes_iota(f.shape) == 0, 0.0, pltpu.roll(f, 1, 1))


def magnetic(e, e_next, h, row_dt):
    ahead_y = -e[1] if e_next is None else e_next[1] - e[1]
    ahead_z = -e[2] if e_next is None else e_next[2] - e[2]
    return (
        h[0] - row_dt * (plus_y(e[2]) - plus_z(e[1])),
        h[1] - row_dt * (plus_z(e[0]) - ahead_z),
        h[2] - row_dt * (ahead_y - plus_y(e[0])),
    )


def electric(e, h, h_prev, coef, drive):
    back_y = h[1] if h_prev is None else h[1] - h_prev[1]
    back_z = h[2] if h_prev is None else h[2] - h_prev[2]
    return (
        e[0] + coef * (minus_y(h[2]) - minus_z(h[1])),
        e[1] + coef * (minus_z(h[0]) - back_z),
        e[2] + coef * (back_y - minus_y(h[0]) - drive),
    )


def amplitude(step_index, ticks, rows):
    tick = lax.rem(step_index[0] + (PERIOD + ticks), PERIOD)
    tile = jnp.sin(RATE * jnp.full((8, 128), tick, jnp.int32).astype(F32))
    return jnp.concatenate([jnp.concatenate([tile] * (NZ // 128), axis=1)] * (rows // 8), axis=0)


def dot_three(a, b):
    return a[0] * b[0] + a[1] * b[1] + a[2] * b[2]


def plus_x(f):
    return jnp.where(rows_iota(f.shape) == f.shape[0] - 1, 0.0, pltpu.roll(f, f.shape[0] - 1, 0)) - f


def minus_x(f):
    return f - jnp.where(rows_iota(f.shape) == 0, 0.0, pltpu.roll(f, 1, 0))


def has_rows():
    place = lax.axis_index("gy")
    return place < lax.axis_size("gy") - 1, place > 0


def row_steps():
    _, has_above = has_rows()
    rows = rows_iota((8, NZ))
    tile = jnp.where((rows >= 6) & jnp.logical_not(has_above), 0.0, DT)
    return jnp.concatenate([jnp.full((CY, NZ), DT, F32), tile], axis=0)


def ring_steps():
    _, has_above = has_rows()
    tile = jnp.where((rows_iota((8, NZ)) == 7) & has_above, DT, 0.0)
    return jnp.concatenate([jnp.full((CY, NZ), DT, F32), tile], axis=0)


class Ghosts:
    def __init__(self, above, below, x):
        has_below, has_above = has_rows()
        self.refs = above, below
        self.flags = jnp.where(has_above, 1.0, 0.0).astype(F32), jnp.where(has_below, 1.0, 0.0).astype(F32)
        self.x = x

    def up(self, k, x=None):
        return self.refs[0][k, pl.ds(self.x if x is None else x, 1), :] * self.flags[0]

    def down(self, k, x=None):
        return self.refs[1][k, pl.ds(self.x if x is None else x, 1), :] * self.flags[1]

    def tile(self, rows):
        at = rows_iota((8, NZ))
        tile = jnp.zeros((8, NZ), F32)
        for row, value in rows.items():
            tile = jnp.where(at == row, value, tile)
        return tile

    def e_before(self, run):
        return (
            self.tile({0: self.down(4 * run)}),
            jnp.zeros((8, NZ), F32),
            self.tile({0: self.down(4 * run + 1)}),
        )

    def e_middle(self, run):
        return (
            self.tile({0: self.down(4 * run + 2), 7: self.up(6 * run)}),
            self.tile({7: self.up(6 * run + 1)}),
            self.tile({0: self.down(4 * run + 3), 7: self.up(6 * run + 2)}),
        )

    def h_before(self, run):
        return tuple(self.tile({7: self.up(6 * run + 3 + c)}) for c in range(3))

    def coef(self):
        return DT * self.tile({0: self.down(8), 7: self.up(12)})


def ring(own, tile):
    return jnp.concatenate([own, tile], axis=0)


def rings(own, tiles):
    return tuple(ring(own[c], tiles[c]) for c in range(3))


def rows_up(amp, e_refs, h_refs, inv, drives, out):
    coef = DT * inv[:, 7, :]
    singles = []
    for run in range(2):
        e, e_in = ([e_refs[run][c, :, r, :] for c in range(3)] for r in (7, 6))
        h, h_in = ([h_refs[run][c, :, r, :] for c in range(3)] for r in (7, 6))
        hx_in = h_in[0] - DT * ((e[2] - e_in[2]) - plus_z(e_in[1]))
        hz_in = h_in[2] - DT * (plus_x(e_in[1]) - (e[0] - e_in[0]))
        out[6 * run] = e[0] - coef * hz_in
        out[6 * run + 1] = e[1]
        out[6 * run + 2] = e[2] + coef * (hx_in - amp[run] * drives[run][:, 7, :])
        out[6 * run + 3] = h[0] + DT * (e[2] + plus_z(e[1]))
        out[6 * run + 4] = h[1] - DT * (plus_z(e[0]) - plus_x(e[2]))
        out[6 * run + 5] = h[2] - DT * (plus_x(e[1]) + e[0])
        singles += [e[2], e_in[1]]
    out[12] = inv[:, 7, :]
    rows = rows_iota((CX, NZ))
    held = singles[0]
    for k in range(1, 4):
        held = jnp.where(rows == k, pltpu.roll(singles[k], k, 0), held)
    out[13] = held


def rows_down(amp, e_refs, h_refs, inv, drives, out):
    coef = DT * inv[:, 0, :]
    singles, others = [], []
    for run in range(2):
        e, e_in = ([e_refs[run][c, :, r, :] for c in range(3)] for r in (0, 1))
        h = [h_refs[run][c, :, 0, :] for c in range(3)]
        hx = h[0] - DT * ((e_in[2] - e[2]) - plus_z(e[1]))
        hy = h[1] - DT * (plus_z(e[0]) - plus_x(e[2]))
        hz = h[2] - DT * (plus_x(e[1]) - (e_in[0] - e[0]))
        out[4 * run] = e[0]
        out[4 * run + 1] = e[2]
        out[4 * run + 2] = e[0] + coef * (hz - minus_z(hy))
        out[4 * run + 3] = e[2] + coef * (minus_x(hy) - hx - amp[run] * drives[run][:, 0, :])
        singles.append(e[1])
        others.append(hy)
    out[8] = inv[:, 0, :]
    rows = rows_iota((CX, NZ))
    held = singles[0]
    for k, (value, by) in enumerate([(singles[1], 1), (others[0], 3), (others[1], 4)], 1):
        held = jnp.where(rows == k, pltpu.roll(value, by, 0), held)
    out[9] = held


def pack_kernel(step_index, e_f, h_f, e_a, h_a, inv, src, adj, far_up, far_down, *scratch):
    sources = (e_f, h_f, e_a, h_a, inv, src, adj)
    places, (up, down, sems, out_sems) = scratch[:7], scratch[7:]
    stores = [pltpu.make_async_copy(up, far_up, out_sems.at[0]), pltpu.make_async_copy(down, far_down, out_sems.at[1])]

    def load(a, side):
        at = pl.ds(24 if side == 0 else 0, 8)
        source = sources[a].at[:, :, at] if a < 4 else sources[a].at[:, at]
        return pltpu.make_async_copy(source, places[a].at[side], sems.at[a, side])

    for side in range(2):
        for a in range(7):
            load(a, side).start()
    amp = [amplitude(step_index, ticks, CX) for ticks in (1, -1)]
    for side, (rows_of, out) in enumerate([(rows_up, up), (rows_down, down)]):
        for a in range(7):
            load(a, side).wait()
        ef, hf, ea, ha, coef, drive_f, drive_a = (place.at[side] for place in places)
        rows_of(amp, (ef, ea), (hf, ha), coef, (drive_f, drive_a), out)
        stores[side].start()
    for copy in stores:
        copy.wait()


def pack_rows(step_index, arrays):
    hbm = pl.BlockSpec(memory_space=pl.ANY)
    shapes = [(UP, CX, NZ), (DOWN, CX, NZ)]
    return pl.pallas_call(
        pack_kernel,
        in_specs=[pl.BlockSpec(memory_space=pltpu.SMEM)] + [hbm] * 7,
        out_specs=[hbm] * 2,
        out_shape=[jax.ShapeDtypeStruct(s, F32) for s in shapes],
        scratch_shapes=[pltpu.VMEM((2, 3, CX, 8, NZ), F32)] * 4
        + [pltpu.VMEM((2, CX, 8, NZ), F32)] * 3
        + [pltpu.VMEM(s, F32) for s in shapes]
        + [pltpu.SemaphoreType.DMA((7, 2)), pltpu.SemaphoreType.DMA((2,))],
        compiler_params=pltpu.CompilerParams(vmem_limit_bytes=VMEM_BYTES),
        cost_estimate=pl.CostEstimate(flops=4 * 10**9, bytes_accessed=0, transcendentals=0),
        name="pack_rows",
    )(step_index, *arrays)


def touch_kernel(*refs):
    refs[-1][...] = refs[4][0, :8, :128]


def touch(arrays):
    whole = pl.BlockSpec(memory_space=pltpu.VMEM)
    return pl.pallas_call(
        touch_kernel,
        in_specs=[whole] * 7,
        out_specs=whole,
        out_shape=jax.ShapeDtypeStruct((8, 128), F32),
        compiler_params=pltpu.CompilerParams(vmem_limit_bytes=TOUCH_BYTES),
        cost_estimate=pl.CostEstimate(flops=6 * 10**9, bytes_accessed=0, transcendentals=0),
        name="touch",
    )(*arrays)


def write_layers(out, values):
    rows = rows_iota((8, NZ))
    for k, value in enumerate(values):
        out[pl.ds(CY * k, CY), :] = value[:CY]
    for k in range(0, 9, 2):
        tile = pltpu.roll(values[k][CY:], 2, 0)
        if k < 8:
            tile = jnp.where(rows < 4, tile, pltpu.roll(values[k + 1][CY:], 6, 0))
        out[pl.ds(9 * CY + 4 * k, 8), :] = tile


def read_layer(ref, k):
    tile = ref[pl.ds(9 * CY + 8 * (k // 2), 8), :]
    return ring(ref[pl.ds(CY * k, CY), :], pltpu.roll(tile, 2 if k % 2 else 6, 0))


def call_edges(kernel, name, step_index, arrays, messages, shapes):
    whole = pl.BlockSpec(memory_space=pltpu.VMEM)

    def body(step_index, *refs):
        sides = []
        for side in range(2):
            at = pl.ds(side * (CX - 2), 2)
            sides += [refs[a].at[:, at] if a < 4 else refs[a].at[at] for a in range(7)]
        kernel(step_index, *sides, *refs[7:9], *refs[10:])

    return pl.pallas_call(
        body,
        in_specs=[pl.BlockSpec(memory_space=pltpu.SMEM)] + [whole] * (7 + len(messages)),
        out_specs=[whole] * len(shapes),
        out_shape=[jax.ShapeDtypeStruct(s, F32) for s in shapes],
        compiler_params=pltpu.CompilerParams(vmem_limit_bytes=EDGE_BYTES),
        cost_estimate=pl.CostEstimate(flops=3 * 10**9, bytes_accessed=0, transcendentals=0),
        name=name,
    )(step_index, *arrays, *messages)


def edge_kernel(step_index, e_f0, h_f0, e_a0, h_a0, inv0, src0, adj0, e_f1, h_f1, e_a1, h_a1, inv1, src1, adj1, above, below, out_prev, out_next, keep):
    row_dt = ring_steps()
    ghosts = {x: Ghosts(above, below, x) for x in (0, 1, CX - 2, CX - 1)}
    still = jnp.zeros((8, NZ), F32)
    amp = [amplitude(step_index, ticks, CY) for ticks in (1, -1)]

    def before(ref, at, run, x):
        return rings([ref[c, at] for c in range(3)], ghosts[x].e_before(run))

    def middle(ref, at, run, x):
        return rings([ref[c, at] for c in range(3)], ghosts[x].e_middle(run))

    def magnet(ref, at, run, x):
        return rings([ref[c, at] for c in range(3)], ghosts[x].h_before(run))

    coef_first = ring(DT * inv0[0], ghosts[0].coef())
    coef_last = ring(DT * inv1[1], ghosts[CX - 1].coef())
    to_prev, to_next = [None] * 9, [None] * 9
    to_prev[8] = coef_first
    to_next[8] = coef_last
    for run, (e0, h0, s0, e1, h1, s1) in enumerate(
        [(e_f0, h_f0, src0, e_f1, h_f1, src1), (e_a0, h_a0, adj0, e_a1, h_a1, adj1)]
    ):
        near = ghosts[0]
        h = magnetic(before(e0, 0, run, 0), before(e0, 1, run, 1), magnet(h0, 0, run, 0), row_dt)
        drive = ring(amp[run] * s0[0], still)
        new = electric(middle(e0, 0, run, 0), h, None, coef_first, drive)
        sides_y = {0: near.down(9, run), 6: near.up(13, 2 * run + 1), 7: near.up(6 * run + 1)}
        sides_z = {0: near.down(4 * run + 1), 7: near.up(13, 2 * run)}
        to_prev[4 * run] = ring(e0[1, 0], near.tile(sides_y))
        to_prev[4 * run + 1] = ring(e0[2, 0], near.tile(sides_z))
        to_prev[4 * run + 2] = new[1]
        to_prev[4 * run + 3] = new[2]
        keep[4 * run] = new[0][:CY]
        e, back = before(e1, 1, run, CX - 1), before(e1, 0, run, CX - 2)
        h = magnetic(e, None, magnet(h1, 1, run, CX - 1), row_dt)
        h_back = magnetic(back, e, magnet(h1, 0, run, CX - 2), row_dt)
        drive = ring(amp[run] * s1[1], still)
        new = electric(middle(e1, 1, run, CX - 1), h, h_back, coef_last, drive)
        later = magnetic(new, None, h, row_dt)
        beyond = ghosts[CX - 1].down(9, 2 + run)
        to_next[4 * run] = jnp.where(rows_iota((RING, NZ)) == CY, beyond, h[1])
        to_next[4 * run + 1] = h[2]
        to_next[4 * run + 2] = later[1]
        to_next[4 * run + 3] = later[2]
        for c in range(3):
            keep[4 * run + 1 + c] = new[c][:CY]
    write_layers(out_prev, to_prev)
    write_layers(out_next, to_next)


def solve_edges(step_index, arrays, above, below, touched):
    shapes = [(9 * CY + 40, NZ), (9 * CY + 40, NZ), (8, CY, NZ)]
    return call_edges(edge_kernel, "solve_edges", step_index, arrays, [above, below, touched], shapes)


CHUNK = 2
DRAIN = 4


def zplus(tile):
    moved = pltpu.roll(tile, NZ - 1, 1)
    last = jnp.where(lanes_iota((8, 128)) == 127, 0.0, moved[:, NZ - 128 :])
    return jnp.concatenate([moved[:, : NZ - 128], last], axis=1) - tile


def zminus(tile):
    moved = pltpu.roll(tile, 1, 1)
    first = jnp.where(lanes_iota((8, 128)) == 0, 0.0, moved[:, :128])
    return tile - jnp.concatenate([first, moved[:, 128:]], axis=1)


def magnetic_tiles(tiles, e, e_next, h, row_dts, put, closed):
    end = rows_iota((8, NZ)) == 7
    firsts = {c: pltpu.roll(e(c, 0), 7, 0) for c in (0, 2)}
    here = firsts
    for t in range(tiles):
        if t == tiles - 1:
            after = {c: jnp.zeros((8, NZ), F32) for c in (0, 2)} if closed else firsts
        else:
            after = {c: pltpu.roll(e(c, t + 1), 7, 0) for c in (0, 2)}
        ex, ey, ez = (e(c, t) for c in range(3))
        put(0, t, h(0, t) - row_dts[t] * ((jnp.where(end, after[2], here[2]) - ez) - zplus(ey)))
        put(1, t, h(1, t) - row_dts[t] * (zplus(ex) - (e_next(2, t) - ez)))
        put(2, t, h(2, t) - row_dts[t] * ((e_next(1, t) - ey) - (jnp.where(end, after[0], here[0]) - ex)))
        here = after


def electric_tile(e, h, h_prev, coef, drive, t, rolled):
    start = rows_iota((8, NZ)) == 0
    hx, hy, hz = (h(c, t) for c in range(3))
    moved = {0: pltpu.roll(hx, 1, 0), 2: pltpu.roll(hz, 1, 0)}
    new_x = e(0, t) + coef * ((hz - jnp.where(start, rolled[2], moved[2])) - zminus(hy))
    new_y = e(1, t) + coef * (zminus(hx) - (hz - h_prev(2, t)))
    curl = (hy - h_prev(1, t)) - (hx - jnp.where(start, rolled[0], moved[0]))
    new_z = e(2, t) + coef * (curl if drive is None else curl - drive)
    return (new_x, new_y, new_z), moved


def sweep(step_index, places, store, mid_h, mid_e, late_h, tiles, at_rows, ghosts, put_last):
    v_ef, v_hf, v_ea, v_ha, v_inv, v_src, v_adj = places
    own = [t for t in range(tiles) if at_rows[t] is not None]
    closed = len(own) == tiles
    mid_h[...] = jnp.zeros_like(mid_h)
    late_h[...] = jnp.zeros_like(late_h)
    ghost_dt = None if closed else ring_steps()[CY:]
    row_dts = [DT if t in own else ghost_dt for t in range(tiles)]
    amp = [[amplitude(step_index, ticks, 8) for ticks in pair] for pair in ((1, 2), (-1, -2))]
    runs = ((v_ef, v_hf, v_src), (v_ea, v_ha, v_adj))
    nothing = {c: jnp.zeros((8, NZ), F32) for c in (0, 2)}

    def rows(t):
        return pl.ds(at_rows[t], 8)

    def ring_rows(t):
        return pl.ds(8 * t, 8)

    def one(step, carry):
        now, then = lax.rem(step, 2), lax.rem(step + 1, 2)

        @pl.when(step <= CX)
        def _():
            x = step - 1
            inside, x_next = step < CX, jnp.minimum(step, CX - 1)
            if not closed:
                here, there = ghosts(x), ghosts(jnp.minimum(step, CX - 1))
                coef_ghost = here.coef()
            for run, (e_ref, h_ref, s_ref) in enumerate(runs):
                beside = beside_next = beside_h = middle = None
                if not closed:
                    beside = here.e_before(run)
                    beside_next = [jnp.where(inside, v, 0.0) for v in there.e_before(run)]
                    beside_h = here.h_before(run)
                    middle = here.e_middle(run)

                def put_h(c, t, value):
                    mid_h[now, 3 * run + c, ring_rows(t), :] = value

                magnetic_tiles(
                    tiles,
                    lambda c, t: e_ref[c, x, rows(t), :] if t in own else beside[c],
                    lambda c, t: jnp.where(inside, e_ref[c, x_next, rows(t), :], 0.0) if t in own else beside_next[c],
                    lambda c, t: h_ref[c, x, rows(t), :] if t in own else beside_h[c],
                    row_dts,
                    put_h,
                    closed,
                )
                rolled = nothing
                if not closed:
                    end = ring_rows(tiles - 1)
                    rolled = {c: pltpu.roll(mid_h[now, 3 * run + c, end, :], 1, 0) for c in (0, 2)}
                for t in range(tiles):
                    if t in own:
                        coef, drive = DT * v_inv[x, rows(t), :], amp[run][0] * s_ref[x, rows(t), :]
                    else:
                        coef, drive = coef_ghost, None
                    new, rolled = electric_tile(
                        lambda c, t: e_ref[c, x, rows(t), :] if t in own else middle[c],
                        lambda c, t: mid_h[now, 3 * run + c, ring_rows(t), :],
                        lambda c, t: mid_h[then, 3 * run + c, ring_rows(t), :],
                        coef,
                        drive,
                        t,
                        rolled,
                    )
                    for c in range(3):
                        mid_e[now, 3 * run + c, ring_rows(t), :] = new[c]

        @pl.when(step > CX)
        def _():
            mid_e[now] = jnp.zeros((6, 8 * tiles, NZ), F32)

        @pl.when(step > 1)
        def _():
            x = step - 2
            rolled = [nothing, nothing]
            for run in range(2):

                def put_late(c, t, value):
                    late_h[now, 3 * run + c, ring_rows(t), :] = value

                magnetic_tiles(
                    tiles,
                    lambda c, t: mid_e[then, 3 * run + c, ring_rows(t), :],
                    lambda c, t: mid_e[now, 3 * run + c, ring_rows(t), :],
                    lambda c, t: mid_h[then, 3 * run + c, ring_rows(t), :],
                    row_dts,
                    put_late,
                    closed,
                )
            for t in range(tiles):
                if t not in own:
                    rolled = [
                        {c: pltpu.roll(late_h[now, 3 * run + c, ring_rows(t), :], 1, 0) for c in (0, 2)}
                        for run in range(2)
                    ]
                    continue
                coef = DT * v_inv[x, rows(t), :]
                new = [None, None]
                for run, (e_ref, _, s_ref) in enumerate(runs):
                    new[run], rolled[run] = electric_tile(
                        lambda c, t: mid_e[then, 3 * run + c, ring_rows(t), :],
                        lambda c, t: late_h[now, 3 * run + c, ring_rows(t), :],
                        lambda c, t: late_h[then, 3 * run + c, ring_rows(t), :],
                        coef,
                        amp[run][1] * s_ref[x, rows(t), :],
                        t,
                        rolled[run],
                    )
                first = [[mid_e[then, 3 * run + c, ring_rows(t), :] for c in range(3)] for run in range(2)]
                put_last(x, t, new, DT * (dot_three(*first) + dot_three(*new)))

        @pl.when((step > 2) & (step % DRAIN == 1))
        def _():
            for a in range(2):
                store(a, step // DRAIN - 1).start()

        return carry

    lax.fori_loop(1, CX + 2, one, 0)
    for part in range(CX // DRAIN):
        for a in range(2):
            store(a, part).wait()


def main_kernel(
    step_index, e_f, h_f, e_a, h_a, inv, src, adj, above, below, out_f, out_a, grad,
    last_f, last_a, mid_h, mid_e, late_h, store_sem,
):
    def store(a, part):
        at = pl.ds(part * DRAIN, DRAIN)
        return pltpu.make_async_copy((last_f, last_a)[a].at[:, at], (out_f, out_a)[a].at[:, at], store_sem.at[a, part])

    def put_last(x, t, new, product):
        for c in range(3):
            last_f[c, x, pl.ds(8 * t - 8, 8), :] = new[0][c]
            last_a[c, x, pl.ds(8 * t - 8, 8), :] = new[1][c]
        grad[x, pl.ds(8 * t - 8, 8), :] = product

    sweep(
        step_index, (e_f, h_f, e_a, h_a, inv, src, adj), store, mid_h, mid_e, late_h, 5, [None, 0, 8, 16, 24],
        lambda x: Ghosts(above, below, x), put_last,
    )


def solve_main(step_index, arrays, above, below):
    free, whole = pl.BlockSpec(memory_space=pl.ANY), pl.BlockSpec(memory_space=pltpu.VMEM)
    field, cells = (3, CX, CY, NZ), (CX, CY, NZ)
    return pl.pallas_call(
        main_kernel,
        in_specs=[pl.BlockSpec(memory_space=pltpu.SMEM)] + [whole] * 9,
        out_specs=[free, free, whole],
        out_shape=[jax.ShapeDtypeStruct(s, F32) for s in (field, field, cells)],
        scratch_shapes=[pltpu.VMEM(field, F32)] * 2
        + [pltpu.VMEM((2, 6, RING, NZ), F32)] * 3
        + [pltpu.SemaphoreType.DMA((2, CX // DRAIN))],
        compiler_params=pltpu.CompilerParams(vmem_limit_bytes=MAIN_BYTES),
        cost_estimate=pl.CostEstimate(flops=14 * 10**9, bytes_accessed=0, transcendentals=0),
        name="solve_main",
    )(step_index, *arrays, above, below)


def split(value):
    high = value.astype(jnp.bfloat16)
    return high, (value - high.astype(F32)).astype(jnp.bfloat16)


def exact_dot(a, b, dims):
    high, low = split(b)
    a = a.astype(jnp.bfloat16)
    return lax.dot_general(a, high, dims, preferred_element_type=F32) + lax.dot_general(
        a, low, dims, preferred_element_type=F32
    )


def correct_prev(run, from_prev, own, row_dt, present):
    e0y, e0z, e1y, e1z = (own[4 * run + k] for k in range(4))
    coef, ghost_coef = own[8], jnp.where(present, from_prev[8], 0.0)
    h1y, h1z, h2y, h2z = (from_prev[4 * run + k] for k in range(4))
    d_h1y, d_h1z = DT * e0z, -DT * e0y
    h1y = jnp.where(present, h1y + d_h1y, 0.0)
    h1z = jnp.where(present, h1z + d_h1z, 0.0)
    d_e1y, d_e1z = coef * h1z, -coef * h1y
    g_e1x = ghost_coef * (minus_y(d_h1z) - minus_z(d_h1y))
    g_e1y, g_e1z = -ghost_coef * d_h1z, ghost_coef * d_h1y
    h2y = jnp.where(present, h2y + d_h1y - DT * (plus_z(g_e1x) - (e1z + d_e1z - g_e1z)), 0.0)
    h2z = jnp.where(present, h2z + d_h1z - DT * ((e1y + d_e1y - g_e1y) - plus_y(g_e1x)), 0.0)
    d_h2x = -row_dt * (plus_y(d_e1z) - plus_z(d_e1y))
    d_h2y, d_h2z = -row_dt * d_e1z, row_dt * d_e1y
    first = (None, d_e1y, d_e1z)
    last = (
        coef * (minus_y(d_h2z) - minus_z(d_h2y)),
        d_e1y + coef * (minus_z(d_h2x) - d_h2z + h2z),
        d_e1z + coef * (d_h2y - h2y - minus_y(d_h2x)),
    )
    return first, last, d_h2y, d_h2z


def correct_next(run, from_next, own, row_dt, present):
    e0y, e0z, e1y, e1z = (jnp.where(present, from_next[4 * run + k], 0.0) for k in range(4))
    coef, ghost_coef = own[8], jnp.where(present, from_next[8], 0.0)
    h1y, h1z = own[4 * run], own[4 * run + 1]
    d_h1y, d_h1z = DT * e0z, -DT * e0y
    d_e1x = coef * (minus_y(d_h1z) - minus_z(d_h1y))
    d_e1y, d_e1z = -coef * d_h1z, coef * d_h1y
    e1y = e1y + ghost_coef * (h1z + d_h1z)
    e1z = e1z - ghost_coef * (h1y + d_h1y)
    d_h2x = -row_dt * (plus_y(d_e1z) - plus_z(d_e1y))
    d_h2y = d_h1y - row_dt * (plus_z(d_e1x) - (e1z - d_e1z))
    d_h2z = d_h1z - row_dt * ((e1y - d_e1y) - plus_y(d_e1x))
    b_h2y, b_h2z = row_dt * d_e1z, -row_dt * d_e1y
    first = (d_e1x, d_e1y, d_e1z)
    last = (
        d_e1x + coef * (minus_y(d_h2z) - minus_z(d_h2y)),
        d_e1y + coef * (minus_z(d_h2x) - d_h2z + b_h2z),
        d_e1z + coef * (d_h2y - b_h2y - minus_y(d_h2x)),
    )
    return first, last, b_h2y, b_h2z


def put_cells(chosen, values, rows_out, q):
    devices = rows_out.shape[0]
    cells = exact_dot(chosen[...], values.reshape(4 * CY, NZ), (((1,), (1,)), ((), ())))
    for part in range(BZ):
        at = part * CX * CY + q * 4 * CY
        rows_out[:, 0, at : at + 4 * CY] = cells[part * devices : (part + 1) * devices]


def inner_kernel(mask, param, grad, rows_out, chosen):
    devices = rows_out.shape[0]
    lanes = lanes_iota((devices, NZ))
    blocks = lax.broadcasted_iota(jnp.int32, (NZ // BZ, NZ), 0)
    spread = (blocks == lanes_iota((NZ // BZ, NZ)) // BZ).astype(jnp.bfloat16)
    owned = NZ // BZ // 2
    owner = jnp.where(mask[0] == 1, param[0] // owned, -1).astype(F32)
    slot = (param[0] & (owned - 1)).astype(F32)
    numbers = jnp.concatenate([owner, slot, jnp.zeros((14, NZ // BZ), F32)], axis=0)
    numbers = jnp.dot(numbers.astype(jnp.bfloat16), spread, preferred_element_type=F32)
    mine = numbers[0:1, :] == rows_iota((devices, NZ)).astype(F32)
    for part in range(BZ):
        chosen[pl.ds(part * devices, devices), :] = jnp.where(mine & (lanes % BZ == part), 1.0, 0.0).astype(jnp.bfloat16)
    found = jnp.sum(jnp.where(mine & (lanes % BZ == 0), numbers[1:2, :] + 1.0, 0.0), axis=1, keepdims=True) - 1.0
    rows_out[:, 0, BZ * CX * CY :] = jnp.broadcast_to(found, (devices, 128))

    for q in (1, 2):
        put_cells(chosen, grad[pl.ds(4 * q, 4)], rows_out, q)


def pack_inner(mask, param, grad, devices):
    whole = pl.BlockSpec(memory_space=pltpu.VMEM)
    return pl.pallas_call(
        inner_kernel,
        in_specs=[whole] * 3,
        out_specs=[whole] * 2,
        out_shape=[
            jax.ShapeDtypeStruct((devices, 1, BZ * CX * CY + 128), F32),
            jax.ShapeDtypeStruct((BZ * devices, NZ), jnp.bfloat16),
        ],
        compiler_params=pltpu.CompilerParams(vmem_limit_bytes=PACK_BYTES),
        cost_estimate=pl.CostEstimate(flops=2 * 10**9, bytes_accessed=0, transcendentals=0),
        name="pack_inner",
    )(mask, param, grad)


def correct_kernel(
    chosen, *refs
):
    far, refs = refs[:5], refs[5:]
    far_inv, far_grad, old_f, old_a, _, out_f, out_a, far_rows, *refs = refs
    near, refs = refs[:5], refs[5:]
    (
    v_inv, work, v_f, v_a, rows_out,
    message_sem, inv_sem, grad_sem, field_sem, store_sem, rows_sem,
    ) = refs
    ref_from_prev, ref_to_prev, keep, ref_from_next, ref_to_next = near
    place = lax.axis_index("gx")
    has_prev, has_next = place > 0, place < lax.axis_size("gx") - 1
    row_dt = row_steps()
    messages = [pltpu.make_async_copy(a, b, message_sem.at[k]) for k, (a, b) in enumerate(zip(far, near))]
    grads = [
        pltpu.make_async_copy(far_grad.at[pl.ds(4 * q, 4)], work.at[pl.ds(4 * q, 4)], grad_sem.at[q]) for q in (0, 3)
    ]
    ends, stores = [], []
    for side in range(2):
        at = pl.ds(side * (CX - 2), 2)
        ends.append(
            [
                pltpu.make_async_copy(far_inv.at[at], v_inv.at[side], inv_sem.at[side]),
                pltpu.make_async_copy(old_f.at[:, at], v_f.at[side], field_sem.at[0, side]),
                pltpu.make_async_copy(old_a.at[:, at], v_a.at[side], field_sem.at[1, side]),
            ]
        )
        stores.append(
            [
                pltpu.make_async_copy(v_f.at[side], out_f.at[:, at], store_sem.at[0, side]),
                pltpu.make_async_copy(v_a.at[side], out_a.at[:, at], store_sem.at[1, side]),
            ]
        )
    for copy in [*messages[:3], *ends[0], grads[0], *messages[3:], *ends[1], grads[1]]:
        copy.start()

    def finish(side, edge_at, inner_at, firsts, lasts, d_inner, inner_coef, base_first):
        total_f, total_a, inner_f, inner_a = [], [], [], []
        fields_f, fields_a = v_f.at[side], v_a.at[side]
        before = jnp.zeros((CY, NZ), F32)
        for c in range(3):
            before = before + fields_f[c, inner_at] * fields_a[c, inner_at]
        for run, (ref, total, inner) in enumerate([(fields_f, total_f, inner_f), (fields_a, total_a, inner_a)]):
            for c in range(3):
                total.append(ref[c, edge_at] + lasts[run][c][:CY])
                ref[c, edge_at] = total[c]
                add = d_inner[run][c]
                inner.append(ref[c, inner_at] if add is None else ref[c, inner_at] + inner_coef * add[:CY])
                ref[c, inner_at] = inner[c]
        e1 = [
            [base_first[run][c] if firsts[run][c] is None else base_first[run][c] + firsts[run][c][:CY] for c in range(3)]
            for run in range(2)
        ]
        edge_grad = DT * (dot_three(e1[0], e1[1]) + dot_three(total_f, total_a))
        inner_change = DT * (dot_three(inner_f, inner_a) - before)
        return edge_grad, inner_change

    def first_edge():
        firsts, lasts, d_inner, base = [], [], [], []
        from_prev, to_prev = ([read_layer(ref, k) for k in range(9)] for ref in (ref_from_prev, ref_to_prev))
        for run in range(2):
            first, last, d_h2y, d_h2z = correct_prev(run, from_prev, to_prev, row_dt, has_prev)
            firsts.append(first)
            lasts.append(last)
            d_inner.append((None, d_h2z, -d_h2y))
            base.append((keep[4 * run], to_prev[4 * run + 2][:CY], to_prev[4 * run + 3][:CY]))
        edge, inner = finish(0, 0, 1, firsts, lasts, d_inner, DT * v_inv[0, 1], base)
        work[0] = edge
        work[1] = work[1] + inner

    def last_edge():
        firsts, lasts, d_inner, base = [], [], [], []
        from_next = [read_layer(ref_from_next, k) for k in range(9)]
        to_next = {k: read_layer(ref_to_next, k) for k in (0, 1, 4, 5, 8)}
        for run in range(2):
            first, last, b_h2y, b_h2z = correct_next(run, from_next, to_next, row_dt, has_next)
            firsts.append(first)
            lasts.append(last)
            d_inner.append((minus_y(b_h2z) - minus_z(b_h2y), -b_h2z, b_h2y))
            base.append(tuple(keep[4 * run + 1 + c] for c in range(3)))
        edge, inner = finish(1, 1, 0, firsts, lasts, d_inner, DT * v_inv[1, 0], base)
        work[CX - 1] = edge
        work[CX - 2] = work[CX - 2] + inner

    row_copies = []

    def pack(q):
        put_cells(chosen, work[pl.ds(4 * q, 4)], rows_out, q)
        for part in range(BZ):
            columns = pl.ds(part * CX * CY + q * 4 * CY, 4 * CY)
            row_copies.append(
                pltpu.make_async_copy(rows_out.at[:, :, columns], far_rows.at[:, :, columns], rows_sem.at[q, part])
            )
            row_copies[-1].start()

    for copy in [*messages[:3], *ends[0], grads[0]]:
        copy.wait()
    first_edge()
    for copy in stores[0]:
        copy.start()
    pack(0)
    for copy in [*messages[3:], *ends[1], grads[1]]:
        copy.wait()
    last_edge()
    for copy in stores[1]:
        copy.start()
    pack(3)
    for copy in [*stores[0], *stores[1], *row_copies]:
        copy.wait()


def correct_and_pack(chosen, messages, inv, grad, fields_f, fields_a, rows):
    free, whole = pl.BlockSpec(memory_space=pl.ANY), pl.BlockSpec(memory_space=pltpu.VMEM)
    vmem = lambda shape: pltpu.VMEM(shape, F32)
    return pl.pallas_call(
        correct_kernel,
        in_specs=[whole] + [free] * 10,
        out_specs=[free] * 3,
        out_shape=[
            jax.ShapeDtypeStruct((3, CX, CY, NZ), F32),
            jax.ShapeDtypeStruct((3, CX, CY, NZ), F32),
            jax.ShapeDtypeStruct(rows.shape, F32),
        ],
        scratch_shapes=[vmem(m.shape) for m in messages]
        + [vmem((2, 2, CY, NZ)), vmem((CX, CY, NZ))]
        + [vmem((2, 3, 2, CY, NZ))] * 2
        + [vmem(rows.shape)]
        + [pltpu.SemaphoreType.DMA(s) for s in ((5,), (2,), (4,), (2, 2), (2, 2), (4, BZ))],
        input_output_aliases={8: 0, 9: 1, 10: 2},
        compiler_params=pltpu.CompilerParams(vmem_limit_bytes=PACK_BYTES),
        cost_estimate=pl.CostEstimate(flops=6 * 10**9, bytes_accessed=0, transcendentals=0),
        name="correct_and_pack",
    )(chosen, *messages, inv, grad, fields_f, fields_a, rows)


def place_kernel(got, out):
    devices = got.shape[0]
    owned = out.shape[0]
    cells = BZ * CX * CY
    numbers = got[:, 0, cells:]
    wanted = (numbers == lanes_iota((devices, 128)).astype(F32)).astype(F32)
    placing = jnp.transpose(wanted)[:owned]
    order_from = rows_iota((4 * 128, 4 * 128))
    order_to = lanes_iota((4 * 128, 4 * 128))
    order = (order_from == (order_to % BZ) * 128 + order_to // BZ).astype(jnp.bfloat16)
    dims = (((1,), (0,)), ((), ()))
    for q in range(4):
        parts = [got[:, 0, part * CX * CY + q * 128 : part * CX * CY + (q + 1) * 128] for part in range(BZ)]
        rows = exact_dot(placing, jnp.concatenate(parts, axis=1), dims)
        high, low = split(rows)
        out[:, q * 512 : (q + 1) * 512] = lax.dot_general(
            high, order, dims, preferred_element_type=F32
        ) + lax.dot_general(low, order, dims, preferred_element_type=F32)


def place_rows(got, owned):
    return pl.pallas_call(
        place_kernel,
        out_shape=jax.ShapeDtypeStruct((owned, BZ * CX * CY), F32),
        compiler_params=pltpu.CompilerParams(vmem_limit_bytes=32 << 20),
        cost_estimate=pl.CostEstimate(flops=2 * 10**9, bytes_accessed=0, transcendentals=0),
        name="place_rows",
    )(got)


def body(e_forward, h_forward, e_adjoint, h_adjoint, inv_eps, source, adj_source, design_mask, param_map, step_index):
    arrays = (e_forward, h_forward, e_adjoint, h_adjoint, inv_eps, source, adj_source)
    devices = lax.axis_size("gx") * lax.axis_size("gy")
    blocks = NZ // BZ
    owned = blocks // 2
    up, down = pack_rows(step_index, arrays)
    above, below = cycled(up, "gy", 1), cycled(down, "gy", -1)
    touched = touch(arrays)
    to_prev, to_next, keep = solve_edges(step_index, arrays, above, below, touched)
    from_next, from_prev = cycled(to_prev, "gx", -1), cycled(to_next, "gx", 1)
    fields_f, fields_a, grad = solve_main(step_index, arrays, above, below)
    messages = (from_prev, to_prev, keep, from_next, to_next)
    rows, chosen = pack_inner(design_mask, param_map, grad, devices)
    fields_f, fields_a, rows = correct_and_pack(chosen, messages, inv_eps, grad, fields_f, fields_a, rows)
    got = lax.all_to_all(rows, ("gx", "gy"), split_axis=0, concat_axis=0, tiled=True)
    return place_rows(got, owned), fields_f, fields_a


def solution(mesh):
    field, cells = P(None, "gx", "gy", None), P("gx", "gy", None)
    in_specs = (field, field, field, field, cells, cells, cells, cells, cells, P())
    out_specs = (P(("gx", "gy"), None), field, field)
    return jax.shard_map(body, mesh=mesh, in_specs=in_specs, out_specs=out_specs, check_vma=False)
```

```python
import functools
import math

import jax
import jax.numpy as jnp
from jax import lax
from jax.experimental import pallas as pl
from jax.experimental.pallas import tpu as pltpu
from jax.sharding import PartitionSpec as P

BZ = 4
STEPS = 2
DT = 0.5
PERIOD = 20
RATE = 2.0 * math.pi / 20.0
CX, CY, NZ = 16, 32, 512
RING = 40
F32 = jnp.float32
VMEM_BYTES = (64 << 20) - (128 << 10)
TOUCH_BYTES, EDGE_BYTES, MAIN_BYTES, PACK_BYTES = 24 << 20, 24 << 20, 24 << 20, 32 << 20

UP, DOWN = 14, 10


def cycled(value, axis, by):
    devices = lax.axis_size(axis)
    return lax.ppermute(value, axis, [(i, (i + by) % devices) for i in range(devices)])


def rows_iota(shape):
    return lax.broadcasted_iota(jnp.int32, shape, 0)


def lanes_iota(shape):
    return lax.broadcasted_iota(jnp.int32, shape, 1)


def plus_y(f):
    return pltpu.roll(f, f.shape[0] - 1, 0) - f


def minus_y(f):
    return f - pltpu.roll(f, 1, 0)


def plus_z(f):
    return jnp.where(lanes_iota(f.shape) == NZ - 1, 0.0, pltpu.roll(f, NZ - 1, 1)) - f


def minus_z(f):
    return f - jnp.where(lanes_iota(f.shape) == 0, 0.0, pltpu.roll(f, 1, 1))


def magnetic(e, e_next, h, row_dt):
    ahead_y = -e[1] if e_next is None else e_next[1] - e[1]
    ahead_z = -e[2] if e_next is None else e_next[2] - e[2]
    return (
        h[0] - row_dt * (plus_y(e[2]) - plus_z(e[1])),
        h[1] - row_dt * (plus_z(e[0]) - ahead_z),
        h[2] - row_dt * (ahead_y - plus_y(e[0])),
    )


def electric(e, h, h_prev, coef, drive):
    back_y = h[1] if h_prev is None else h[1] - h_prev[1]
    back_z = h[2] if h_prev is None else h[2] - h_prev[2]
    return (
        e[0] + coef * (minus_y(h[2]) - minus_z(h[1])),
        e[1] + coef * (minus_z(h[0]) - back_z),
        e[2] + coef * (back_y - minus_y(h[0]) - drive),
    )


def amplitude(step_index, ticks, rows):
    tick = lax.rem(step_index[0] + (PERIOD + ticks), PERIOD)
    tile = jnp.sin(RATE * jnp.full((8, 128), tick, jnp.int32).astype(F32))
    return jnp.concatenate([jnp.concatenate([tile] * (NZ // 128), axis=1)] * (rows // 8), axis=0)


def dot_three(a, b):
    return a[0] * b[0] + a[1] * b[1] + a[2] * b[2]


def plus_x(f):
    return jnp.where(rows_iota(f.shape) == f.shape[0] - 1, 0.0, pltpu.roll(f, f.shape[0] - 1, 0)) - f


def minus_x(f):
    return f - jnp.where(rows_iota(f.shape) == 0, 0.0, pltpu.roll(f, 1, 0))


def has_rows():
    place = lax.axis_index("gy")
    return place < lax.axis_size("gy") - 1, place > 0


def row_steps():
    _, has_above = has_rows()
    rows = rows_iota((8, NZ))
    tile = jnp.where((rows >= 6) & jnp.logical_not(has_above), 0.0, DT)
    return jnp.concatenate([jnp.full((CY, NZ), DT, F32), tile], axis=0)


def ring_steps():
    _, has_above = has_rows()
    tile = jnp.where((rows_iota((8, NZ)) == 7) & has_above, DT, 0.0)
    return jnp.concatenate([jnp.full((CY, NZ), DT, F32), tile], axis=0)


class Ghosts:
    def __init__(self, above, below, x):
        has_below, has_above = has_rows()
        self.refs = above, below
        self.flags = jnp.where(has_above, 1.0, 0.0).astype(F32), jnp.where(has_below, 1.0, 0.0).astype(F32)
        self.x = x

    def up(self, k, x=None):
        return self.refs[0][k, pl.ds(self.x if x is None else x, 1), :] * self.flags[0]

    def down(self, k, x=None):
        return self.refs[1][k, pl.ds(self.x if x is None else x, 1), :] * self.flags[1]

    def tile(self, rows):
        at = rows_iota((8, NZ))
        tile = jnp.zeros((8, NZ), F32)
        for row, value in rows.items():
            tile = jnp.where(at == row, value, tile)
        return tile

    def e_before(self, run):
        return (
            self.tile({0: self.down(4 * run)}),
            jnp.zeros((8, NZ), F32),
            self.tile({0: self.down(4 * run + 1)}),
        )

    def e_middle(self, run):
        return (
            self.tile({0: self.down(4 * run + 2), 7: self.up(6 * run)}),
            self.tile({7: self.up(6 * run + 1)}),
            self.tile({0: self.down(4 * run + 3), 7: self.up(6 * run + 2)}),
        )

    def h_before(self, run):
        return tuple(self.tile({7: self.up(6 * run + 3 + c)}) for c in range(3))

    def coef(self):
        return DT * self.tile({0: self.down(8), 7: self.up(12)})


def ring(own, tile):
    return jnp.concatenate([own, tile], axis=0)


def rings(own, tiles):
    return tuple(ring(own[c], tiles[c]) for c in range(3))


def rows_up(amp, e_refs, h_refs, inv, drives, out):
    coef = DT * inv[:, 7, :]
    singles = []
    for run in range(2):
        e, e_in = ([e_refs[run][c, :, r, :] for c in range(3)] for r in (7, 6))
        h, h_in = ([h_refs[run][c, :, r, :] for c in range(3)] for r in (7, 6))
        hx_in = h_in[0] - DT * ((e[2] - e_in[2]) - plus_z(e_in[1]))
        hz_in = h_in[2] - DT * (plus_x(e_in[1]) - (e[0] - e_in[0]))
        out[6 * run] = e[0] - coef * hz_in
        out[6 * run + 1] = e[1]
        out[6 * run + 2] = e[2] + coef * (hx_in - amp[run] * drives[run][:, 7, :])
        out[6 * run + 3] = h[0] + DT * (e[2] + plus_z(e[1]))
        out[6 * run + 4] = h[1] - DT * (plus_z(e[0]) - plus_x(e[2]))
        out[6 * run + 5] = h[2] - DT * (plus_x(e[1]) + e[0])
        singles += [e[2], e_in[1]]
    out[12] = inv[:, 7, :]
    rows = rows_iota((CX, NZ))
    held = singles[0]
    for k in range(1, 4):
        held = jnp.where(rows == k, pltpu.roll(singles[k], k, 0), held)
    out[13] = held


def rows_down(amp, e_refs, h_refs, inv, drives, out):
    coef = DT * inv[:, 0, :]
    singles, others = [], []
    for run in range(2):
        e, e_in = ([e_refs[run][c, :, r, :] for c in range(3)] for r in (0, 1))
        h = [h_refs[run][c, :, 0, :] for c in range(3)]
        hx = h[0] - DT * ((e_in[2] - e[2]) - plus_z(e[1]))
        hy = h[1] - DT * (plus_z(e[0]) - plus_x(e[2]))
        hz = h[2] - DT * (plus_x(e[1]) - (e_in[0] - e[0]))
        out[4 * run] = e[0]
        out[4 * run + 1] = e[2]
        out[4 * run + 2] = e[0] + coef * (hz - minus_z(hy))
        out[4 * run + 3] = e[2] + coef * (minus_x(hy) - hx - amp[run] * drives[run][:, 0, :])
        singles.append(e[1])
        others.append(hy)
    out[8] = inv[:, 0, :]
    rows = rows_iota((CX, NZ))
    held = singles[0]
    for k, (value, by) in enumerate([(singles[1], 1), (others[0], 3), (others[1], 4)], 1):
        held = jnp.where(rows == k, pltpu.roll(value, by, 0), held)
    out[9] = held


def pack_kernel(step_index, e_f, h_f, e_a, h_a, inv, src, adj, far_up, far_down, *scratch):
    sources = (e_f, h_f, e_a, h_a, inv, src, adj)
    places, (up, down, sems, out_sems) = scratch[:7], scratch[7:]
    stores = [pltpu.make_async_copy(up, far_up, out_sems.at[0]), pltpu.make_async_copy(down, far_down, out_sems.at[1])]

    def load(a, side):
        at = pl.ds(24 if side == 0 else 0, 8)
        source = sources[a].at[:, :, at] if a < 4 else sources[a].at[:, at]
        return pltpu.make_async_copy(source, places[a].at[side], sems.at[a, side])

    for side in range(2):
        for a in range(7):
            load(a, side).start()
    amp = [amplitude(step_index, ticks, CX) for ticks in (1, -1)]
    for side, (rows_of, out) in enumerate([(rows_up, up), (rows_down, down)]):
        for a in range(7):
            load(a, side).wait()
        ef, hf, ea, ha, coef, drive_f, drive_a = (place.at[side] for place in places)
        rows_of(amp, (ef, ea), (hf, ha), coef, (drive_f, drive_a), out)
        stores[side].start()
    for copy in stores:
        copy.wait()


def pack_rows(step_index, arrays):
    hbm = pl.BlockSpec(memory_space=pl.ANY)
    shapes = [(UP, CX, NZ), (DOWN, CX, NZ)]
    return pl.pallas_call(
        pack_kernel,
        in_specs=[pl.BlockSpec(memory_space=pltpu.SMEM)] + [hbm] * 7,
        out_specs=[hbm] * 2,
        out_shape=[jax.ShapeDtypeStruct(s, F32) for s in shapes],
        scratch_shapes=[pltpu.VMEM((2, 3, CX, 8, NZ), F32)] * 4
        + [pltpu.VMEM((2, CX, 8, NZ), F32)] * 3
        + [pltpu.VMEM(s, F32) for s in shapes]
        + [pltpu.SemaphoreType.DMA((7, 2)), pltpu.SemaphoreType.DMA((2,))],
        compiler_params=pltpu.CompilerParams(vmem_limit_bytes=VMEM_BYTES),
        cost_estimate=pl.CostEstimate(flops=4 * 10**9, bytes_accessed=0, transcendentals=0),
        name="pack_rows",
    )(step_index, *arrays)


def touch_kernel(*refs):
    refs[-1][...] = refs[4][0, :8, :128]


def touch(arrays):
    whole = pl.BlockSpec(memory_space=pltpu.VMEM)
    return pl.pallas_call(
        touch_kernel,
        in_specs=[whole] * 7,
        out_specs=whole,
        out_shape=jax.ShapeDtypeStruct((8, 128), F32),
        compiler_params=pltpu.CompilerParams(vmem_limit_bytes=TOUCH_BYTES),
        cost_estimate=pl.CostEstimate(flops=6 * 10**9, bytes_accessed=0, transcendentals=0),
        name="touch",
    )(*arrays)


def write_layers(out, values):
    rows = rows_iota((8, NZ))
    for k, value in enumerate(values):
        out[pl.ds(CY * k, CY), :] = value[:CY]
    for k in range(0, 9, 2):
        tile = pltpu.roll(values[k][CY:], 2, 0)
        if k < 8:
            tile = jnp.where(rows < 4, tile, pltpu.roll(values[k + 1][CY:], 6, 0))
        out[pl.ds(9 * CY + 4 * k, 8), :] = tile


def read_layer(ref, k):
    tile = ref[pl.ds(9 * CY + 8 * (k // 2), 8), :]
    return ring(ref[pl.ds(CY * k, CY), :], pltpu.roll(tile, 2 if k % 2 else 6, 0))


def call_edges(kernel, name, step_index, arrays, messages, shapes):
    whole = pl.BlockSpec(memory_space=pltpu.VMEM)

    def body(step_index, *refs):
        sides = []
        for side in range(2):
            at = pl.ds(side * (CX - 2), 2)
            sides += [refs[a].at[:, at] if a < 4 else refs[a].at[at] for a in range(7)]
        kernel(step_index, *sides, *refs[7:9], *refs[10:])

    return pl.pallas_call(
        body,
        in_specs=[pl.BlockSpec(memory_space=pltpu.SMEM)] + [whole] * (7 + len(messages)),
        out_specs=[whole] * len(shapes),
        out_shape=[jax.ShapeDtypeStruct(s, F32) for s in shapes],
        compiler_params=pltpu.CompilerParams(vmem_limit_bytes=EDGE_BYTES),
        cost_estimate=pl.CostEstimate(flops=3 * 10**9, bytes_accessed=0, transcendentals=0),
        name=name,
    )(step_index, *arrays, *messages)


def edge_kernel(step_index, e_f0, h_f0, e_a0, h_a0, inv0, src0, adj0, e_f1, h_f1, e_a1, h_a1, inv1, src1, adj1, above, below, out_prev, out_next, keep):
    row_dt = ring_steps()
    ghosts = {x: Ghosts(above, below, x) for x in (0, 1, CX - 2, CX - 1)}
    still = jnp.zeros((8, NZ), F32)
    amp = [amplitude(step_index, ticks, CY) for ticks in (1, -1)]

    def before(ref, at, run, x):
        return rings([ref[c, at] for c in range(3)], ghosts[x].e_before(run))

    def middle(ref, at, run, x):
        return rings([ref[c, at] for c in range(3)], ghosts[x].e_middle(run))

    def magnet(ref, at, run, x):
        return rings([ref[c, at] for c in range(3)], ghosts[x].h_before(run))

    coef_first = ring(DT * inv0[0], ghosts[0].coef())
    coef_last = ring(DT * inv1[1], ghosts[CX - 1].coef())
    to_prev, to_next = [None] * 9, [None] * 9
    to_prev[8] = coef_first
    to_next[8] = coef_last
    for run, (e0, h0, s0, e1, h1, s1) in enumerate(
        [(e_f0, h_f0, src0, e_f1, h_f1, src1), (e_a0, h_a0, adj0, e_a1, h_a1, adj1)]
    ):
        near = ghosts[0]
        h = magnetic(before(e0, 0, run, 0), before(e0, 1, run, 1), magnet(h0, 0, run, 0), row_dt)
        drive = ring(amp[run] * s0[0], still)
        new = electric(middle(e0, 0, run, 0), h, None, coef_first, drive)
        sides_y = {0: near.down(9, run), 6: near.up(13, 2 * run + 1), 7: near.up(6 * run + 1)}
        sides_z = {0: near.down(4 * run + 1), 7: near.up(13, 2 * run)}
        to_prev[4 * run] = ring(e0[1, 0], near.tile(sides_y))
        to_prev[4 * run + 1] = ring(e0[2, 0], near.tile(sides_z))
        to_prev[4 * run + 2] = new[1]
        to_prev[4 * run + 3] = new[2]
        keep[4 * run] = new[0][:CY]
        e, back = before(e1, 1, run, CX - 1), before(e1, 0, run, CX - 2)
        h = magnetic(e, None, magnet(h1, 1, run, CX - 1), row_dt)
        h_back = magnetic(back, e, magnet(h1, 0, run, CX - 2), row_dt)
        drive = ring(amp[run] * s1[1], still)
        new = electric(middle(e1, 1, run, CX - 1), h, h_back, coef_last, drive)
        later = magnetic(new, None, h, row_dt)
        beyond = ghosts[CX - 1].down(9, 2 + run)
        to_next[4 * run] = jnp.where(rows_iota((RING, NZ)) == CY, beyond, h[1])
        to_next[4 * run + 1] = h[2]
        to_next[4 * run + 2] = later[1]
        to_next[4 * run + 3] = later[2]
        for c in range(3):
            keep[4 * run + 1 + c] = new[c][:CY]
    write_layers(out_prev, to_prev)
    write_layers(out_next, to_next)


def solve_edges(step_index, arrays, above, below, touched):
    shapes = [(9 * CY + 40, NZ), (9 * CY + 40, NZ), (8, CY, NZ)]
    return call_edges(edge_kernel, "solve_edges", step_index, arrays, [above, below, touched], shapes)


CHUNK = 2
DRAIN = 4


def zplus(tile):
    moved = pltpu.roll(tile, NZ - 1, 1)
    last = jnp.where(lanes_iota((8, 128)) == 127, 0.0, moved[:, NZ - 128 :])
    return jnp.concatenate([moved[:, : NZ - 128], last], axis=1) - tile


def zminus(tile):
    moved = pltpu.roll(tile, 1, 1)
    first = jnp.where(lanes_iota((8, 128)) == 0, 0.0, moved[:, :128])
    return tile - jnp.concatenate([first, moved[:, 128:]], axis=1)


def magnetic_tiles(tiles, e, e_next, h, row_dts, put, closed):
    end = rows_iota((8, NZ)) == 7
    firsts = {c: pltpu.roll(e(c, 0), 7, 0) for c in (0, 2)}
    here = firsts
    for t in range(tiles):
        if t == tiles - 1:
            after = {c: jnp.zeros((8, NZ), F32) for c in (0, 2)} if closed else firsts
        else:
            after = {c: pltpu.roll(e(c, t + 1), 7, 0) for c in (0, 2)}
        ex, ey, ez = (e(c, t) for c in range(3))
        put(0, t, h(0, t) - row_dts[t] * ((jnp.where(end, after[2], here[2]) - ez) - zplus(ey)))
        put(1, t, h(1, t) - row_dts[t] * (zplus(ex) - (e_next(2, t) - ez)))
        put(2, t, h(2, t) - row_dts[t] * ((e_next(1, t) - ey) - (jnp.where(end, after[0], here[0]) - ex)))
        here = after


def electric_tile(e, h, h_prev, coef, drive, t, rolled):
    start = rows_iota((8, NZ)) == 0
    hx, hy, hz = (h(c, t) for c in range(3))
    moved = {0: pltpu.roll(hx, 1, 0), 2: pltpu.roll(hz, 1, 0)}
    new_x = e(0, t) + coef * ((hz - jnp.where(start, rolled[2], moved[2])) - zminus(hy))
    new_y = e(1, t) + coef * (zminus(hx) - (hz - h_prev(2, t)))
    curl = (hy - h_prev(1, t)) - (hx - jnp.where(start, rolled[0], moved[0]))
    new_z = e(2, t) + coef * (curl if drive is None else curl - drive)
    return (new_x, new_y, new_z), moved


def sweep(step_index, places, store, mid_h, mid_e, late_h, tiles, at_rows, ghosts, put_last):
    v_ef, v_hf, v_ea, v_ha, v_inv, v_src, v_adj = places
    own = [t for t in range(tiles) if at_rows[t] is not None]
    closed = len(own) == tiles
    mid_h[...] = jnp.zeros_like(mid_h)
    late_h[...] = jnp.zeros_like(late_h)
    ghost_dt = None if closed else ring_steps()[CY:]
    row_dts = [DT if t in own else ghost_dt for t in range(tiles)]
    amp = [[amplitude(step_index, ticks, 8) for ticks in pair] for pair in ((1, 2), (-1, -2))]
    runs = ((v_ef, v_hf, v_src), (v_ea, v_ha, v_adj))
    nothing = {c: jnp.zeros((8, NZ), F32) for c in (0, 2)}

    def rows(t):
        return pl.ds(at_rows[t], 8)

    def ring_rows(t):
        return pl.ds(8 * t, 8)

    def one(step, carry):
        now, then = lax.rem(step, 2), lax.rem(step + 1, 2)

        @pl.when(step <= CX)
        def _():
            x = step - 1
            inside, x_next = step < CX, jnp.minimum(step, CX - 1)
            if not closed:
                here, there = ghosts(x), ghosts(jnp.minimum(step, CX - 1))
                coef_ghost = here.coef()
            for run, (e_ref, h_ref, s_ref) in enumerate(runs):
                beside = beside_next = beside_h = middle = None
                if not closed:
                    beside = here.e_before(run)
                    beside_next = [jnp.where(inside, v, 0.0) for v in there.e_before(run)]
                    beside_h = here.h_before(run)
                    middle = here.e_middle(run)

                def put_h(c, t, value):
                    mid_h[now, 3 * run + c, ring_rows(t), :] = value

                magnetic_tiles(
                    tiles,
                    lambda c, t: e_ref[c, x, rows(t), :] if t in own else beside[c],
                    lambda c, t: jnp.where(inside, e_ref[c, x_next, rows(t), :], 0.0) if t in own else beside_next[c],
                    lambda c, t: h_ref[c, x, rows(t), :] if t in own else beside_h[c],
                    row_dts,
                    put_h,
                    closed,
                )
                rolled = nothing
                if not closed:
                    end = ring_rows(tiles - 1)
                    rolled = {c: pltpu.roll(mid_h[now, 3 * run + c, end, :], 1, 0) for c in (0, 2)}
                for t in range(tiles):
                    if t in own:
                        coef, drive = DT * v_inv[x, rows(t), :], amp[run][0] * s_ref[x, rows(t), :]
                    else:
                        coef, drive = coef_ghost, None
                    new, rolled = electric_tile(
                        lambda c, t: e_ref[c, x, rows(t), :] if t in own else middle[c],
                        lambda c, t: mid_h[now, 3 * run + c, ring_rows(t), :],
                        lambda c, t: mid_h[then, 3 * run + c, ring_rows(t), :],
                        coef,
                        drive,
                        t,
                        rolled,
                    )
                    for c in range(3):
                        mid_e[now, 3 * run + c, ring_rows(t), :] = new[c]

        @pl.when(step > CX)
        def _():
            mid_e[now] = jnp.zeros((6, 8 * tiles, NZ), F32)

        @pl.when(step > 1)
        def _():
            x = step - 2
            rolled = [nothing, nothing]
            for run in range(2):

                def put_late(c, t, value):
                    late_h[now, 3 * run + c, ring_rows(t), :] = value

                magnetic_tiles(
                    tiles,
                    lambda c, t: mid_e[then, 3 * run + c, ring_rows(t), :],
                    lambda c, t: mid_e[now, 3 * run + c, ring_rows(t), :],
                    lambda c, t: mid_h[then, 3 * run + c, ring_rows(t), :],
                    row_dts,
                    put_late,
                    closed,
                )
            for t in range(tiles):
                if t not in own:
                    rolled = [
                        {c: pltpu.roll(late_h[now, 3 * run + c, ring_rows(t), :], 1, 0) for c in (0, 2)}
                        for run in range(2)
                    ]
                    continue
                coef = DT * v_inv[x, rows(t), :]
                new = [None, None]
                for run, (e_ref, _, s_ref) in enumerate(runs):
                    new[run], rolled[run] = electric_tile(
                        lambda c, t: mid_e[then, 3 * run + c, ring_rows(t), :],
                        lambda c, t: late_h[now, 3 * run + c, ring_rows(t), :],
                        lambda c, t: late_h[then, 3 * run + c, ring_rows(t), :],
                        coef,
                        amp[run][1] * s_ref[x, rows(t), :],
                        t,
                        rolled[run],
                    )
                first = [[mid_e[then, 3 * run + c, ring_rows(t), :] for c in range(3)] for run in range(2)]
                put_last(x, t, new, DT * (dot_three(*first) + dot_three(*new)))

        @pl.when((step > 2) & (step % DRAIN == 1))
        def _():
            for a in range(2):
                store(a, step // DRAIN - 1).start()

        return carry

    lax.fori_loop(1, CX + 2, one, 0)
    for part in range(CX // DRAIN):
        for a in range(2):
            store(a, part).wait()


def main_kernel(
    step_index, e_f, h_f, e_a, h_a, inv, src, adj, above, below, out_f, out_a, grad,
    last_f, last_a, mid_h, mid_e, late_h, store_sem,
):
    def store(a, part):
        at = pl.ds(part * DRAIN, DRAIN)
        return pltpu.make_async_copy((last_f, last_a)[a].at[:, at], (out_f, out_a)[a].at[:, at], store_sem.at[a, part])

    def put_last(x, t, new, product):
        for c in range(3):
            last_f[c, x, pl.ds(8 * t - 8, 8), :] = new[0][c]
            last_a[c, x, pl.ds(8 * t - 8, 8), :] = new[1][c]
        grad[x, pl.ds(8 * t - 8, 8), :] = product

    sweep(
        step_index, (e_f, h_f, e_a, h_a, inv, src, adj), store, mid_h, mid_e, late_h, 5, [None, 0, 8, 16, 24],
        lambda x: Ghosts(above, below, x), put_last,
    )


def solve_main(step_index, arrays, above, below):
    free, whole = pl.BlockSpec(memory_space=pl.ANY), pl.BlockSpec(memory_space=pltpu.VMEM)
    field, cells = (3, CX, CY, NZ), (CX, CY, NZ)
    return pl.pallas_call(
        main_kernel,
        in_specs=[pl.BlockSpec(memory_space=pltpu.SMEM)] + [whole] * 9,
        out_specs=[free, free, whole],
        out_shape=[jax.ShapeDtypeStruct(s, F32) for s in (field, field, cells)],
        scratch_shapes=[pltpu.VMEM(field, F32)] * 2
        + [pltpu.VMEM((2, 6, RING, NZ), F32)] * 3
        + [pltpu.SemaphoreType.DMA((2, CX // DRAIN))],
        compiler_params=pltpu.CompilerParams(vmem_limit_bytes=MAIN_BYTES),
        cost_estimate=pl.CostEstimate(flops=14 * 10**9, bytes_accessed=0, transcendentals=0),
        name="solve_main",
    )(step_index, *arrays, above, below)


def split(value):
    high = value.astype(jnp.bfloat16)
    return high, (value - high.astype(F32)).astype(jnp.bfloat16)


def exact_dot(a, b, dims):
    high, low = split(b)
    a = a.astype(jnp.bfloat16)
    return lax.dot_general(a, high, dims, preferred_element_type=F32) + lax.dot_general(
        a, low, dims, preferred_element_type=F32
    )


def correct_prev(run, from_prev, own, row_dt, present):
    e0y, e0z, e1y, e1z = (own[4 * run + k] for k in range(4))
    coef, ghost_coef = own[8], jnp.where(present, from_prev[8], 0.0)
    h1y, h1z, h2y, h2z = (from_prev[4 * run + k] for k in range(4))
    d_h1y, d_h1z = DT * e0z, -DT * e0y
    h1y = jnp.where(present, h1y + d_h1y, 0.0)
    h1z = jnp.where(present, h1z + d_h1z, 0.0)
    d_e1y, d_e1z = coef * h1z, -coef * h1y
    g_e1x = ghost_coef * (minus_y(d_h1z) - minus_z(d_h1y))
    g_e1y, g_e1z = -ghost_coef * d_h1z, ghost_coef * d_h1y
    h2y = jnp.where(present, h2y + d_h1y - DT * (plus_z(g_e1x) - (e1z + d_e1z - g_e1z)), 0.0)
    h2z = jnp.where(present, h2z + d_h1z - DT * ((e1y + d_e1y - g_e1y) - plus_y(g_e1x)), 0.0)
    d_h2x = -row_dt * (plus_y(d_e1z) - plus_z(d_e1y))
    d_h2y, d_h2z = -row_dt * d_e1z, row_dt * d_e1y
    first = (None, d_e1y, d_e1z)
    last = (
        coef * (minus_y(d_h2z) - minus_z(d_h2y)),
        d_e1y + coef * (minus_z(d_h2x) - d_h2z + h2z),
        d_e1z + coef * (d_h2y - h2y - minus_y(d_h2x)),
    )
    return first, last, d_h2y, d_h2z


def correct_next(run, from_next, own, row_dt, present):
    e0y, e0z, e1y, e1z = (jnp.where(present, from_next[4 * run + k], 0.0) for k in range(4))
    coef, ghost_coef = own[8], jnp.where(present, from_next[8], 0.0)
    h1y, h1z = own[4 * run], own[4 * run + 1]
    d_h1y, d_h1z = DT * e0z, -DT * e0y
    d_e1x = coef * (minus_y(d_h1z) - minus_z(d_h1y))
    d_e1y, d_e1z = -coef * d_h1z, coef * d_h1y
    e1y = e1y + ghost_coef * (h1z + d_h1z)
    e1z = e1z - ghost_coef * (h1y + d_h1y)
    d_h2x = -row_dt * (plus_y(d_e1z) - plus_z(d_e1y))
    d_h2y = d_h1y - row_dt * (plus_z(d_e1x) - (e1z - d_e1z))
    d_h2z = d_h1z - row_dt * ((e1y - d_e1y) - plus_y(d_e1x))
    b_h2y, b_h2z = row_dt * d_e1z, -row_dt * d_e1y
    first = (d_e1x, d_e1y, d_e1z)
    last = (
        d_e1x + coef * (minus_y(d_h2z) - minus_z(d_h2y)),
        d_e1y + coef * (minus_z(d_h2x) - d_h2z + b_h2z),
        d_e1z + coef * (d_h2y - b_h2y - minus_y(d_h2x)),
    )
    return first, last, b_h2y, b_h2z


def put_cells(chosen, values, rows_out, q):
    devices = rows_out.shape[0]
    cells = exact_dot(chosen[...], values.reshape(4 * CY, NZ), (((1,), (1,)), ((), ())))
    for part in range(BZ):
        at = part * CX * CY + q * 4 * CY
        rows_out[:, 0, at : at + 4 * CY] = cells[part * devices : (part + 1) * devices]


def inner_kernel(mask, param, grad, rows_out, chosen):
    devices = rows_out.shape[0]
    lanes = lanes_iota((devices, NZ))
    blocks = lax.broadcasted_iota(jnp.int32, (NZ // BZ, NZ), 0)
    spread = (blocks == lanes_iota((NZ // BZ, NZ)) // BZ).astype(jnp.bfloat16)
    owned = NZ // BZ // 2
    owner = jnp.where(mask[0] == 1, param[0] // owned, -1).astype(F32)
    slot = (param[0] & (owned - 1)).astype(F32)
    numbers = jnp.concatenate([owner, slot, jnp.zeros((14, NZ // BZ), F32)], axis=0)
    numbers = jnp.dot(numbers.astype(jnp.bfloat16), spread, preferred_element_type=F32)
    mine = numbers[0:1, :] == rows_iota((devices, NZ)).astype(F32)
    for part in range(BZ):
        chosen[pl.ds(part * devices, devices), :] = jnp.where(mine & (lanes % BZ == part), 1.0, 0.0).astype(jnp.bfloat16)
    found = jnp.sum(jnp.where(mine & (lanes % BZ == 0), numbers[1:2, :] + 1.0, 0.0), axis=1, keepdims=True) - 1.0
    rows_out[:, 0, BZ * CX * CY :] = jnp.broadcast_to(found, (devices, 128))

    for q in (1, 2):
        put_cells(chosen, grad[pl.ds(4 * q, 4)], rows_out, q)


def pack_inner(mask, param, grad, devices):
    whole = pl.BlockSpec(memory_space=pltpu.VMEM)
    return pl.pallas_call(
        inner_kernel,
        in_specs=[whole] * 3,
        out_specs=[whole] * 2,
        out_shape=[
            jax.ShapeDtypeStruct((devices, 1, BZ * CX * CY + 128), F32),
            jax.ShapeDtypeStruct((BZ * devices, NZ), jnp.bfloat16),
        ],
        compiler_params=pltpu.CompilerParams(vmem_limit_bytes=PACK_BYTES),
        cost_estimate=pl.CostEstimate(flops=2 * 10**9, bytes_accessed=0, transcendentals=0),
        name="pack_inner",
    )(mask, param, grad)


def correct_kernel(
    chosen, *refs
):
    (ref_to_prev, keep, ref_to_next), far, refs = refs[:3], refs[3:5], refs[5:]
    far_inv, far_grad, old_f, old_a, _, out_f, out_a, far_rows, *refs = refs
    near, refs = refs[:2], refs[2:]
    (
    v_inv, work, v_f, v_a, rows_out,
    message_sem, inv_sem, grad_sem, field_sem, store_sem, rows_sem,
    ) = refs
    ref_from_prev, ref_from_next = near
    place = lax.axis_index("gx")
    has_prev, has_next = place > 0, place < lax.axis_size("gx") - 1
    row_dt = row_steps()
    messages = [pltpu.make_async_copy(a, b, message_sem.at[k]) for k, (a, b) in enumerate(zip(far, near))]
    grads = [
        pltpu.make_async_copy(far_grad.at[pl.ds(4 * q, 4)], work.at[pl.ds(4 * q, 4)], grad_sem.at[q]) for q in (0, 3)
    ]
    ends, stores = [], []
    for side in range(2):
        at = pl.ds(side * (CX - 2), 2)
        ends.append(
            [
                pltpu.make_async_copy(far_inv.at[at], v_inv.at[side], inv_sem.at[side]),
                pltpu.make_async_copy(old_f.at[:, at], v_f.at[side], field_sem.at[0, side]),
                pltpu.make_async_copy(old_a.at[:, at], v_a.at[side], field_sem.at[1, side]),
            ]
        )
        stores.append(
            [
                pltpu.make_async_copy(v_f.at[side], out_f.at[:, at], store_sem.at[0, side]),
                pltpu.make_async_copy(v_a.at[side], out_a.at[:, at], store_sem.at[1, side]),
            ]
        )
    for copy in [*messages[:1], *ends[0], grads[0], *messages[1:], *ends[1], grads[1]]:
        copy.start()

    def finish(side, edge_at, inner_at, firsts, lasts, d_inner, inner_coef, base_first):
        total_f, total_a, inner_f, inner_a = [], [], [], []
        fields_f, fields_a = v_f.at[side], v_a.at[side]
        before = jnp.zeros((CY, NZ), F32)
        for c in range(3):
            before = before + fields_f[c, inner_at] * fields_a[c, inner_at]
        for run, (ref, total, inner) in enumerate([(fields_f, total_f, inner_f), (fields_a, total_a, inner_a)]):
            for c in range(3):
                total.append(ref[c, edge_at] + lasts[run][c][:CY])
                ref[c, edge_at] = total[c]
                add = d_inner[run][c]
                inner.append(ref[c, inner_at] if add is None else ref[c, inner_at] + inner_coef * add[:CY])
                ref[c, inner_at] = inner[c]
        e1 = [
            [base_first[run][c] if firsts[run][c] is None else base_first[run][c] + firsts[run][c][:CY] for c in range(3)]
            for run in range(2)
        ]
        edge_grad = DT * (dot_three(e1[0], e1[1]) + dot_three(total_f, total_a))
        inner_change = DT * (dot_three(inner_f, inner_a) - before)
        return edge_grad, inner_change

    def first_edge():
        firsts, lasts, d_inner, base = [], [], [], []
        from_prev, to_prev = ([read_layer(ref, k) for k in range(9)] for ref in (ref_from_prev, ref_to_prev))
        for run in range(2):
            first, last, d_h2y, d_h2z = correct_prev(run, from_prev, to_prev, row_dt, has_prev)
            firsts.append(first)
            lasts.append(last)
            d_inner.append((None, d_h2z, -d_h2y))
            base.append((keep[4 * run], to_prev[4 * run + 2][:CY], to_prev[4 * run + 3][:CY]))
        edge, inner = finish(0, 0, 1, firsts, lasts, d_inner, DT * v_inv[0, 1], base)
        work[0] = edge
        work[1] = work[1] + inner

    def last_edge():
        firsts, lasts, d_inner, base = [], [], [], []
        from_next = [read_layer(ref_from_next, k) for k in range(9)]
        to_next = {k: read_layer(ref_to_next, k) for k in (0, 1, 4, 5, 8)}
        for run in range(2):
            first, last, b_h2y, b_h2z = correct_next(run, from_next, to_next, row_dt, has_next)
            firsts.append(first)
            lasts.append(last)
            d_inner.append((minus_y(b_h2z) - minus_z(b_h2y), -b_h2z, b_h2y))
            base.append(tuple(keep[4 * run + 1 + c] for c in range(3)))
        edge, inner = finish(1, 1, 0, firsts, lasts, d_inner, DT * v_inv[1, 0], base)
        work[CX - 1] = edge
        work[CX - 2] = work[CX - 2] + inner

    row_copies = []

    def pack(q):
        put_cells(chosen, work[pl.ds(4 * q, 4)], rows_out, q)
        for part in range(BZ):
            columns = pl.ds(part * CX * CY + q * 4 * CY, 4 * CY)
            row_copies.append(
                pltpu.make_async_copy(rows_out.at[:, :, columns], far_rows.at[:, :, columns], rows_sem.at[q, part])
            )
            row_copies[-1].start()

    for copy in [*messages[:1], *ends[0], grads[0]]:
        copy.wait()
    first_edge()
    for copy in stores[0]:
        copy.start()
    pack(0)
    for copy in [*messages[1:], *ends[1], grads[1]]:
        copy.wait()
    last_edge()
    for copy in stores[1]:
        copy.start()
    pack(3)
    for copy in [*stores[0], *stores[1], *row_copies]:
        copy.wait()


def correct_and_pack(chosen, messages, inv, grad, fields_f, fields_a, rows):
    free, whole = pl.BlockSpec(memory_space=pl.ANY), pl.BlockSpec(memory_space=pltpu.VMEM)
    vmem = lambda shape: pltpu.VMEM(shape, F32)
    return pl.pallas_call(
        correct_kernel,
        in_specs=[whole] * 4 + [free] * 7,
        out_specs=[free] * 3,
        out_shape=[
            jax.ShapeDtypeStruct((3, CX, CY, NZ), F32),
            jax.ShapeDtypeStruct((3, CX, CY, NZ), F32),
            jax.ShapeDtypeStruct(rows.shape, F32),
        ],
        scratch_shapes=[vmem(m.shape) for m in messages[3:]]
        + [vmem((2, 2, CY, NZ)), vmem((CX, CY, NZ))]
        + [vmem((2, 3, 2, CY, NZ))] * 2
        + [vmem(rows.shape)]
        + [pltpu.SemaphoreType.DMA(s) for s in ((2,), (2,), (4,), (2, 2), (2, 2), (4, BZ))],
        input_output_aliases={8: 0, 9: 1, 10: 2},
        compiler_params=pltpu.CompilerParams(vmem_limit_bytes=PACK_BYTES),
        cost_estimate=pl.CostEstimate(flops=6 * 10**9, bytes_accessed=0, transcendentals=0),
        name="correct_and_pack",
    )(chosen, *messages, inv, grad, fields_f, fields_a, rows)


def place_kernel(got, out):
    devices = got.shape[0]
    owned = out.shape[0]
    cells = BZ * CX * CY
    numbers = got[:, 0, cells:]
    wanted = (numbers == lanes_iota((devices, 128)).astype(F32)).astype(F32)
    placing = jnp.transpose(wanted)[:owned]
    order_from = rows_iota((4 * 128, 4 * 128))
    order_to = lanes_iota((4 * 128, 4 * 128))
    order = (order_from == (order_to % BZ) * 128 + order_to // BZ).astype(jnp.bfloat16)
    dims = (((1,), (0,)), ((), ()))
    for q in range(4):
        parts = [got[:, 0, part * CX * CY + q * 128 : part * CX * CY + (q + 1) * 128] for part in range(BZ)]
        rows = exact_dot(placing, jnp.concatenate(parts, axis=1), dims)
        high, low = split(rows)
        out[:, q * 512 : (q + 1) * 512] = lax.dot_general(
            high, order, dims, preferred_element_type=F32
        ) + lax.dot_general(low, order, dims, preferred_element_type=F32)


def place_rows(got, owned):
    return pl.pallas_call(
        place_kernel,
        out_shape=jax.ShapeDtypeStruct((owned, BZ * CX * CY), F32),
        compiler_params=pltpu.CompilerParams(vmem_limit_bytes=32 << 20),
        cost_estimate=pl.CostEstimate(flops=2 * 10**9, bytes_accessed=0, transcendentals=0),
        name="place_rows",
    )(got)


def body(e_forward, h_forward, e_adjoint, h_adjoint, inv_eps, source, adj_source, design_mask, param_map, step_index):
    arrays = (e_forward, h_forward, e_adjoint, h_adjoint, inv_eps, source, adj_source)
    devices = lax.axis_size("gx") * lax.axis_size("gy")
    blocks = NZ // BZ
    owned = blocks // 2
    up, down = pack_rows(step_index, arrays)
    above, below = cycled(up, "gy", 1), cycled(down, "gy", -1)
    touched = touch(arrays)
    to_prev, to_next, keep = solve_edges(step_index, arrays, above, below, touched)
    from_next, from_prev = cycled(to_prev, "gx", -1), cycled(to_next, "gx", 1)
    fields_f, fields_a, grad = solve_main(step_index, arrays, above, below)
    messages = (to_prev, keep, to_next, from_prev, from_next)
    rows, chosen = pack_inner(design_mask, param_map, grad, devices)
    fields_f, fields_a, rows = correct_and_pack(chosen, messages, inv_eps, grad, fields_f, fields_a, rows)
    got = lax.all_to_all(rows, ("gx", "gy"), split_axis=0, concat_axis=0, tiled=True)
    return place_rows(got, owned), fields_f, fields_a


def solution(mesh):
    field, cells = P(None, "gx", "gy", None), P("gx", "gy", None)
    in_specs = (field, field, field, field, cells, cells, cells, cells, cells, P())
    out_specs = (P(("gx", "gy"), None), field, field)
    return jax.shard_map(body, mesh=mesh, in_specs=in_specs, out_specs=out_specs, check_vma=False)
```
